32 devices in a mesh: batch: 8 (over y, x, core), frames: 4 (over z).
Axes of the slice: x: 2, y: 2, z: 4, core: 2. Of those that a mesh axis runs over, the one named last changes fastest.
Arguments:
- frames_in: bfloat16 [16, 1280, 1024], P('batch', 'frames'), may hold values from -6 to 6
- positions: int32 [16, 640], P('batch'), may hold values from -1 to 1279, as said below
- mask_vector: bfloat16 [1024], P(('batch', 'frames')), may hold values from -6 to 6
- norm_gains: bfloat16 [5, 1024], P(None, ('batch', 'frames')), may hold values from 0.5 to 1.5
- norm_biases: bfloat16 [5, 1024], P(None, ('batch', 'frames')), may hold values from -1.75 to 1.75
- depth_gain: bfloat16 [2048], P(('batch', 'frames')), may hold values from 0.5 to 1.5
- depth_bias: bfloat16 [2048], P(('batch', 'frames')), may hold values from -1.75 to 1.75
- early_in: bfloat16 [1024, 4096], P(('batch', 'frames')), may hold values from -0.1875 to 0.1875
- early_out: bfloat16 [4096, 1024], P(('batch', 'frames')), may hold values from -0.1875 to 0.1875
- qkv_weight: bfloat16 [1024, 3072], P(('batch', 'frames')), may hold values from -0.1875 to 0.1875
- mixer_out: bfloat16 [1024, 1024], P(('batch', 'frames')), may hold values from -1.5 to 1.5
- pointwise_in: bfloat16 [1024, 4096], P(('batch', 'frames')), may hold values from -0.1875 to 0.1875
- pointwise_out: bfloat16 [2048, 1024], P(('batch', 'frames')), may hold values from -0.1875 to 0.1875
- depth_kernel: bfloat16 [31, 2048], P(None, ('batch', 'frames')), may hold values from -1 to 1
- late_in: bfloat16 [1024, 4096], P(('batch', 'frames')), may hold values from -0.1875 to 0.1875
- late_out: bfloat16 [4096, 1024], P(('batch', 'frames')), may hold values from -0.1875 to 0.1875
- position_bias: bfloat16 [512], P(('batch', 'frames')), may hold values from -6 to 6
- cotangent: bfloat16 [16, 1280, 1024], P('batch', 'frames'), may hold values from -6 to 6
Outputs:
- activations: bfloat16 [16, 1280, 1024], P('batch', 'frames')
- grad_frames: float32 [16, 1280, 1024], P('batch', 'frames')
- grad_mask_vector: float32 [1024], P(('batch', 'frames'))
- grad_norm_gains: float32 [5, 1024], P(None, ('batch', 'frames'))
- grad_norm_biases: float32 [5, 1024], P(None, ('batch', 'frames'))
- grad_depth_gain: float32 [2048], P(('batch', 'frames'))
- grad_depth_bias: float32 [2048], P(('batch', 'frames'))
- grad_early_in: float32 [1024, 4096], P(('batch', 'frames'))
- grad_early_out: float32 [4096, 1024], P(('batch', 'frames'))
- grad_qkv_weight: float32 [1024, 3072], P(('batch', 'frames'))
- grad_mixer_out: float32 [1024, 1024], P(('batch', 'frames'))
- grad_pointwise_in: float32 [1024, 4096], P(('batch', 'frames'))
- grad_pointwise_out: float32 [2048, 1024], P(('batch', 'frames'))
- grad_depth_kernel: float32 [31, 2048], P(None, ('batch', 'frames'))
- grad_late_in: float32 [1024, 4096], P(('batch', 'frames'))
- grad_late_out: float32 [4096, 1024], P(('batch', 'frames'))
- grad_position_bias: float32 [512], P(('batch', 'frames'))
The draws below stay inside these ranges and needn't reach their ends.
Inputs may be any that keep to these rules, and one draw needn't show every extreme that they name: `positions`: each row lists distinct frame numbers of its utterance, followed by -1 entries in the remaining slots; at least one row has no -1.
All inputs are finite; a program needn't handle non-finite values.
Results may differ from the reference program's by a relative error of at most 0.03.
Values may be sent and summed in bfloat16 or wider, within the bound.
A program may use at most 512 MiB of HBM per device.

```python
import math
import jax
import jax.numpy as jnp
from jax import lax

D = 1024
H = 16
DH = 64
FF = 4096
C = 2048
KERNEL = 31
HALF = 15
NB = 32
FRAMES_UTT = 1280
UTTS = 16
MAXM = 640


def draw_positions(key, part):
    key = jax.random.fold_in(key, 7)
    row_keys = jax.random.split(key, UTTS)
    shuffled = jax.vmap(lambda row_key: jax.random.permutation(row_key, FRAMES_UTT))(row_keys)[:, :MAXM]
    levels = jax.random.randint(jax.random.fold_in(key, 1), (UTTS,), 0, 6)
    counts = jnp.maximum(MAXM // jnp.power(2, levels), 1)
    fullest = jax.random.randint(jax.random.fold_in(key, 2), (), 0, UTTS)
    counts = jnp.where(jnp.arange(UTTS) == fullest, MAXM, counts)
    slots = jnp.arange(MAXM)
    return jnp.where(slots[None, :] < counts[:, None], shuffled, -1).astype(jnp.int32)


def level_of(stream_key, extent, shards, least, top_value):
    gain = 1.0
    for axis_at, blocks in shards:
        steps = jax.random.uniform(jax.random.fold_in(jax.random.fold_in(stream_key, 6), axis_at), (blocks,), jnp.float32, least / len(shards), top_value / len(shards))
        gain = gain * jnp.repeat(jnp.exp(steps), extent[axis_at] // blocks).reshape((-1,) + (1,) * (len(extent) - 1 - axis_at))
    return gain


def scatter_about(rng, dims, scale, most, pieces=(), held_as=jnp.bfloat16):
    entries = scale * jax.random.normal(rng, dims, jnp.float32)
    if pieces:
        entries = entries * level_of(rng, dims, pieces, -0.22, 0.18)
    return jnp.clip(entries, -most, most).astype(held_as)


def setup_inputs(seed: int = 0) -> dict:
    key_of = jax.random.split(jax.random.key(seed), 19)
    return {
        "frames_in": scatter_about(key_of[0], (UTTS, FRAMES_UTT, D), 1.0, 6.0, ((0, 8), (1, 4))),
        "positions": draw_positions(jax.random.fold_in(key_of[18], 71), 0),
        "mask_vector": scatter_about(key_of[2], (D,), 1.0, 6.0, ((0, 32),)),
        "norm_gains": jnp.clip(1.0 + 0.1 * jax.random.normal(key_of[3], (5, D), jnp.float32), 0.5, 1.5).astype(jnp.bfloat16),
        "norm_biases": scatter_about(key_of[4], (5, D), 0.3, 1.75, ((1, 32),)),
        "depth_gain": jnp.clip(1.0 + 0.1 * jax.random.normal(key_of[5], (C,), jnp.float32), 0.5, 1.5).astype(jnp.bfloat16),
        "depth_bias": scatter_about(key_of[6], (C,), 0.3, 1.75, ((0, 32),)),
        "early_in": scatter_about(key_of[7], (D, FF), D ** -0.5, 0.1875, ((0, 32),)),
        "early_out": scatter_about(key_of[8], (FF, D), (FF // 4) ** -0.5, 0.1875, ((0, 32),)),
        "qkv_weight": scatter_about(key_of[9], (D, 3 * D), D ** -0.5, 0.1875, ((0, 32),)),
        "mixer_out": scatter_about(key_of[10], (D, D), (D // 64) ** -0.5, 1.5, ((0, 32),)),
        "pointwise_in": scatter_about(key_of[11], (D, 2 * C), D ** -0.5, 0.1875, ((0, 32),)),
        "pointwise_out": scatter_about(key_of[12], (C, D), (C // 2) ** -0.5, 0.1875, ((0, 32),)),
        "depth_kernel": scatter_about(key_of[13], (KERNEL, C), KERNEL ** -0.5, 1.0, ((1, 32),)),
        "late_in": scatter_about(key_of[14], (D, FF), D ** -0.5, 0.1875, ((0, 32),)),
        "late_out": scatter_about(key_of[15], (FF, D), (FF // 4) ** -0.5, 0.1875, ((0, 32),)),
        "position_bias": scatter_about(key_of[16], (H * NB,), 1.0, 6.0, ((0, 32),)),
        "cotangent": scatter_about(key_of[17], (UTTS, FRAMES_UTT, D), 1.0, 6.0, ((0, 8), (1, 4))),
    }


EPS = 1e-05
LIMITS = (8, 12, 16, 24, 32, 48, 64, 96)

@jax.custom_vjp
def low(v):
    return lax.optimization_barrier(v.astype(jnp.bfloat16)).astype(jnp.float32)

@jax.custom_vjp
def low_back(v):
    return v

def low_keep(v):
    return (low(v), None)

def low_pass(kept, grad):
    return (grad,)

def back_keep(v):
    return (v, None)

def back_low(kept, grad):
    return (low(grad),)
low.defvjp(low_keep, low_pass)
low_back.defvjp(back_keep, back_low)

def precise_dot(operand_a, operand_b):
    return jnp.dot(operand_a, operand_b, precision=lax.Precision.HIGHEST)

def layer_norm(values, norm_gain, norm_shift):
    centred = values - lax.optimization_barrier(jnp.mean(values, axis=-1, keepdims=True))
    spread = lax.optimization_barrier(jnp.mean(centred * centred, axis=-1, keepdims=True))
    return centred * lax.rsqrt(spread + EPS) * norm_gain + norm_shift

def bucket_of(relative):
    magnitude = jnp.abs(relative)
    above = jnp.zeros_like(relative)
    for threshold in LIMITS:
        above = above + (magnitude >= threshold).astype(jnp.int32)
    inner_bucket = jnp.where(magnitude < 8, magnitude, 7 + above)
    return (inner_bucket + NB // 2 * (relative > 0).astype(jnp.int32)).astype(jnp.int32)

def feed_forward(hidden, norm_gain, norm_shift, weight_in, weight_out):
    normed = low(layer_norm(hidden, norm_gain, norm_shift))
    inner_rows = low_back(precise_dot(normed, weight_in))
    return hidden + 0.5 * low_back(precise_dot(low(jax.nn.silu(inner_rows)), weight_out))

def attend(hidden, norm_gain, norm_shift, weight_qkv, weight_out, bias_table, bucket_index):
    normed = low(layer_norm(hidden, norm_gain, norm_shift))
    packed = low_back(low(precise_dot(normed, weight_qkv)))
    length = hidden.shape[0]
    split_heads = packed.reshape(length, 3, H, DH).transpose(1, 2, 0, 3)
    score_scale = 1.0 / math.sqrt(DH)

    def one_head(head_inputs):
        queries, key_rows, value_rows, table_row = head_inputs
        scores = low_back(precise_dot(queries, key_rows.T) * score_scale + jnp.take(table_row, bucket_index))
        row_max = lax.optimization_barrier(jnp.max(scores, axis=-1, keepdims=True))
        weights = jnp.exp(scores - row_max)
        probabilities = weights / lax.optimization_barrier(jnp.sum(weights, axis=-1, keepdims=True))
        return precise_dot(low(probabilities), value_rows)
    per_head = lax.map(jax.checkpoint(one_head), (split_heads[0], split_heads[1], split_heads[2], bias_table.reshape(H, NB)))
    mixed_rows = low_back(low(per_head.transpose(1, 0, 2).reshape(length, H * DH)))
    return hidden + low_back(precise_dot(mixed_rows, weight_out))

def convolve(hidden, norm_gain, norm_shift, weight_in, weight_out, kernel, depth_gain, depth_bias):
    normed = low(layer_norm(hidden, norm_gain, norm_shift))
    paired = low_back(precise_dot(normed, weight_in))
    gated = low(paired[:, :C] * jax.nn.sigmoid(paired[:, C:]))
    length = hidden.shape[0]
    padded = jnp.pad(gated, ((HALF, HALF), (0, 0)))
    depth_values = jnp.zeros_like(gated)
    for offset in range(KERNEL):
        depth_values = depth_values + padded[offset:offset + length] * kernel[offset]
    depth_values = low_back(depth_values)
    post = low(jax.nn.silu(layer_norm(depth_values, depth_gain, depth_bias)))
    return hidden + low_back(precise_dot(post, weight_out))

def layer(frames, params, masked, bucket_index):
    mask_vector, norm_gains, norm_biases, depth_gain, depth_bias, early_in, early_out, qkv_weight, mixer_out, pointwise_in, pointwise_out, depth_kernel, late_in, late_out, position_bias = params
    hidden0 = jnp.where(masked[:, None], mask_vector[None, :], frames)
    hidden1 = feed_forward(hidden0, norm_gains[0], norm_biases[0], early_in, early_out)
    hidden2 = attend(hidden1, norm_gains[1], norm_biases[1], qkv_weight, mixer_out, position_bias, bucket_index)
    hidden3 = convolve(hidden2, norm_gains[2], norm_biases[2], pointwise_in, pointwise_out, depth_kernel, depth_gain, depth_bias)
    hidden4 = feed_forward(hidden3, norm_gains[3], norm_biases[3], late_in, late_out)
    return layer_norm(hidden4, norm_gains[4], norm_biases[4])

def reference(frames_in, positions, mask_vector, norm_gains, norm_biases, depth_gain, depth_bias, early_in, early_out, qkv_weight, mixer_out, pointwise_in, pointwise_out, depth_kernel, late_in, late_out, position_bias, cotangent):
    params = (mask_vector.astype(jnp.float32), norm_gains.astype(jnp.float32), norm_biases.astype(jnp.float32), depth_gain.astype(jnp.float32), depth_bias.astype(jnp.float32), early_in.astype(jnp.float32), early_out.astype(jnp.float32), qkv_weight.astype(jnp.float32), mixer_out.astype(jnp.float32), pointwise_in.astype(jnp.float32), pointwise_out.astype(jnp.float32), depth_kernel.astype(jnp.float32), late_in.astype(jnp.float32), late_out.astype(jnp.float32), position_bias.astype(jnp.float32))
    frame_ids = jnp.arange(FRAMES_UTT, dtype=jnp.int32)
    bucket_index = bucket_of(frame_ids[None, :] - frame_ids[:, None])

    def per_utterance(summed, utterance):
        frames, listed, incoming = utterance
        masked = jnp.any(listed[:, None] == frame_ids[None, :], axis=0)

        def run(values, weights):
            return layer(values, weights, masked, bucket_index)
        result, pull_back = jax.vjp(run, frames.astype(jnp.float32), params)
        grad_input, grad_params = pull_back(incoming.astype(jnp.float32))
        summed = jax.tree.map(lambda first_term, second_term: first_term + second_term, summed, grad_params)
        return (summed, (result.astype(jnp.bfloat16), grad_input))
    zeros = jax.tree.map(jnp.zeros_like, params)
    summed, (activations, grad_frames) = lax.scan(per_utterance, zeros, (frames_in, positions, cotangent))
    return (activations, grad_frames, summed[0], summed[1], summed[2], summed[3], summed[4], summed[5], summed[6], summed[7], summed[8], summed[9], summed[10], summed[11], summed[12], summed[13], summed[14])
```

```python
import functools
import math

import jax
import jax.numpy as jnp
from jax import lax
from jax.experimental import pallas as pl
from jax.experimental.pallas import tpu as pltpu
from jax.sharding import PartitionSpec as P

MESH = pl.DeviceIdType.MESH


def ring_spot(index, count):
    half = count // 2
    return index + (index // half) * (3 * half - 1 - 2 * index)


def places(chips, frames):
    batch, depth = lax.axis_index("batch"), lax.axis_index("frames")
    chip, core = batch // 2, lax.rem(batch, 2)
    spot = ring_spot(chip, chips)

    def chip_at(offset):
        return ring_spot(lax.rem(spot + offset + chips, chips), chips)

    return chip, core, depth, chip_at


def shares(columns):
    first = columns * 3 // 4 if columns % 1024 == 0 else columns
    return ((0, first), (first, columns - first))


def greet(chips, frames, partners):
    chip, core, depth, chip_at = places(chips, frames)
    barrier = pltpu.get_barrier_semaphore()
    for offset in (1, -1):
        pl.semaphore_signal(
            barrier, inc=1, device_id=(chip_at(offset) * 2 + core, depth), device_id_type=MESH
        )
    pl.semaphore_signal(
        barrier, inc=1, device_id=(chip * 2 + 1 - core, depth), device_id_type=MESH
    )

    @pl.when(depth > 0)
    def _():
        pl.semaphore_signal(barrier, inc=1, device_id=(chip * 2 + core, depth - 1), device_id_type=MESH)

    @pl.when(depth < frames - 1)
    def _():
        pl.semaphore_signal(barrier, inc=1, device_id=(chip * 2 + core, depth + 1), device_id_type=MESH)

    count = 3 + jnp.minimum(depth, 1) + jnp.minimum(frames - 1 - depth, 1)
    if partners:
        groups = frames // 2
        for place in range(groups):
            there, side = core * groups + place, depth // groups

            @pl.when(jnp.logical_or(there != depth, side != core))
            def _():
                pl.semaphore_signal(
                    barrier, inc=1, device_id=(chip * 2 + side, there), device_id_type=MESH
                )

        count = count + groups - (1 - jnp.abs(depth // groups - core))
    pl.semaphore_wait(barrier, count)


def swap_frames(chips, frames, sources, targets, send_sems, recv_sems, local_sem):
    chip, core, depth, chip_at = places(chips, frames)
    groups = frames // 2
    later = []
    for at, (source, target) in enumerate(zip(sources, targets)):
        for place in range(groups):
            there, side = core * groups + place, depth // groups
            mine = jnp.logical_and(there == depth, side == core)
            slot = lax.rem(depth, groups)
            remote = pltpu.make_async_remote_copy(
                src_ref=source.at[place],
                dst_ref=target.at[slot],
                send_sem=send_sems.at[at * groups + place],
                recv_sem=recv_sems.at[at * groups + slot],
                device_id=(chip * 2 + side, there),
                device_id_type=MESH,
            )
            here = pltpu.make_async_copy(source.at[place], target.at[slot], local_sem.at[at])
            pl.when(jnp.logical_not(mine))(remote.start)
            pl.when(mine)(here.start)
            arrival = pltpu.make_async_remote_copy(
                src_ref=source.at[place],
                dst_ref=target.at[place],
                send_sem=send_sems.at[at * groups + place],
                recv_sem=recv_sems.at[at * groups + place],
                device_id=(chip * 2 + side, there),
                device_id_type=MESH,
            )
            later.append((mine, remote, arrival, here))

    def finish():
        for mine, remote, arrival, here in later:
            pl.when(jnp.logical_not(mine))(remote.wait_send)
            pl.when(jnp.logical_not(mine))(arrival.wait_recv)
            pl.when(mine)(here.wait)

    return finish


class Gather:
    def __init__(self, spots, chips, frames, shard, whole, send_sems, recv_sems, local_sem):
        self.chips, self.frames = chips, frames
        self.chip, self.core, self.depth, self.chip_at = spots
        self.shard, self.whole = shard, whole
        self.send_sems, self.recv_sems, self.local_sem = send_sems, recv_sems, local_sem
        self.sent = []
        self.local = None
        self.phases = (frames - 1) + chips // 2
        self.waiting = []
        self.used = 0
        self.pair = None

    def copy(self, source, target, device, condition=None):
        at = self.used
        self.used += 1
        made = pltpu.make_async_remote_copy(
            src_ref=source,
            dst_ref=target,
            send_sem=self.send_sems.at[at],
            recv_sem=self.recv_sems.at[at],
            device_id=device,
            device_id_type=MESH,
        )
        return made

    def line_step(self, step, start, width, wide):
        columns = pl.ds(start, width)
        for way in (1, -1):
            origin = self.depth - way * (step - 1)
            to = self.depth + way
            valid = jnp.logical_and(
                jnp.logical_and(origin >= 0, origin < self.frames),
                jnp.logical_and(to >= 0, to < self.frames),
            )
            held = jnp.clip(origin, 0, self.frames - 1)
            into = jnp.clip(to, 0, self.frames - 1)
            if wide:
                source = self.whole.at[:, self.core, held, :, columns]
                target = source
            else:
                target = self.whole.at[self.chip, self.core, held, :, columns]
                source = self.shard.at[:, columns] if step == 1 else target
            made = self.copy(source, target, (self.chip * 2 + self.core, into))
            pl.when(valid)(made.start)
            self.sent.append((valid, made))
            before = self.depth - way * step
            comes = jnp.logical_and(before >= 0, before < self.frames)
            self.waiting.append((comes, made))

    def ring_step(self, step, start, width, wide):
        last = step == self.chips // 2
        for side, way in enumerate((1, -1)):
            origin = self.chip_at(-way * (step - 1))
            columns = pl.ds(start + (side * width // 2 if last else 0), width // 2 if last else width)
            if wide:
                source = self.whole.at[origin, self.core, :, :, columns]
                target = source
            else:
                target = self.whole.at[origin, self.core, self.depth, :, columns]
                source = self.shard.at[:, columns] if step == 1 else target
            made = self.copy(source, target, (self.chip_at(way) * 2 + self.core, self.depth))
            made.start()
            self.sent.append((None, made))
            self.waiting.append((None, made))

    def arrive(self):
        for condition, made in self.waiting:
            if condition is None:
                made.wait_recv()
            else:
                pl.when(condition)(made.wait_recv)
        self.waiting = []

    def phase(self, at):
        line, ring = self.frames - 1, self.chips // 2
        if at == 0:
            self.local = pltpu.make_async_copy(
                self.shard, self.whole.at[self.chip, self.core, self.depth], self.local_sem
            )
            self.local.start()
        self.arrive()
        if at == min(line, ring):
            self.local.wait()
        (first_start, first_width), (last_start, last_width) = shares(self.shard.shape[1])
        if at < self.phases:
            if at < line:
                self.line_step(at + 1, first_start, first_width, False)
            else:
                self.ring_step(at - line + 1, first_start, first_width, True)
            if last_width:
                if at < ring:
                    self.ring_step(at + 1, last_start, last_width, False)
                else:
                    self.line_step(at - ring + 1, last_start, last_width, True)
        elif at == self.phases:
            half = self.whole.at[:, self.core]
            self.pair = self.copy(half, half, (self.chip * 2 + 1 - self.core, self.depth))
            self.pair.start()
        else:
            self.pair.wait()

    def drain(self):
        for condition, made in self.sent:
            if condition is None:
                made.wait_send()
            else:
                pl.when(condition)(made.wait_send)


def gather_kernel(chips, frames, count, swaps, *refs):
    shards, refs = refs[:count], refs[count:]
    sources, refs = refs[:swaps], refs[swaps:]
    wholes, refs = refs[:count], refs[count:]
    targets, refs = refs[:swaps], refs[swaps:]
    send_sems, recv_sems, local_sems, swap_send, swap_recv, swap_local = refs
    greet(chips, frames, swaps > 0)
    finish = (
        swap_frames(chips, frames, sources, targets, swap_send, swap_recv, swap_local)
        if swaps
        else None
    )
    spots = places(chips, frames)
    parts = [
        Gather(
            spots, chips, frames, shard, whole, send_sems.at[at], recv_sems.at[at], local_sems.at[at]
        )
        for at, (shard, whole) in enumerate(zip(shards, wholes))
    ]
    phases = parts[0].phases + 2
    for time in range(phases + count - 1):
        for at, part in enumerate(parts):
            if 0 <= time - at < phases:
                part.phase(time - at)
    for part in parts:
        part.drain()
    if finish is not None:
        finish()


def gather_all(mesh_sizes, shards, swapped, identity):
    chips, frames = mesh_sizes
    count, swaps = len(shards), len(swapped)
    copies = 2 * 2 * (frames - 1 + chips // 2) + 1
    out_shape = [
        jax.ShapeDtypeStruct((chips, 2, frames) + shard.shape, shard.dtype) for shard in shards
    ] + [jax.ShapeDtypeStruct(array.shape, array.dtype) for array in swapped]
    groups = frames // 2
    return pl.pallas_call(
        functools.partial(gather_kernel, chips, frames, count, swaps),
        out_shape=out_shape,
        in_specs=[pl.BlockSpec(memory_space=pl.ANY)] * (count + swaps),
        out_specs=[pl.BlockSpec(memory_space=pl.ANY)] * (count + swaps),
        scratch_shapes=[
            pltpu.SemaphoreType.DMA((count, copies)),
            pltpu.SemaphoreType.DMA((count, copies)),
            pltpu.SemaphoreType.DMA((count,)),
            pltpu.SemaphoreType.DMA((max(swaps, 1) * groups,)),
            pltpu.SemaphoreType.DMA((max(swaps, 1) * groups,)),
            pltpu.SemaphoreType.DMA((max(swaps, 1),)),
        ],
        compiler_params=pltpu.CompilerParams(collective_id=identity, has_side_effects=True),
    )(*shards, *swapped)


class Scatter:
    def __init__(self, spots, chips, frames, grads, out, total, stage, bounds, send_sems, recv_sems, local_sems):
        self.chips, self.frames = chips, frames
        self.chip, self.core, self.depth, self.chip_at = spots
        self.grads, self.out, self.total, self.stage = grads, out, total, stage
        self.bounds = list(bounds)
        self.send_sems, self.recv_sems, self.local_sems = send_sems, recv_sems, local_sems
        self.sent = []
        self.waiting = []
        self.phases = (frames - 1) + chips // 2
        self.used = 0
        self.pair = None

    def copy(self, source, target, device):
        at = self.used
        self.used += 1
        return pltpu.make_async_remote_copy(
            src_ref=source,
            dst_ref=target,
            send_sem=self.send_sems.at[at],
            recv_sem=self.recv_sems.at[at],
            device_id=device,
            device_id_type=MESH,
        )

    def begin(self):
        self.pair = self.copy(
            self.grads.at[:, 1 - self.core], self.total, (self.chip * 2 + 1 - self.core, self.depth)
        )
        self.pair.start()

    def load(self, chip):
        slot = chip % 2
        made = pltpu.make_async_copy(
            self.grads.at[chip, self.core], self.stage.at[slot], self.local_sems.at[slot]
        )
        made.start()
        return made

    def merge(self):
        loads = [self.load(0)]
        self.pair.wait()
        total, stage = self.total, self.stage
        for chip in range(self.chips):
            if chip + 1 < self.chips:
                loads.append(self.load(chip + 1))
            loads[chip].wait()

            @pl.loop(0, self.frames)
            def _(depth):
                total[chip, depth] = (
                    total[chip, depth].astype(jnp.float32)
                    + stage[chip % 2, depth].astype(jnp.float32)
                ).astype(total.dtype)

    def line_step(self, step, start, width, wide):
        frames = self.frames
        for way in (1, -1):
            reach = frames - step
            goal = self.depth + way * reach
            valid = jnp.logical_and(goal >= 0, goal < frames)
            held = jnp.clip(goal, 0, frames - 1)
            into = jnp.clip(self.depth + way, 0, frames - 1)
            columns = pl.ds(start, width)
            if wide:
                source = self.total.at[:, held, :, columns]
            else:
                source = self.total.at[self.chip, held, :, columns]
            landed = self.bounds.pop(0)
            made = self.copy(source, landed, (self.chip * 2 + self.core, into))
            pl.when(valid)(made.start)
            self.sent.append((valid, made))
            before = self.depth - way
            origin_goal = before + way * reach
            comes = jnp.logical_and(
                jnp.logical_and(before >= 0, before < frames),
                jnp.logical_and(origin_goal >= 0, origin_goal < frames),
            )
            goes = jnp.clip(origin_goal, 0, frames - 1)
            self.waiting.append((comes, made, landed, ("line", goes, wide, start, width)))

    def ring_step(self, step, start, width, wide):
        half = self.chips // 2
        for side, way in enumerate((1, -1)):
            reach = half - step + 1
            first = start + (side * width // 2 if step == 1 else 0)
            extent = width // 2 if step == 1 else width
            columns = pl.ds(first, extent)
            goal = self.chip_at(way * reach)
            if wide:
                source = self.total.at[goal, :, :, columns]
            else:
                source = self.total.at[goal, self.depth, :, columns]
            landed = self.bounds.pop(0)
            made = self.copy(source, landed, (self.chip_at(way) * 2 + self.core, self.depth))
            made.start()
            self.sent.append((None, made))
            goes = self.chip_at(way * (reach - 1))
            self.waiting.append((None, made, landed, ("ring", goes, wide, first, extent)))

    def arrive(self):
        for condition, made, landed, place in self.waiting:
            kind, goes, wide, start, width = place

            def settle(made=made, landed=landed, kind=kind, goes=goes, wide=wide, start=start, width=width):
                made.wait_recv()
                columns = pl.ds(start, width)
                total = self.total

                def merged(at, piece):
                    total[at] = (total[at].astype(jnp.float32) + piece.astype(jnp.float32)).astype(
                        total.dtype
                    )

                if not wide:
                    where = (self.chip, goes) if kind == "line" else (goes, self.depth)
                    merged(where + (slice(None), columns), landed[...])
                else:
                    count = self.chips if kind == "line" else self.frames

                    @pl.loop(0, count)
                    def _(at):
                        where = (at, goes) if kind == "line" else (goes, at)
                        merged(where + (slice(None), columns), landed[at])

            if condition is None:
                settle()
            else:
                pl.when(condition)(settle)
        self.waiting = []

    def phase(self, at):
        line, ring = self.frames - 1, self.chips // 2
        self.arrive()
        (first_start, first_width), (last_start, last_width) = shares(self.total.shape[-1])
        if at < self.phases:
            if at < ring:
                self.ring_step(at + 1, first_start, first_width, True)
            else:
                self.line_step(at - ring + 1, first_start, first_width, False)
            if last_width:
                if at < line:
                    self.line_step(at + 1, last_start, last_width, True)
                else:
                    self.ring_step(at - line + 1, last_start, last_width, False)
        else:
            self.out[...] = self.total[self.chip, self.depth].astype(self.out.dtype)

    def drain(self):
        for condition, made in self.sent:
            if condition is None:
                made.wait_send()
            else:
                pl.when(condition)(made.wait_send)


def landing_shapes(chips, frames, rows, columns):
    (_, first), (_, last) = shares(columns)
    line, ring = frames - 1, chips // 2
    shapes = []
    for at in range(line + ring):
        if at < ring:
            shapes += [(frames, rows, first // 2 if at == 0 else first)] * 2
        else:
            shapes += [(rows, first)] * 2
        if last:
            if at < line:
                shapes += [(chips, rows, last)] * 2
            else:
                shapes += [(rows, last // 2 if at == line else last)] * 2
    return shapes


def scatter_kernel(chips, frames, count, swaps, landings, *refs):
    grads, refs = refs[:count], refs[count:]
    sources, refs = refs[:swaps], refs[swaps:]
    outs, refs = refs[:count], refs[count:]
    targets, refs = refs[:swaps], refs[swaps:]
    totals, refs = refs[:count], refs[count:]
    stages, refs = refs[:count], refs[count:]
    bounds = []
    for many in landings:
        bounds.append(refs[:many])
        refs = refs[many:]
    send_sems, recv_sems, local_sems, swap_send, swap_recv, swap_local = refs
    greet(chips, frames, swaps > 0)
    finish = (
        swap_frames(chips, frames, sources, targets, swap_send, swap_recv, swap_local)
        if swaps
        else None
    )
    spots = places(chips, frames)
    parts = [
        Scatter(
            spots,
            chips,
            frames,
            grads[at],
            outs[at],
            totals[at],
            stages[at],
            bounds[at],
            send_sems.at[at],
            recv_sems.at[at],
            local_sems.at[at],
        )
        for at in range(count)
    ]
    for part in parts:
        part.begin()
    phases = parts[0].phases + 1
    for time in range(phases + count - 1):
        for at, part in enumerate(parts):
            if 0 <= time - at < phases:
                if time == at:
                    part.merge()
                part.phase(time - at)
    for part in parts:
        part.drain()
    if finish is not None:
        finish()


def scatter_all(mesh_sizes, grads, swapped, identity):
    chips, frames = mesh_sizes
    count, swaps = len(grads), len(swapped)
    copies = 2 * 2 * (frames - 1 + chips // 2) + 1
    groups = frames // 2
    shards = [grad.shape[3:] for grad in grads]
    landings = [landing_shapes(chips, frames, *shard) for shard in shards]
    any_spec = pl.BlockSpec(memory_space=pl.ANY)
    scratch = [pltpu.VMEM((chips, frames) + shard, jnp.bfloat16) for shard in shards]
    scratch += [pltpu.VMEM((2, frames) + shard, jnp.bfloat16) for shard in shards]
    scratch += [pltpu.VMEM(shape, jnp.bfloat16) for shapes in landings for shape in shapes]
    return pl.pallas_call(
        functools.partial(
            scatter_kernel, chips, frames, count, swaps, [len(shapes) for shapes in landings]
        ),
        out_shape=[jax.ShapeDtypeStruct(shard, jnp.float32) for shard in shards]
        + [jax.ShapeDtypeStruct(array.shape, array.dtype) for array in swapped],
        in_specs=[any_spec] * (count + swaps),
        out_specs=[pl.BlockSpec(memory_space=pltpu.VMEM)] * count + [any_spec] * swaps,
        scratch_shapes=scratch
        + [
            pltpu.SemaphoreType.DMA((count, copies)),
            pltpu.SemaphoreType.DMA((count, copies)),
            pltpu.SemaphoreType.DMA((count, 2)),
            pltpu.SemaphoreType.DMA((max(swaps, 1) * groups,)),
            pltpu.SemaphoreType.DMA((max(swaps, 1) * groups,)),
            pltpu.SemaphoreType.DMA((max(swaps, 1),)),
        ],
        compiler_params=pltpu.CompilerParams(
            collective_id=identity, has_side_effects=True, vmem_limit_bytes=58 * 1024 * 1024
        ),
    )(*grads, *swapped)


D = 1024
H = 16
DH = 64
C = 2048
KERNEL = 31
HALF = 15
NB = 32
EPS = 1e-05
LIMITS = (8, 12, 16, 24, 32, 48, 64, 96)
BOTH = ("batch", "frames")
SMALL = (16, 512)


def layer_norm(values, norm_gain, norm_shift):
    centred = values - jnp.mean(values, axis=-1, keepdims=True)
    spread = jnp.mean(centred * centred, axis=-1, keepdims=True)
    return centred * lax.rsqrt(spread + EPS) * norm_gain + norm_shift


def bucket_of(relative):
    magnitude = jnp.abs(relative)
    above = jnp.zeros_like(relative)
    for threshold in LIMITS:
        above = above + (magnitude >= threshold).astype(jnp.int32)
    inner_bucket = jnp.where(magnitude < 8, magnitude, 7 + above)
    return inner_bucket + NB // 2 * (relative > 0).astype(jnp.int32)


def product(operand_a, operand_b):
    return jnp.dot(operand_a, operand_b, preferred_element_type=jnp.float32)


def weight_grad(operand_a, operand_b):
    return lax.dot_general(
        operand_a, operand_b, (((0,), (0,)), ((), ())), preferred_element_type=jnp.float32
    ).astype(jnp.bfloat16)


def back_product(operand_a, operand_b):
    return lax.dot_general(
        operand_a, operand_b, (((1,), (1,)), ((), ())), preferred_element_type=jnp.float32
    )


def gated_unit(paired):
    return paired[:, :C] * jax.nn.sigmoid(paired[:, C:])


def depth_post(depth_values, norm_gain, norm_shift):
    return jax.nn.silu(layer_norm(depth_values, norm_gain, norm_shift))


def norm_back(hidden, norm_gain, norm_shift, upstream):
    normed_unused, pull_back = jax.vjp(layer_norm, hidden, norm_gain, norm_shift)
    return pull_back(upstream)


def as_shard(array):
    rows = array.shape[0]
    return array if rows % 16 == 0 else array.reshape(16, rows * array.shape[1] // 16)


def as_weight(whole, like):
    devices = math.prod(whole.shape[:3])
    return whole.reshape(devices * like.shape[0], like.shape[1])


def as_parts(grad, sizes, like):
    chips, frames = sizes
    shard = as_shard(jnp.zeros(like.shape, jnp.bfloat16)).shape
    return grad.reshape((chips, 2, frames) + shard)


def pack_small(values, small_shapes):
    flat = jnp.concatenate([value.reshape(-1) for value in values])
    return jnp.pad(flat, (0, SMALL[0] * SMALL[1] - flat.shape[0])).reshape(SMALL)


def unpack_small(packed, shapes):
    devices = packed.shape[0]
    at, out = 0, []
    for shape in shapes:
        size = math.prod(shape)
        piece = packed[:, at : at + size].reshape((devices,) + shape)
        at += size
        piece = jnp.moveaxis(piece, 0, -2)
        out.append(piece.reshape(shape[:-1] + (devices * shape[-1],)))
    return out


def repack_small(values, shapes, devices):
    pieces = []
    for value, shape in zip(values, shapes):
        piece = value.reshape(shape[:-1] + (devices, shape[-1]))
        pieces.append(jnp.moveaxis(piece, -2, 0).reshape(devices, -1))
    flat = jnp.concatenate(pieces, axis=1)
    return jnp.pad(flat, ((0, 0), (0, SMALL[0] * SMALL[1] - flat.shape[1])))


def shards(
    frames_in,
    positions,
    mask_vector,
    norm_gains,
    norm_biases,
    depth_gain,
    depth_bias,
    early_in,
    early_out,
    qkv_weight,
    mixer_out,
    pointwise_in,
    pointwise_out,
    depth_kernel,
    late_in,
    late_out,
    position_bias,
    cotangent,
):
    groups, run, model_width = frames_in.shape
    line = lax.axis_size("frames")
    chips = lax.axis_size("batch") // 2
    sizes = (chips, line)
    devices = 2 * chips * line
    length = run * line
    rows = groups * run
    score_scale = 1.0 / math.sqrt(DH)
    batch, depth = lax.axis_index("batch"), lax.axis_index("frames")
    core = lax.rem(batch, 2)
    first_frame = core * rows
    partner = [(at, at + 1 - 2 * (at % 2)) for at in range(2 * chips)]

    def from_other(array):
        return lax.ppermute(array, "batch", partner)

    big = [early_in, early_out, qkv_weight, mixer_out, pointwise_in, pointwise_out, late_in, late_out]
    small = [mask_vector, norm_gains, norm_biases, depth_gain, depth_bias, depth_kernel, position_bias]
    small_shapes = [value.shape for value in small]
    small_size = sum(math.prod(shape) for shape in small_shapes)
    gathered = gather_all(
        sizes,
        [as_shard(value) for value in big] + [pack_small(small, small_shapes)],
        [frames_in, cotangent],
        0,
    )
    wholes = [as_weight(whole, like) for whole, like in zip(gathered, big)]
    w_early_in, w_early_out, w_qkv, w_mixer, w_point_in, w_point_out, w_late_in, w_late_out = wholes
    small_whole = gathered[len(big)].reshape(devices, SMALL[0] * SMALL[1])
    mask_full, gains, biases, channel_gain, channel_bias, kernel_full, table = [
        value.astype(jnp.float32) for value in unpack_small(small_whole, small_shapes)
    ]
    table = table.reshape(H, NB)
    frames_here = gathered[len(big) + 1].reshape(rows, D)
    upstream = gathered[len(big) + 2].reshape(rows, D).astype(jnp.float32)

    both = jnp.where(core == 0, 0, 1)
    other_positions = from_other(positions)
    owner = depth // groups
    listed = jnp.where(owner == both, positions, other_positions)
    listed = lax.dynamic_index_in_dim(listed, lax.rem(depth, groups), 0, keepdims=False)
    frame_ids = first_frame + jnp.arange(rows, dtype=jnp.int32)
    masked = jnp.any(listed[:, None] == frame_ids[None, :], axis=0).reshape(rows, 1)

    relative = jnp.arange(length, dtype=jnp.int32)[None, :] - frame_ids[:, None]
    bucket_index = bucket_of(relative)
    bias_grid = jnp.zeros((H, rows, length), jnp.float32)
    for at in range(NB):
        bias_grid = jnp.where(bucket_index[None] == at, table[:, at][:, None, None], bias_grid)

    def ffn_inner(hidden, which_norm, weight_in):
        normed = layer_norm(hidden, gains[which_norm], biases[which_norm]).astype(jnp.bfloat16)
        inner_rows = product(normed, weight_in)
        return (normed, inner_rows, jax.nn.silu(inner_rows).astype(jnp.bfloat16))

    def ffn_back(hidden, which_norm, kept, weight_in, weight_out, grad_hidden):
        normed, inner_rows, activated = kept
        grad_out = (0.5 * grad_hidden).astype(jnp.bfloat16)
        grad_weight_out = weight_grad(activated, grad_out)
        grad_act = back_product(grad_out, weight_out)
        silu_unused, silu_pull = jax.vjp(jax.nn.silu, inner_rows)
        grad_inner = silu_pull(grad_act)[0].astype(jnp.bfloat16)
        grad_weight_in = weight_grad(normed, grad_inner)
        grad_normed = back_product(grad_inner, weight_in)
        grad_input, gain_grad, bias_grad = norm_back(
            hidden, gains[which_norm], biases[which_norm], grad_normed
        )
        return (grad_hidden + grad_input, grad_weight_in, grad_weight_out, gain_grad, bias_grad)

    def in_order(mine, other):
        return jnp.where(
            core == 0,
            jnp.concatenate([mine, other], axis=0),
            jnp.concatenate([other, mine], axis=0),
        )

    def halves(whole):
        first, second = whole[:rows], whole[rows:]
        return jnp.where(core == 0, first, second), jnp.where(core == 0, second, first)

    hidden0 = jnp.where(masked, mask_full[None, :], frames_here.astype(jnp.float32))
    kept1 = ffn_inner(hidden0, 0, w_early_in)
    hidden1 = hidden0 + 0.5 * product(kept1[2], w_early_out)
    normed2 = layer_norm(hidden1, gains[1], biases[1]).astype(jnp.bfloat16)
    packed = product(normed2, w_qkv).astype(jnp.bfloat16)
    key_values = in_order(packed[:, D:], from_other(packed[:, D:]))
    queries = packed[:, :D].reshape(rows, H, DH)
    key_rows = key_values[:, :D].reshape(length, H, DH)
    value_rows = key_values[:, D:].reshape(length, H, DH)
    scores = (
        jnp.einsum("qhd,khd->hqk", queries, key_rows, preferred_element_type=jnp.float32)
        * score_scale
        + bias_grid
    )
    probabilities = jax.nn.softmax(scores, axis=-1)
    mixed_rows = (
        jnp.einsum(
            "hqk,khd->qhd",
            probabilities.astype(jnp.bfloat16),
            value_rows,
            preferred_element_type=jnp.float32,
        )
        .reshape(rows, D)
        .astype(jnp.bfloat16)
    )
    hidden2 = hidden1 + product(mixed_rows, w_mixer)

    normed3 = layer_norm(hidden2, gains[2], biases[2]).astype(jnp.bfloat16)
    paired = product(normed3, w_point_in)
    gated = gated_unit(paired).astype(jnp.bfloat16)

    def with_edges(array):
        sent = jnp.where(core == 0, array[rows - HALF :], array[:HALF])
        edge = from_other(sent)
        nothing = jnp.zeros_like(edge)
        return jnp.concatenate(
            [jnp.where(core == 0, nothing, edge), array, jnp.where(core == 0, edge, nothing)], axis=0
        )

    padded = with_edges(gated)
    depth_values = jnp.zeros((rows, C), jnp.float32)
    for offset in range(KERNEL):
        depth_values = (
            depth_values + padded[offset : offset + rows].astype(jnp.float32) * kernel_full[offset]
        )
    post_values, post_pull = jax.vjp(depth_post, depth_values, channel_gain, channel_bias)
    post = post_values.astype(jnp.bfloat16)
    hidden3 = hidden2 + product(post, w_point_out)
    kept5 = ffn_inner(hidden3, 3, w_late_in)
    hidden4 = hidden3 + 0.5 * product(kept5[2], w_late_out)
    activations = layer_norm(hidden4, gains[4], biases[4]).astype(jnp.bfloat16)

    grad4, gain_grad4, bias_grad4 = norm_back(hidden4, gains[4], biases[4], upstream)
    grad3, late_in_grad, late_out_grad, gain_grad3, bias_grad3 = ffn_back(
        hidden3, 3, kept5, w_late_in, w_late_out, grad4
    )
    grad_out3 = grad3.astype(jnp.bfloat16)
    pointwise_out_grad = weight_grad(post, grad_out3)
    grad_post = back_product(grad_out3, w_point_out)
    grad_depth, channel_gain_grad, channel_bias_grad = post_pull(grad_post)
    grad_depth_low = grad_depth.astype(jnp.bfloat16)
    grad_depth_wide = grad_depth_low.astype(jnp.float32)
    kernel_grad = jnp.stack(
        [
            jnp.sum(padded[offset : offset + rows].astype(jnp.float32) * grad_depth_wide, axis=0)
            for offset in range(KERNEL)
        ]
    )
    extended = with_edges(grad_depth_low)
    grad_gated = jnp.zeros((rows, C), jnp.float32)
    for offset in range(KERNEL):
        start_at = 2 * HALF - offset
        grad_gated = (
            grad_gated
            + extended[start_at : start_at + rows].astype(jnp.float32) * kernel_full[offset]
        )
    pair_unused, pair_pull = jax.vjp(gated_unit, paired)
    grad_paired = pair_pull(grad_gated)[0].astype(jnp.bfloat16)
    pointwise_in_grad = weight_grad(normed3, grad_paired)
    grad_normed3 = back_product(grad_paired, w_point_in)
    grad_in3, gain_grad2, bias_grad2 = norm_back(hidden2, gains[2], biases[2], grad_normed3)
    grad2 = grad3 + grad_in3

    grad_out2 = grad2.astype(jnp.bfloat16)
    mixer_out_grad = weight_grad(mixed_rows, grad_out2)
    grad_heads = back_product(grad_out2, w_mixer).astype(jnp.bfloat16).reshape(rows, H, DH)
    grad_probs = jnp.einsum(
        "qhd,khd->hqk", grad_heads, value_rows, preferred_element_type=jnp.float32
    )
    centre = jnp.sum(probabilities * grad_probs, axis=-1, keepdims=True)
    grad_scores = probabilities * (grad_probs - centre)
    table_grad = jnp.stack(
        [
            jnp.sum(jnp.where(bucket_index[None] == at, grad_scores, 0.0), axis=(1, 2))
            for at in range(NB)
        ],
        axis=-1,
    ).reshape(H * NB)
    grad_scores = grad_scores.astype(jnp.bfloat16)
    grad_queries = (
        jnp.einsum("hqk,khd->qhd", grad_scores, key_rows, preferred_element_type=jnp.float32)
        * score_scale
    )
    grad_keys = (
        jnp.einsum("hqk,qhd->khd", grad_scores, queries, preferred_element_type=jnp.float32)
        * score_scale
    )
    grad_values = jnp.einsum(
        "hqk,qhd->khd",
        probabilities.astype(jnp.bfloat16),
        grad_heads,
        preferred_element_type=jnp.float32,
    )
    merged = jnp.concatenate([grad_keys.reshape(length, D), grad_values.reshape(length, D)], axis=-1)
    merged_own, merged_other = halves(merged)
    grad_kv = merged_own + from_other(merged_other.astype(jnp.bfloat16)).astype(jnp.float32)
    grad_packed = jnp.concatenate(
        [grad_queries.reshape(rows, D).astype(jnp.bfloat16), grad_kv.astype(jnp.bfloat16)], axis=-1
    )
    qkv_grad = weight_grad(normed2, grad_packed)
    grad_normed2 = back_product(grad_packed, w_qkv)
    grad_in2, gain_grad1, bias_grad1 = norm_back(hidden1, gains[1], biases[1], grad_normed2)
    grad1 = grad2 + grad_in2
    grad0, early_in_grad, early_out_grad, gain_grad0, bias_grad0 = ffn_back(
        hidden0, 0, kept1, w_early_in, w_early_out, grad1
    )
    grad_frames = jnp.where(masked, 0.0, grad0).astype(jnp.bfloat16)
    mask_grad = jnp.sum(jnp.where(masked, grad0, 0.0), axis=0)
    gain_stack = jnp.stack([gain_grad0, gain_grad1, gain_grad2, gain_grad3, gain_grad4])
    bias_stack = jnp.stack([bias_grad0, bias_grad1, bias_grad2, bias_grad3, bias_grad4])
    small_grads = repack_small(
        [mask_grad, gain_stack, bias_stack, channel_gain_grad, channel_bias_grad, kernel_grad, table_grad],
        small_shapes,
        devices,
    ).astype(jnp.bfloat16)

    def parts(grad, like):
        return as_parts(grad, sizes, like)

    sums_late = scatter_all(
        sizes,
        [
            parts(late_out_grad, late_out),
            parts(late_in_grad, late_in),
            parts(pointwise_out_grad, pointwise_out),
            parts(pointwise_in_grad, pointwise_in),
        ],
        [],
        1,
    )
    sums_early = scatter_all(
        sizes,
        [
            parts(mixer_out_grad, mixer_out),
            parts(qkv_grad, qkv_weight),
            parts(early_out_grad, early_out),
            parts(early_in_grad, early_in),
            small_grads.reshape((chips, 2, line) + SMALL),
        ],
        [activations.reshape(groups, run, D), grad_frames.reshape(groups, run, D)],
        2,
    )
    small_sums = sums_early[4].reshape(-1)[:small_size]
    small_out, at = [], 0
    for shape in small_shapes:
        size = math.prod(shape)
        small_out.append(small_sums[at : at + size].reshape(shape))
        at += size
    return (
        sums_early[5],
        sums_early[6].astype(jnp.float32),
        small_out[0],
        small_out[1],
        small_out[2],
        small_out[3],
        small_out[4],
        sums_early[3].reshape(early_in.shape),
        sums_early[2].reshape(early_out.shape),
        sums_early[1].reshape(qkv_weight.shape),
        sums_early[0].reshape(mixer_out.shape),
        sums_late[3].reshape(pointwise_in.shape),
        sums_late[2].reshape(pointwise_out.shape),
        small_out[5],
        sums_late[1].reshape(late_in.shape),
        sums_late[0].reshape(late_out.shape),
        small_out[6],
    )


def solution(mesh):
    in_specs = (
        P("batch", "frames", None),
        P("batch", None),
        P(("batch", "frames")),
        P(None, ("batch", "frames")),
        P(None, ("batch", "frames")),
        P(("batch", "frames")),
        P(("batch", "frames")),
        P(("batch", "frames"), None),
        P(("batch", "frames"), None),
        P(("batch", "frames"), None),
        P(("batch", "frames"), None),
        P(("batch", "frames"), None),
        P(("batch", "frames"), None),
        P(None, ("batch", "frames")),
        P(("batch", "frames"), None),
        P(("batch", "frames"), None),
        P(("batch", "frames")),
        P("batch", "frames", None),
    )
    out_specs = (
        P("batch", "frames", None),
        P("batch", "frames", None),
        P(("batch", "frames")),
        P(None, ("batch", "frames")),
        P(None, ("batch", "frames")),
        P(("batch", "frames")),
        P(("batch", "frames")),
        P(("batch", "frames"), None),
        P(("batch", "frames"), None),
        P(("batch", "frames"), None),
        P(("batch", "frames"), None),
        P(("batch", "frames"), None),
        P(("batch", "frames"), None),
        P(None, ("batch", "frames")),
        P(("batch", "frames"), None),
        P(("batch", "frames"), None),
        P(("batch", "frames")),
    )
    return jax.shard_map(shards, mesh=mesh, in_specs=in_specs, out_specs=out_specs, check_vma=False)
```

```python
import functools
import math

import jax
import jax.numpy as jnp
from jax import lax
from jax.experimental import pallas as pl
from jax.experimental.pallas import tpu as pltpu
from jax.sharding import PartitionSpec as P

D = 1024
H = 16
DH = 64
C = 2048
KERNEL = 31
HALF = 15
NB = 32
EPS = 1e-05
LIMITS = (8, 12, 16, 24, 32, 48, 64, 96)
BOTH = ("batch", "frames")
SMALL = (16, 512)


MESH = pl.DeviceIdType.MESH
VMEM_BYTES = 58 * 1024 * 1024


def ring_spot(index, count):
    half = count // 2
    return index + (index // half) * (3 * half - 1 - 2 * index)


def places(chips, frames):
    batch, depth = lax.axis_index("batch"), lax.axis_index("frames")
    chip, core = batch // 2, lax.rem(batch, 2)
    spot = ring_spot(chip, chips)

    def chip_at(offset):
        return ring_spot(lax.rem(spot + offset + chips, chips), chips)

    return chip, core, depth, chip_at


def greet(chips, frames, partners):
    chip, core, depth, chip_at = places(chips, frames)
    barrier = pltpu.get_barrier_semaphore()
    for offset in (1, -1):
        pl.semaphore_signal(
            barrier, inc=1, device_id=(chip_at(offset) * 2 + core, depth), device_id_type=MESH
        )
    pl.semaphore_signal(
        barrier, inc=1, device_id=(chip * 2 + 1 - core, depth), device_id_type=MESH
    )

    @pl.when(depth > 0)
    def _():
        pl.semaphore_signal(barrier, inc=1, device_id=(chip * 2 + core, depth - 1), device_id_type=MESH)

    @pl.when(depth < frames - 1)
    def _():
        pl.semaphore_signal(barrier, inc=1, device_id=(chip * 2 + core, depth + 1), device_id_type=MESH)

    count = 3 + jnp.minimum(depth, 1) + jnp.minimum(frames - 1 - depth, 1)
    if partners:
        groups = frames // 2
        for place in range(groups):
            there, side = core * groups + place, depth // groups

            @pl.when(jnp.logical_or(there != depth, side != core))
            def _():
                pl.semaphore_signal(
                    barrier, inc=1, device_id=(chip * 2 + side, there), device_id_type=MESH
                )

        count = count + groups - (1 - jnp.abs(depth // groups - core))
    pl.semaphore_wait(barrier, count)


def swap_frames(chips, frames, sources, targets, send_sems, recv_sems, local_sem):
    chip, core, depth, chip_at = places(chips, frames)
    groups = frames // 2
    starts, ends = [], []
    for at, (source, target) in enumerate(zip(sources, targets)):
        for place in range(groups):
            there, side = core * groups + place, depth // groups
            mine = jnp.logical_and(there == depth, side == core)
            slot = lax.rem(depth, groups)
            remote = pltpu.make_async_remote_copy(
                src_ref=source.at[place],
                dst_ref=target.at[slot],
                send_sem=send_sems.at[at * groups + place],
                recv_sem=recv_sems.at[at * groups + slot],
                device_id=(chip * 2 + side, there),
                device_id_type=MESH,
            )
            arrival = pltpu.make_async_remote_copy(
                src_ref=source.at[place],
                dst_ref=target.at[place],
                send_sem=send_sems.at[at * groups + place],
                recv_sem=recv_sems.at[at * groups + place],
                device_id=(chip * 2 + side, there),
                device_id_type=MESH,
            )
            here = pltpu.make_async_copy(source.at[place], target.at[slot], local_sem.at[at])
            away = jnp.logical_not(mine)
            starts += [gated(away, remote.start), gated(mine, here.start)]
            ends += [
                gated(away, remote.wait_send),
                gated(away, arrival.wait_recv),
                gated(mine, here.wait),
            ]
    return starts, ends


def gated(condition, action):
    if condition is None:
        return action
    return lambda: pl.when(condition)(action)


class Mover:
    def __init__(self, spots, sizes, send_sems, recv_sems):
        self.chips, self.frames = sizes
        self.chip, self.core, self.depth, self.chip_at = spots
        self.send_sems, self.recv_sems = send_sems, recv_sems
        self.used = 0
        self.levels = [[] for _ in range(self.frames + self.chips // 2 + 1)]
        self.departures = []

    def copy(self, source, target, device, condition):
        at = self.used
        self.used += 1
        made = pltpu.make_async_remote_copy(
            src_ref=source,
            dst_ref=target,
            send_sem=self.send_sems.at[at],
            recv_sem=self.recv_sems.at[at],
            device_id=device,
            device_id_type=MESH,
        )
        self.departures.append(gated(condition, made.wait_send))
        return made

    def other_core(self):
        return (self.chip * 2 + 1 - self.core, self.depth)

    def group(self, offset):
        at = self.depth + offset
        if offset == 0:
            return at, None
        return jnp.clip(at, 0, self.frames - 1), jnp.logical_and(at >= 0, at < self.frames)

    def offsets(self, distance):
        return (0,) if distance == 0 else (-distance, distance)


class Gather(Mover):
    def __init__(self, spots, sizes, shard, whole, send_sems, recv_sems, local_sems):
        super().__init__(spots, sizes, send_sems, recv_sems)
        self.shard, self.whole = shard, whole
        self.local = pltpu.make_async_copy(
            shard, whole.at[self.chip, self.core, self.depth], local_sems.at[0]
        )
        self.levels[0].append(self.local.start)
        for distance in range(self.frames):
            self.spread(distance)
        self.levels[-1] += self.departures

    def spread(self, distance):
        chip, core, depth, half = self.chip, self.core, self.depth, self.chips // 2
        for offset in self.offsets(distance):
            held, valid = self.group(offset)
            block = self.whole.at[chip, core, held]
            source = block if distance else self.shard
            for way in (1, -1):
                if distance + 1 == self.frames or offset * way > 0:
                    continue
                into, there = self.group(way)
                condition = there if valid is None else jnp.logical_and(valid, there)
                made = self.copy(source, block, (chip * 2 + core, into), condition)
                self.levels[distance].append(gated(condition, made.start))
                comes = self.group(offset - way)[1]
                self.levels[distance + 1].insert(0, gated(comes, made.wait_recv))
            columns = self.shard.shape[1]
            for step in range(1, half + 1):
                level = distance + step - 1
                for side, way in enumerate((1, -1)):
                    part = slice(None)
                    if step == half:
                        part = pl.ds(side * columns // 2, columns // 2)
                    origin = self.chip_at(-way * (step - 1))
                    target = self.whole.at[origin, core, held, :, part]
                    start = self.shard.at[:, part] if distance == 0 and step == 1 else target
                    made = self.copy(start, target, (self.chip_at(way) * 2 + core, depth), valid)
                    self.levels[level].append(gated(valid, made.start))
                    self.levels[level + 1].append(gated(valid, made.wait_recv))
            if distance == 0:
                self.levels[half].append(self.local.wait)
            line = self.whole.at[:, core, held]
            pair = self.copy(line, line, self.other_core(), valid)
            self.levels[distance + half].append(gated(valid, pair.start))
            self.levels[-1].append(gated(valid, pair.wait_recv))


class Scatter(Mover):
    def __init__(
        self, spots, sizes, grads, out, total, stage, landings, send_sems, recv_sems, local_sems
    ):
        super().__init__(spots, sizes, send_sems, recv_sems)
        self.grads, self.out, self.total, self.stage = grads, out, total, stage
        self.landings = list(landings)
        self.local_sems = local_sems
        self.begins = []
        self.columns = out.shape[1]
        self.merges = 0
        for distance in reversed(range(self.frames)):
            self.collect(distance)
        self.levels[-1] += [self.finish] + self.departures

    def add(self, where, piece):
        total = self.total
        total[where] = (total[where].astype(jnp.float32) + piece.astype(jnp.float32)).astype(
            total.dtype
        )

    def merge(self, held, pair, load, stage):
        load.wait()
        pair.wait_recv()

        @pl.loop(0, self.chips)
        def _(chip):
            self.add((chip, held), stage[chip])

    def settle(self, made, where, landed):
        made.wait_recv()
        self.add(where, landed[...])

    def collect(self, distance):
        core, depth, half = self.core, self.depth, self.chips // 2
        first = self.frames - 1 - distance
        for offset in self.offsets(distance):
            held, valid = self.group(offset)
            pair = self.copy(
                self.grads.at[:, 1 - core, held], self.total.at[:, held], self.other_core(), valid
            )
            stage = self.stage.at[self.merges]
            load = pltpu.make_async_copy(
                self.grads.at[:, core, held], stage, self.local_sems.at[self.merges]
            )
            self.merges += 1
            self.begins += [gated(valid, pair.start), gated(valid, load.start)]
            self.levels[0].append(
                gated(valid, functools.partial(self.merge, held, pair, load, stage))
            )
            for step in range(1, half + 1):
                for side, way in enumerate((1, -1)):
                    part = slice(None)
                    if step == 1:
                        part = pl.ds(side * self.columns // 2, self.columns // 2)
                    reach = half - step + 1
                    goal = self.chip_at(way * reach)
                    landed = self.landings.pop(0)
                    made = self.copy(
                        self.total.at[goal, held, :, part],
                        landed,
                        (self.chip_at(way) * 2 + core, depth),
                        valid,
                    )
                    self.levels[step - 1 if step == 1 else first + step - 1].append(
                        gated(valid, made.start)
                    )
                    where = (self.chip_at(way * (reach - 1)), held, slice(None), part)
                    self.levels[first + step].append(
                        gated(valid, functools.partial(self.settle, made, where, landed))
                    )
            if distance == 0:
                continue
            way = 1 if offset > 0 else -1
            landed = self.landings.pop(0)
            made = self.copy(
                self.total.at[self.chip, held],
                landed,
                (self.chip * 2 + core, self.group(way)[0]),
                valid,
            )
            self.levels[first + half].append(gated(valid, made.start))
            before = self.group(-way)[1]
            goes, there = self.group(offset - way)
            comes = before if there is None else jnp.logical_and(before, there)
            where = (self.chip, goes, slice(None), slice(None))
            self.levels[first + half + 1].append(
                gated(comes, functools.partial(self.settle, made, where, landed))
            )

    def finish(self):
        self.out[...] = self.total[self.chip, self.depth].astype(self.out.dtype)


def landing_shapes(sizes, rows, columns):
    chips, frames = sizes
    shapes = []
    for distance in reversed(range(frames)):
        for _ in range(2 if distance else 1):
            shapes += [(rows, columns // 2)] * 2 + [(rows, columns)] * (2 * (chips // 2 - 1))
            if distance:
                shapes.append((rows, columns))
    return shapes


class Traffic:
    def __init__(self, sizes, identity, shards=(), grads=(), swapped=(), swap_at=0):
        self.sizes, self.identity = sizes, identity
        self.shards, self.grads, self.swapped = list(shards), list(grads), list(swapped)
        self.swap_at = swap_at
        self.active = bool(self.shards or self.grads or self.swapped)

    def operands(self):
        return self.shards + self.grads + self.swapped

    def in_specs(self):
        return [pl.BlockSpec(memory_space=pl.ANY)] * len(self.operands())

    def out_shapes(self):
        chips, frames = self.sizes
        return (
            [jax.ShapeDtypeStruct((chips, 2, frames) + s.shape, s.dtype) for s in self.shards]
            + [jax.ShapeDtypeStruct(g.shape[3:], jnp.float32) for g in self.grads]
            + [jax.ShapeDtypeStruct(s.shape, s.dtype) for s in self.swapped]
        )

    def out_specs(self):
        anywhere = pl.BlockSpec(memory_space=pl.ANY)
        return (
            [anywhere] * len(self.shards)
            + [pl.BlockSpec(memory_space=pltpu.VMEM)] * len(self.grads)
            + [anywhere] * len(self.swapped)
        )

    def scratch(self):
        if not self.active:
            return []
        chips, frames = self.sizes
        shapes = []
        for grad in self.grads:
            shard = grad.shape[3:]
            shapes += [
                pltpu.VMEM((chips, frames) + shard, grad.dtype),
                pltpu.VMEM((2 * frames - 1, chips) + shard, grad.dtype),
            ]
            shapes += [pltpu.VMEM(shape, grad.dtype) for shape in landing_shapes(self.sizes, *shard)]
        copies = (2 * frames - 1) * (3 + chips)
        arrays = max(len(self.shards) + len(self.grads), 1)
        swaps = max(len(self.swapped), 1)
        return shapes + [
            pltpu.SemaphoreType.DMA((arrays, copies)),
            pltpu.SemaphoreType.DMA((arrays, copies)),
            pltpu.SemaphoreType.DMA((arrays, 2 * frames - 1)),
            pltpu.SemaphoreType.DMA((swaps * (frames // 2),)),
            pltpu.SemaphoreType.DMA((swaps * (frames // 2),)),
            pltpu.SemaphoreType.DMA((swaps,)),
        ]

    def plan(self, ins, outs, scratch):
        if not self.active:
            return []
        chips, frames = self.sizes
        scratch = list(scratch)
        send_sems, recv_sems, local_sems, swap_send, swap_recv, swap_local = scratch[-6:]
        spots = places(chips, frames)
        gathers, scatters = len(self.shards), len(self.grads)
        parts, begins = [], []
        for at in range(gathers + scatters):
            sems = (send_sems.at[at], recv_sems.at[at], local_sems.at[at])
            if at < gathers:
                parts.append(Gather(spots, self.sizes, ins[at], outs[at], *sems))
                continue
            total, stage = scratch.pop(0), scratch.pop(0)
            many = len(landing_shapes(self.sizes, *outs[at].shape))
            landings = [scratch.pop(0) for _ in range(many)]
            parts.append(
                Scatter(spots, self.sizes, ins[at], outs[at], total, stage, landings, *sems)
            )
            begins += parts[-1].begins
        times = [[], []]
        if parts:
            times = [sum(level, []) for level in zip(*[part.levels for part in parts])]
        if self.swapped:
            starts, ends = swap_frames(
                chips, frames, ins[gathers + scatters :], outs[gathers + scatters :],
                swap_send, swap_recv, swap_local,
            )
            times[min(self.swap_at, len(times) - 1)] += starts
            times[-1] += ends
        times[0] = [functools.partial(greet, chips, frames, bool(self.swapped))] + begins + times[0]
        return times


def run_plan(times, step=None, steps=1):
    if step is None:
        for actions in times:
            for action in actions:
                action()
        return
    by_step = {}
    for at, actions in enumerate(times):
        by_step.setdefault(at * steps // len(times), []).extend(actions)
    for at, actions in by_step.items():

        def run(actions=actions):
            for action in actions:
                action()

        pl.when(step == at)(run)


def finish_plan(times):
    for action in times[-1]:
        action()


def traffic_kernel(traffic, *refs):
    count = len(traffic.operands())
    run_plan(traffic.plan(refs[:count], refs[count : 2 * count], refs[2 * count :]))


def move(traffic):
    return pl.pallas_call(
        functools.partial(traffic_kernel, traffic),
        out_shape=traffic.out_shapes(),
        in_specs=traffic.in_specs(),
        out_specs=traffic.out_specs(),
        scratch_shapes=traffic.scratch(),
        compiler_params=traffic_params(traffic),
    )(*traffic.operands())


def traffic_params(traffic):
    if not traffic.active:
        return pltpu.CompilerParams(vmem_limit_bytes=VMEM_BYTES)
    return pltpu.CompilerParams(
        collective_id=traffic.identity, has_side_effects=True, vmem_limit_bytes=VMEM_BYTES
    )


def layer_norm(values, norm_gain, norm_shift):
    centred = values - jnp.mean(values, axis=-1, keepdims=True)
    spread = jnp.mean(centred * centred, axis=-1, keepdims=True)
    return centred * lax.rsqrt(spread + EPS) * norm_gain + norm_shift


def bucket_of(relative):
    magnitude = jnp.abs(relative)
    above = jnp.zeros_like(relative)
    for threshold in LIMITS:
        above = above + (magnitude >= threshold).astype(jnp.int32)
    inner_bucket = jnp.where(magnitude < 8, magnitude, 7 + above)
    return inner_bucket + NB // 2 * (relative > 0).astype(jnp.int32)


def product(operand_a, operand_b):
    return jnp.dot(operand_a, operand_b, preferred_element_type=jnp.float32)


def weight_grad(operand_a, operand_b):
    return lax.dot_general(
        operand_a, operand_b, (((0,), (0,)), ((), ())), preferred_element_type=jnp.float32
    ).astype(jnp.bfloat16)


def back_product(operand_a, operand_b):
    return lax.dot_general(
        operand_a, operand_b, (((1,), (1,)), ((), ())), preferred_element_type=jnp.float32
    )


def gated_unit(paired):
    return paired[:, :C] * jax.nn.sigmoid(paired[:, C:])


def depth_post(depth_values, norm_gain, norm_shift):
    return jax.nn.silu(layer_norm(depth_values, norm_gain, norm_shift))


def norm_back(hidden, norm_gain, norm_shift, upstream):
    normed_unused, pull_back = jax.vjp(layer_norm, hidden, norm_gain, norm_shift)
    return pull_back(upstream)


TILE = 512
CHUNK = 64


def dot_nt(left, right):
    return lax.dot_general(left, right, (((1,), (1,)), ((), ())), preferred_element_type=jnp.float32)


def dot_nn(left, right):
    return lax.dot_general(left, right, (((1,), (0,)), ((), ())), preferred_element_type=jnp.float32)


def sigmoid(values):
    return 0.5 * jnp.tanh(0.5 * values) + 0.5


def norm_parts(values):
    centred = values - jnp.mean(values, axis=-1, keepdims=True)
    rstd = lax.rsqrt(jnp.mean(centred * centred, axis=-1, keepdims=True) + EPS)
    return centred * rstd, rstd


def norm_chunk(values, norms_ref, which):
    scaled, _ = norm_parts(values)
    return scaled * norms_ref[2 * which : 2 * which + 1, :] + norms_ref[2 * which + 1 : 2 * which + 2, :]


def chunks(rows):
    def each(body):
        @pl.loop(0, rows // CHUNK)
        def _(at):
            body(pl.ds(pl.multiple_of(at * CHUNK, CHUNK), CHUNK))

    return each


def ffn_kernel(traffic, hidden_ref, norms_ref, w_in_ref, w_out_ref, *refs):
    moved = len(traffic.operands())
    ins, refs = refs[:moved], refs[moved:]
    out_ref, inner_ref, normed_ref, next_ref = refs[:4]
    outs, refs = refs[4 : 4 + moved], refs[4 + moved :]
    total, refs = refs[0], refs[1:]
    step, steps = pl.program_id(0), pl.num_programs(0)
    run_plan(traffic.plan(ins, outs, refs), step, FFN_STEPS)
    each = chunks(hidden_ref.shape[0])

    @pl.when(step == 0)
    def _():
        def body(here):
            normed_ref[here, :] = norm_chunk(hidden_ref[here, :], norms_ref, 0).astype(jnp.bfloat16)
            total[here, :] = jnp.zeros((CHUNK, total.shape[1]), jnp.float32)

        each(body)

    inner = dot_nn(normed_ref[...], w_in_ref[...])
    inner_ref[...] = inner.astype(jnp.bfloat16)
    total[...] += dot_nn((inner * sigmoid(inner)).astype(jnp.bfloat16), w_out_ref[...])

    @pl.when(step == steps - 1)
    def _():
        def body(here):
            hidden = hidden_ref[here, :] + 0.5 * total[here, :]
            out_ref[here, :] = hidden
            next_ref[here, :] = norm_chunk(hidden, norms_ref, 1).astype(jnp.bfloat16)

        each(body)


FFN_STEPS = 8


def resident(shape):
    return pl.BlockSpec(shape, lambda step: (0,) * len(shape))


def ffn(hidden, norms, weight_in, weight_out, traffic):
    rows, width = hidden.shape
    tile = weight_in.shape[1] // FFN_STEPS
    return pl.pallas_call(
        functools.partial(ffn_kernel, traffic),
        grid=(FFN_STEPS,),
        out_shape=[
            jax.ShapeDtypeStruct((rows, width), jnp.float32),
            jax.ShapeDtypeStruct((rows, weight_in.shape[1]), jnp.bfloat16),
            jax.ShapeDtypeStruct((rows, width), jnp.bfloat16),
            jax.ShapeDtypeStruct((rows, width), jnp.bfloat16),
        ]
        + traffic.out_shapes(),
        in_specs=[
            resident((rows, width)),
            resident(norms.shape),
            pl.BlockSpec((width, tile), lambda step: (0, step)),
            pl.BlockSpec((tile, width), lambda step: (step, 0)),
        ]
        + traffic.in_specs(),
        out_specs=[
            resident((rows, width)),
            pl.BlockSpec((rows, tile), lambda step: (0, step)),
            resident((rows, width)),
            resident((rows, width)),
        ]
        + traffic.out_specs(),
        scratch_shapes=[pltpu.VMEM((rows, width), jnp.float32)] + traffic.scratch(),
        compiler_params=traffic_params(traffic),
    )(hidden, norms, weight_in, weight_out, *traffic.operands())


def ffn_back_kernel(
    traffic, hidden_ref, normed_ref, grad_ref, norms_ref, inner_ref, w_in_ref, w_out_ref, *refs
):
    moved = len(traffic.operands())
    ins, refs = refs[:moved], refs[moved:]
    out_ref, g_in_ref, g_out_ref, sums_ref = refs[:4]
    outs, refs = refs[4 : 4 + moved], refs[4 + moved :]
    (half_grad, turned, total), refs = refs[:3], refs[3:]
    step, steps = pl.program_id(0), pl.num_programs(0)
    run_plan(traffic.plan(ins, outs, refs), step, FFN_STEPS)
    each = chunks(hidden_ref.shape[0])

    @pl.when(step == 0)
    def _():
        def body(here):
            half_grad[here, :] = (0.5 * grad_ref[here, :]).astype(jnp.bfloat16)
            total[here, :] = jnp.zeros((CHUNK, total.shape[1]), jnp.float32)

        each(body)
        turned[...] = normed_ref[...].T
        sums_ref[...] = jnp.zeros_like(sums_ref)

    inner = inner_ref[...].astype(jnp.float32)
    gate = sigmoid(inner)
    active = (inner * gate).astype(jnp.bfloat16)
    g_out_ref[...] = dot_nn(active.T, half_grad[...]).astype(jnp.bfloat16)
    slope = gate * (1.0 + inner * (1.0 - gate))
    grad_inner = (dot_nt(half_grad[...], w_out_ref[...]) * slope).astype(jnp.bfloat16)
    g_in_ref[...] = dot_nn(turned[...], grad_inner).astype(jnp.bfloat16)
    total[...] += dot_nt(grad_inner, w_in_ref[...])

    @pl.when(step == steps - 1)
    def _():
        def body(here):
            scaled, rstd = norm_parts(hidden_ref[here, :])
            upstream = total[here, :]
            sums_ref[0:1, :] += jnp.sum(upstream * scaled, axis=0, keepdims=True)
            sums_ref[1:2, :] += jnp.sum(upstream, axis=0, keepdims=True)
            weighted = upstream * norms_ref[0:1, :]
            back = weighted - jnp.mean(weighted, axis=-1, keepdims=True)
            back = back - scaled * jnp.mean(weighted * scaled, axis=-1, keepdims=True)
            out_ref[here, :] = grad_ref[here, :] + rstd * back

        each(body)


def ffn_back(hidden, normed, grad, norms, inner, weight_in, weight_out, traffic):
    rows, width = hidden.shape
    tile = weight_in.shape[1] // FFN_STEPS
    return pl.pallas_call(
        functools.partial(ffn_back_kernel, traffic),
        grid=(FFN_STEPS,),
        out_shape=[
            jax.ShapeDtypeStruct((rows, width), jnp.float32),
            jax.ShapeDtypeStruct(weight_in.shape, jnp.bfloat16),
            jax.ShapeDtypeStruct(weight_out.shape, jnp.bfloat16),
            jax.ShapeDtypeStruct((8, width), jnp.float32),
        ]
        + traffic.out_shapes(),
        in_specs=[
            resident((rows, width)),
            resident((rows, width)),
            resident((rows, width)),
            resident(norms.shape),
            pl.BlockSpec((rows, tile), lambda step: (0, step)),
            pl.BlockSpec((width, tile), lambda step: (0, step)),
            pl.BlockSpec((tile, width), lambda step: (step, 0)),
        ]
        + traffic.in_specs(),
        out_specs=[
            resident((rows, width)),
            pl.BlockSpec((width, tile), lambda step: (0, step)),
            pl.BlockSpec((tile, width), lambda step: (step, 0)),
            resident((8, width)),
        ]
        + traffic.out_specs(),
        scratch_shapes=[
            pltpu.VMEM((rows, width), jnp.bfloat16),
            pltpu.VMEM((width, rows), jnp.bfloat16),
            pltpu.VMEM((rows, width), jnp.float32),
        ]
        + traffic.scratch(),
        compiler_params=traffic_params(traffic),
    )(hidden, normed, grad, norms, inner, weight_in, weight_out, *traffic.operands())


QB = 128
PAIRS = H // 2
BAND = 3 * QB


def stacked(block):
    lanes = lax.broadcasted_iota(jnp.int32, block.shape, 1)
    nothing = jnp.zeros_like(block)
    return jnp.concatenate(
        [jnp.where(lanes < DH, block, nothing), jnp.where(lanes >= DH, block, nothing)], axis=0
    )


def own_halves(both):
    channels = lax.broadcasted_iota(jnp.int32, (2 * DH, QB), 0)
    return jnp.where(channels < DH, both[:, :QB], both[:, QB:]).T


def offset_rows(table):
    offsets = (jnp.arange(4, dtype=jnp.int32)[:, None] - 1) * QB - jnp.arange(QB, dtype=jnp.int32)
    onehot = (jnp.arange(NB)[:, None, None] == bucket_of(offsets)[None]).astype(jnp.float32)
    rows = jnp.dot(table, onehot.reshape(NB, 4 * QB), precision=lax.Precision.HIGHEST)
    return rows.reshape(PAIRS, 8, QB)


def fill_strip(strip, rows_ref, length):
    far = length - 2 * QB
    rows_of = lax.broadcasted_iota(jnp.int32, (QB, QB), 0)
    lanes_of = lax.broadcasted_iota(jnp.int32, (QB, QB), 1)
    for head in range(2):
        columns = slice(head * QB, (head + 1) * QB)
        turned = []
        for at in range(4):
            row = jnp.broadcast_to(rows_ref[0, head * 4 + at : head * 4 + at + 1, :], (QB, QB))
            turned.append(pltpu.roll(row, 0, 1, stride=1, stride_axis=0))
        for tile in range(3):
            strip[far + tile * QB : far + (tile + 1) * QB, columns] = jnp.where(
                lanes_of >= rows_of, turned[tile], turned[tile + 1]
            )

        @pl.loop(0, far // QB)
        def _(at):
            before, after = pl.multiple_of(at * QB, QB), pl.multiple_of(far + BAND + at * QB, QB)
            strip[pl.ds(before, QB), columns] = turned[0]
            strip[pl.ds(after, QB), columns] = turned[3]


def strip_start(rows, length):
    first = lax.rem(lax.axis_index("batch"), 2) * rows + pl.program_id(1) * QB
    return pl.multiple_of(length - QB - first, QB), first


def attend_kernel(rows, length, traffic, rows_ref, q_ref, k_ref, v_ref, *refs):
    moved = len(traffic.operands())
    ins, refs = refs[:moved], refs[moved:]
    (out_ref, log_ref), refs = refs[:2], refs[2:]
    outs, refs = refs[:moved], refs[moved:]
    (strip, score, prob, vt), refs = refs[:4], refs[4:]
    blocks = rows // QB
    run_plan(
        traffic.plan(ins, outs, refs), pl.program_id(0) * blocks + pl.program_id(1), PAIRS * blocks
    )

    @pl.when(pl.program_id(1) == 0)
    def _():
        fill_strip(strip, rows_ref, length)
        vt[...] = v_ref[...].T

    start, _ = strip_start(rows, length)
    score[...] = dot_nt(k_ref[...], stacked(q_ref[...] * 0.125))

    def highest(at, most):
        here = pl.ds(pl.multiple_of(at * QB, QB), QB)
        values = score[here, :] + strip[pl.ds(pl.multiple_of(start + at * QB, QB), QB), :]
        score[here, :] = values
        return jnp.maximum(most, jnp.max(values.reshape(QB // 8, 8, 2 * QB), axis=0))

    most = lax.fori_loop(
        0, length // QB, highest, jnp.full((8, 2 * QB), -jnp.inf, jnp.float32), unroll=True
    )
    most = jnp.max(most, axis=0, keepdims=True)

    def weigh(at, total):
        here = pl.ds(pl.multiple_of(at * QB, QB), QB)
        values = jnp.exp(score[here, :] - most)
        prob[here, :] = values.astype(jnp.bfloat16)
        return total + jnp.sum(values.reshape(QB // 8, 8, 2 * QB), axis=0)

    total = lax.fori_loop(
        0, length // QB, weigh, jnp.zeros((8, 2 * QB), jnp.float32), unroll=True
    )
    total = jnp.sum(total, axis=0, keepdims=True)
    mixed = dot_nn(vt[...], prob[...]) / total
    out_ref[...] = own_halves(mixed).astype(out_ref.dtype)
    log_ref[0] = most + jnp.log(total)


def attend(queries, key_values, offsets, traffic):
    rows, length = queries.shape[0], key_values.shape[0]
    blocks = rows // QB
    return pl.pallas_call(
        functools.partial(attend_kernel, rows, length, traffic),
        grid=(PAIRS, blocks),
        out_shape=[
            jax.ShapeDtypeStruct((rows, D), jnp.bfloat16),
            jax.ShapeDtypeStruct((PAIRS * blocks, 1, 2 * QB), jnp.float32),
        ]
        + traffic.out_shapes(),
        in_specs=[
            pl.BlockSpec((1, 8, QB), lambda p, b: (p, 0, 0)),
            pl.BlockSpec((QB, 2 * DH), lambda p, b: (b, p)),
            pl.BlockSpec((length, 2 * DH), lambda p, b: (0, p)),
            pl.BlockSpec((length, 2 * DH), lambda p, b: (0, PAIRS + p)),
        ]
        + traffic.in_specs(),
        out_specs=[
            pl.BlockSpec((QB, 2 * DH), lambda p, b: (b, p)),
            pl.BlockSpec((1, 1, 2 * QB), lambda p, b: (p * blocks + b, 0, 0)),
        ]
        + traffic.out_specs(),
        scratch_shapes=[
            pltpu.VMEM((2 * length - QB, 2 * QB), jnp.float32),
            pltpu.VMEM((length, 2 * QB), jnp.float32),
            pltpu.VMEM((length, 2 * QB), jnp.bfloat16),
            pltpu.VMEM((2 * DH, length), jnp.bfloat16),
        ]
        + traffic.scratch(),
        compiler_params=traffic_params(traffic),
    )(offsets, queries, key_values, key_values, *traffic.operands())


def attend_back_kernel(
    rows, length, traffic, rows_ref, q_ref, k_ref, v_ref, g_ref, log_ref, *refs
):
    moved = len(traffic.operands())
    ins, refs = refs[:moved], refs[moved:]
    (dq_ref, dk_ref, dv_ref, near_ref, sums_ref), refs = refs[:5], refs[5:]
    outs, refs = refs[:moved], refs[moved:]
    (strip, score, slope, prob, change, kt, dk_sum, dv_sum, near), refs = refs[:9], refs[9:]
    block, blocks = pl.program_id(1), rows // QB
    run_plan(traffic.plan(ins, outs, refs), pl.program_id(0) * blocks + block, PAIRS * blocks)

    @pl.when(block == 0)
    def _():
        fill_strip(strip, rows_ref, length)
        kt[...] = k_ref[...].T
        dk_sum[...] = jnp.zeros_like(dk_sum)
        dv_sum[...] = jnp.zeros_like(dv_sum)
        near[...] = jnp.zeros_like(near)
        change[0:QB, :] = jnp.zeros((QB, 2 * QB), jnp.bfloat16)
        change[length + QB : length + 2 * QB, :] = jnp.zeros((QB, 2 * QB), jnp.bfloat16)

    start, first = strip_start(rows, length)
    q_both = stacked(q_ref[...] * 0.125)
    g_both = stacked(g_ref[...])
    score[...] = dot_nt(k_ref[...], q_both)
    slope[...] = dot_nt(v_ref[...], g_both)
    log_total = log_ref[0]

    def weigh(at, total):
        here = pl.ds(pl.multiple_of(at * QB, QB), QB)
        values = jnp.exp(
            score[here, :] + strip[pl.ds(pl.multiple_of(start + at * QB, QB), QB), :] - log_total
        )
        score[here, :] = values
        prob[here, :] = values.astype(jnp.bfloat16)
        return total + jnp.sum((values * slope[here, :]).reshape(QB // 8, 8, 2 * QB), axis=0)

    centre = lax.fori_loop(
        0, length // QB, weigh, jnp.zeros((8, 2 * QB), jnp.float32), unroll=True
    )
    centre = jnp.sum(centre, axis=0, keepdims=True)

    for at in range(length // QB):
        here = pl.ds(at * QB, QB)
        values = score[here, :] * (slope[here, :] - centre)
        change[pl.ds(at * QB + QB, QB), :] = values.astype(jnp.bfloat16)
        sums_ref[0, at : at + 1, :] = jnp.sum(values, axis=0, keepdims=True)

    dv_sum[...] += dot_nn(prob[...], g_both)
    moved = change[QB : QB + length, :]
    dk_sum[...] += dot_nn(moved, q_both)
    dq_ref[...] = (own_halves(dot_nn(kt[...], moved)) * 0.125).astype(dq_ref.dtype)
    near[...] += change[pl.ds(pl.multiple_of(first, QB), BAND), :].astype(jnp.float32)

    @pl.when(block == pl.num_programs(1) - 1)
    def _():
        dk_ref[...] = dk_sum[...].astype(dk_ref.dtype)
        dv_ref[...] = dv_sum[...].astype(dv_ref.dtype)
        rows_of = lax.broadcasted_iota(jnp.int32, (QB, QB), 0)
        lanes_of = lax.broadcasted_iota(jnp.int32, (QB, QB), 1)
        for head in range(2):
            for tile in range(3):
                turned = near[tile * QB : (tile + 1) * QB, head * QB : (head + 1) * QB]
                step = 1
                while step < QB:
                    turned = jnp.where(
                        lax.rem(rows_of // step, 2) == 1, pltpu.roll(turned, QB - step, 1), turned
                    )
                    step *= 2
                upper = jnp.where((lanes_of >= 1) & (lanes_of + rows_of < QB), turned, 0.0)
                for half, piece in enumerate((upper, turned - upper)):
                    at = head * 6 + tile * 2 + half
                    near_ref[0, at : at + 1, :] = jnp.sum(piece, axis=0, keepdims=True)


def attend_back(queries, key_values, offsets, log_total, grads, traffic):
    rows, length = queries.shape[0], key_values.shape[0]
    blocks = rows // QB
    big = (length, 2 * QB)
    return pl.pallas_call(
        functools.partial(attend_back_kernel, rows, length, traffic),
        grid=(PAIRS, blocks),
        out_shape=[
            jax.ShapeDtypeStruct((rows, D), jnp.bfloat16),
            jax.ShapeDtypeStruct((length, D), jnp.bfloat16),
            jax.ShapeDtypeStruct((length, D), jnp.bfloat16),
            jax.ShapeDtypeStruct((PAIRS, 12, QB), jnp.float32),
            jax.ShapeDtypeStruct((PAIRS * blocks, length // QB, 2 * QB), jnp.float32),
        ]
        + traffic.out_shapes(),
        in_specs=[
            pl.BlockSpec((1, 8, QB), lambda p, b: (p, 0, 0)),
            pl.BlockSpec((QB, 2 * DH), lambda p, b: (b, p)),
            pl.BlockSpec((length, 2 * DH), lambda p, b: (0, p)),
            pl.BlockSpec((length, 2 * DH), lambda p, b: (0, PAIRS + p)),
            pl.BlockSpec((QB, 2 * DH), lambda p, b: (b, p)),
            pl.BlockSpec((1, 1, 2 * QB), lambda p, b: (p * blocks + b, 0, 0)),
        ]
        + traffic.in_specs(),
        out_specs=[
            pl.BlockSpec((QB, 2 * DH), lambda p, b: (b, p)),
            pl.BlockSpec((length, 2 * DH), lambda p, b: (0, p)),
            pl.BlockSpec((length, 2 * DH), lambda p, b: (0, p)),
            pl.BlockSpec((1, 12, QB), lambda p, b: (p, 0, 0)),
            pl.BlockSpec((1, length // QB, 2 * QB), lambda p, b: (p * blocks + b, 0, 0)),
        ]
        + traffic.out_specs(),
        scratch_shapes=[
            pltpu.VMEM((2 * length - QB, 2 * QB), jnp.float32),
            pltpu.VMEM(big, jnp.float32),
            pltpu.VMEM(big, jnp.float32),
            pltpu.VMEM(big, jnp.bfloat16),
            pltpu.VMEM((length + 2 * QB, 2 * QB), jnp.bfloat16),
            pltpu.VMEM((2 * DH, length), jnp.bfloat16),
            pltpu.VMEM((length, 2 * DH), jnp.float32),
            pltpu.VMEM((length, 2 * DH), jnp.float32),
            pltpu.VMEM((BAND, 2 * QB), jnp.float32),
        ]
        + traffic.scratch(),
        compiler_params=traffic_params(traffic),
    )(offsets, queries, key_values, key_values, grads, log_total, *traffic.operands())


def table_back(near, sums, first_block):
    blocks = sums.shape[0] // PAIRS
    count = sums.shape[1]
    lane = jnp.arange(QB, dtype=jnp.int32)[None, None, :]
    tile = jnp.arange(3, dtype=jnp.int32)[:, None, None]
    half = jnp.arange(2, dtype=jnp.int32)[None, :, None]
    behind = jnp.where(half == 0, jnp.where(lane == 0, QB, lane), jnp.where(lane == 0, 0, lane - QB))
    offsets = (tile - 1) * QB - behind
    onehot = (bucket_of(offsets)[..., None] == jnp.arange(NB)).astype(jnp.float32)
    close = jnp.einsum(
        "zthl,thlb->zb",
        near.reshape(H, 3, 2, QB),
        onehot,
        precision=lax.Precision.HIGHEST,
    )
    by_block = sums.reshape(PAIRS, blocks, count, 2, QB).sum(axis=4)
    here = first_block + jnp.arange(blocks, dtype=jnp.int32)[:, None]
    there = jnp.arange(count, dtype=jnp.int32)[None, :]
    below = jnp.einsum(
        "pbch,bc->ph", by_block, (there < here - 1).astype(jnp.float32), precision=lax.Precision.HIGHEST
    ).reshape(H)
    above = jnp.einsum(
        "pbch,bc->ph", by_block, (there > here + 1).astype(jnp.float32), precision=lax.Precision.HIGHEST
    ).reshape(H)
    spread = jnp.arange(NB)[None, :]
    close = close + jnp.where(spread == NB // 2 - 1, below[:, None], 0.0)
    return close + jnp.where(spread == NB - 1, above[:, None], 0.0)


EDGE = 16
LANES = 128
BLOCK = 128


def shifted_rows(window):
    for low in range(8):
        turned = pltpu.roll(window, window.shape[0] - low, 0) if low else window
        for high in range(4):
            offset = 8 * high + low
            if 1 <= offset <= KERNEL:
                yield offset, turned[8 * high : 8 * high + BLOCK, :]


def conv_kernel(traffic, padded_ref, taps_ref, norms_ref, *refs):
    moved = len(traffic.operands())
    ins, refs = refs[:moved], refs[moved:]
    (depth_ref, post_ref), refs = refs[:2], refs[2:]
    outs, refs = refs[:moved], refs[moved:]
    step = pl.program_id(0)
    run_plan(traffic.plan(ins, outs, refs), step, CONV_BLOCKS)
    first = pl.multiple_of(step * BLOCK, BLOCK)

    @pl.loop(0, C // LANES)
    def _(at):
        lanes = pl.ds(pl.multiple_of(at * LANES, LANES), LANES)
        window = padded_ref[pl.ds(first, BLOCK + 2 * EDGE), lanes].astype(jnp.float32)
        total = jnp.zeros((BLOCK, LANES), jnp.float32)
        for offset, rows in shifted_rows(window):
            total = total + rows * taps_ref[offset - 1 : offset, lanes]
        depth_ref[:, lanes] = total

    @pl.loop(0, BLOCK // 16)
    def _(at):
        here = pl.ds(pl.multiple_of(at * 16, 16), 16)
        scaled, _ = norm_parts(depth_ref[here, :])
        normed = scaled * norms_ref[0:1, :] + norms_ref[1:2, :]
        post_ref[here, :] = (normed * sigmoid(normed)).astype(jnp.bfloat16)


CONV_BLOCKS = 5


def convolve(padded, taps, norms, traffic):
    rows = padded.shape[0] - 2 * EDGE
    return pl.pallas_call(
        functools.partial(conv_kernel, traffic),
        grid=(CONV_BLOCKS,),
        out_shape=[
            jax.ShapeDtypeStruct((rows, C), jnp.float32),
            jax.ShapeDtypeStruct((rows, C), jnp.bfloat16),
        ]
        + traffic.out_shapes(),
        in_specs=[resident(padded.shape), resident(taps.shape), resident(norms.shape)]
        + traffic.in_specs(),
        out_specs=[
            pl.BlockSpec((BLOCK, C), lambda step: (step, 0)),
            pl.BlockSpec((BLOCK, C), lambda step: (step, 0)),
        ]
        + traffic.out_specs(),
        scratch_shapes=traffic.scratch(),
        compiler_params=traffic_params(traffic),
    )(padded, taps, norms, *traffic.operands())


def conv_back_kernel(traffic, change_ref, gated_ref, first_ref, second_ref, taps_ref, *refs):
    moved = len(traffic.operands())
    ins, refs = refs[:moved], refs[moved:]
    (g_first_ref, g_second_ref, g_taps_ref), refs = refs[:3], refs[3:]
    outs, refs = refs[:moved], refs[moved:]
    sums, refs = refs[0], refs[1:]
    run_plan(traffic.plan(ins, outs, refs), pl.program_id(0), C // LANES)
    sums[...] = jnp.zeros_like(sums)

    @pl.loop(0, CONV_BLOCKS)
    def _(block):
        first = pl.multiple_of(block * BLOCK, BLOCK)
        here = pl.ds(first, BLOCK)
        around = pl.ds(first, BLOCK + 2 * EDGE)
        window = change_ref[around, :].astype(jnp.float32)
        total = jnp.zeros((BLOCK, LANES), jnp.float32)
        for offset, rows in shifted_rows(window):
            total = total + rows * taps_ref[KERNEL - offset : KERNEL - offset + 1, :]
        gate = sigmoid(second_ref[here, :].astype(jnp.float32))
        through = total * gate
        g_first_ref[here, :] = through.astype(jnp.bfloat16)
        g_second_ref[here, :] = (
            through * first_ref[here, :].astype(jnp.float32) * (1.0 - gate)
        ).astype(jnp.bfloat16)

        change = change_ref[pl.ds(pl.multiple_of(first + EDGE, EDGE), BLOCK), :].astype(jnp.float32)
        window = gated_ref[around, :].astype(jnp.float32)
        for offset, rows in shifted_rows(window):
            part = jnp.sum((rows * change).reshape(BLOCK // 8, 8, LANES), axis=0)
            sums[8 * (offset - 1) : 8 * offset, :] += part

    for tap in range(KERNEL):
        g_taps_ref[tap : tap + 1, :] = jnp.sum(sums[8 * tap : 8 * tap + 8, :], axis=0, keepdims=True)


def convolve_back(change, gated, paired, taps, traffic):
    rows = change.shape[0] - 2 * EDGE
    half = C // LANES
    column = pl.BlockSpec((rows, LANES), lambda step: (0, step))
    edged = pl.BlockSpec((rows + 2 * EDGE, LANES), lambda step: (0, step))
    return pl.pallas_call(
        functools.partial(conv_back_kernel, traffic),
        grid=(half,),
        out_shape=[
            jax.ShapeDtypeStruct((rows, C), jnp.bfloat16),
            jax.ShapeDtypeStruct((rows, C), jnp.bfloat16),
            jax.ShapeDtypeStruct((KERNEL + 1, C), jnp.float32),
        ]
        + traffic.out_shapes(),
        in_specs=[
            edged,
            edged,
            column,
            pl.BlockSpec((rows, LANES), lambda step: (0, half + step)),
            pl.BlockSpec((KERNEL + 1, LANES), lambda step: (0, step)),
        ]
        + traffic.in_specs(),
        out_specs=[column, column, pl.BlockSpec((KERNEL + 1, LANES), lambda step: (0, step))]
        + traffic.out_specs(),
        scratch_shapes=[pltpu.VMEM((8 * KERNEL, LANES), jnp.float32)] + traffic.scratch(),
        compiler_params=traffic_params(traffic),
    )(change, gated, paired, paired, taps, *traffic.operands())


def as_shard(array):
    rows = array.shape[0]
    return array if rows % 16 == 0 else array.reshape(16, rows * array.shape[1] // 16)


def as_weight(whole, like):
    devices = math.prod(whole.shape[:3])
    return whole.reshape(devices * like.shape[0], like.shape[1])


def as_parts(grad, sizes, like):
    chips, frames = sizes
    shard = as_shard(jnp.zeros(like.shape, jnp.bfloat16)).shape
    return grad.reshape((chips, 2, frames) + shard)


def pack_small(values, small_shapes):
    flat = jnp.concatenate([value.reshape(-1) for value in values])
    return jnp.pad(flat, (0, SMALL[0] * SMALL[1] - flat.shape[0])).reshape(SMALL)


def unpack_small(packed, shapes):
    devices = packed.shape[0]
    at, out = 0, []
    for shape in shapes:
        size = math.prod(shape)
        piece = packed[:, at : at + size].reshape((devices,) + shape)
        at += size
        piece = jnp.moveaxis(piece, 0, -2)
        out.append(piece.reshape(shape[:-1] + (devices * shape[-1],)))
    return out


def repack_small(values, shapes, devices):
    pieces = []
    for value, shape in zip(values, shapes):
        piece = value.reshape(shape[:-1] + (devices, shape[-1]))
        pieces.append(jnp.moveaxis(piece, -2, 0).reshape(devices, -1))
    flat = jnp.concatenate(pieces, axis=1)
    return jnp.pad(flat, ((0, 0), (0, SMALL[0] * SMALL[1] - flat.shape[1])))


def shards(
    frames_in,
    positions,
    mask_vector,
    norm_gains,
    norm_biases,
    depth_gain,
    depth_bias,
    early_in,
    early_out,
    qkv_weight,
    mixer_out,
    pointwise_in,
    pointwise_out,
    depth_kernel,
    late_in,
    late_out,
    position_bias,
    cotangent,
):
    groups, run, model_width = frames_in.shape
    line = lax.axis_size("frames")
    chips = lax.axis_size("batch") // 2
    sizes = (chips, line)
    devices = 2 * chips * line
    length = run * line
    rows = groups * run
    batch, depth = lax.axis_index("batch"), lax.axis_index("frames")
    core = lax.rem(batch, 2)
    first_frame = core * rows
    partner = [(at, at + 1 - 2 * (at % 2)) for at in range(2 * chips)]

    def from_other(array):
        return lax.ppermute(array, "batch", partner)

    big = [early_in, early_out, qkv_weight, mixer_out, pointwise_in, pointwise_out, late_in, late_out]
    small = [mask_vector, norm_gains, norm_biases, depth_gain, depth_bias, depth_kernel, position_bias]
    small_shapes = [value.shape for value in small]
    small_size = sum(math.prod(shape) for shape in small_shapes)
    shard_of = [as_shard(value) for value in big]
    gathered = move(
        Traffic(
            sizes,
            0,
            shards=shard_of[:2] + [pack_small(small, small_shapes)],
            swapped=[frames_in],
            swap_at=2,
        )
    )
    w_early_in, w_early_out = as_weight(gathered[0], early_in), as_weight(gathered[1], early_out)
    small_whole = gathered[2].reshape(devices, SMALL[0] * SMALL[1])
    mask_full, gains, biases, channel_gain, channel_bias, kernel_full, table = [
        value.astype(jnp.float32) for value in unpack_small(small_whole, small_shapes)
    ]
    table = table.reshape(H, NB)
    frames_here = gathered[3].reshape(rows, D)

    both = jnp.where(core == 0, 0, 1)
    other_positions = from_other(positions)
    owner = depth // groups
    listed = jnp.where(owner == both, positions, other_positions)
    listed = lax.dynamic_index_in_dim(listed, lax.rem(depth, groups), 0, keepdims=False)
    frame_ids = first_frame + jnp.arange(rows, dtype=jnp.int32)
    masked = jnp.any(listed[:, None] == frame_ids[None, :], axis=0).reshape(rows, 1)

    offsets = offset_rows(table)

    def norms_of(*which):
        rows_of = [row for at in which for row in (gains[at], biases[at])]
        return jnp.stack(rows_of + [jnp.zeros((D,), jnp.float32)] * (8 - len(rows_of)))

    def parts(grad, like):
        return as_parts(grad, sizes, like)

    def in_order(mine, other):
        return jnp.where(
            core == 0,
            jnp.concatenate([mine, other], axis=0),
            jnp.concatenate([other, mine], axis=0),
        )

    def halves(whole):
        first, second = whole[:rows], whole[rows:]
        return jnp.where(core == 0, first, second), jnp.where(core == 0, second, first)

    hidden0 = jnp.where(masked, mask_full[None, :], frames_here.astype(jnp.float32))
    hidden1, inner1, normed1, normed2, *gathered = ffn(
        hidden0, norms_of(0, 1), w_early_in, w_early_out, Traffic(sizes, 1, shards=shard_of[2:4])
    )
    w_qkv, w_mixer = as_weight(gathered[0], qkv_weight), as_weight(gathered[1], mixer_out)
    packed = product(normed2, w_qkv).astype(jnp.bfloat16)
    key_values = in_order(packed[:, D:], from_other(packed[:, D:]))
    mixed_rows, log_total, *gathered = attend(
        packed, key_values, offsets, Traffic(sizes, 2, shards=shard_of[4:6], swapped=[cotangent], swap_at=3)
    )
    w_point_in = as_weight(gathered[0], pointwise_in)
    w_point_out = as_weight(gathered[1], pointwise_out)
    upstream = gathered[2].reshape(rows, D).astype(jnp.float32)
    hidden2 = hidden1 + product(mixed_rows, w_mixer)

    normed3 = layer_norm(hidden2, gains[2], biases[2]).astype(jnp.bfloat16)
    paired = product(normed3, w_point_in).astype(jnp.bfloat16)
    gated = gated_unit(paired.astype(jnp.float32)).astype(jnp.bfloat16)

    def with_edges(array):
        sent = jnp.where(core == 0, array[rows - EDGE :], array[:EDGE])
        edge = from_other(sent)
        nothing = jnp.zeros_like(edge)
        return jnp.concatenate(
            [jnp.where(core == 0, nothing, edge), array, jnp.where(core == 0, edge, nothing)], axis=0
        )

    padded = with_edges(gated)
    taps = jnp.pad(kernel_full, ((0, 1), (0, 0)))
    channel_norms = jnp.pad(jnp.stack([channel_gain, channel_bias]), ((0, 6), (0, 0)))
    depth_values, post, *gathered = convolve(
        padded, taps, channel_norms, Traffic(sizes, 3, shards=shard_of[6:])
    )
    w_late_in, w_late_out = as_weight(gathered[0], late_in), as_weight(gathered[1], late_out)
    hidden3 = hidden2 + product(post, w_point_out)
    hidden4, inner5, normed5, activations = ffn(
        hidden3, norms_of(3, 4), w_late_in, w_late_out, Traffic(sizes, None)
    )

    grad4, gain_grad4, bias_grad4 = norm_back(hidden4, gains[4], biases[4], upstream)
    grad3, late_in_grad, late_out_grad, norm_sums3 = ffn_back(
        hidden3, normed5, grad4, norms_of(3), inner5, w_late_in, w_late_out, Traffic(sizes, None)
    )
    grad_out3 = grad3.astype(jnp.bfloat16)
    pointwise_out_grad = weight_grad(post, grad_out3)
    grad_post = back_product(grad_out3, w_point_out)
    post_unused, post_pull = jax.vjp(depth_post, depth_values, channel_gain, channel_bias)
    grad_depth, channel_gain_grad, channel_bias_grad = post_pull(grad_post)
    grad_depth_low = grad_depth.astype(jnp.bfloat16)
    grad_first, grad_second, taps_grad, *sums_late = convolve_back(
        with_edges(grad_depth_low),
        padded,
        paired,
        taps,
        Traffic(
            sizes, 4, grads=[parts(late_out_grad, late_out), parts(late_in_grad, late_in)]
        ),
    )
    kernel_grad = taps_grad[:KERNEL]
    grad_paired = jnp.concatenate([grad_first, grad_second], axis=1)
    pointwise_in_grad = weight_grad(normed3, grad_paired)
    grad_normed3 = back_product(grad_paired, w_point_in)
    grad_in3, gain_grad2, bias_grad2 = norm_back(hidden2, gains[2], biases[2], grad_normed3)
    grad2 = grad3 + grad_in3

    grad_out2 = grad2.astype(jnp.bfloat16)
    mixer_out_grad = weight_grad(mixed_rows, grad_out2)
    grad_mixed = back_product(grad_out2, w_mixer).astype(jnp.bfloat16)
    grad_queries, grad_keys, grad_values, near, far_sums, *sums_depth = attend_back(
        packed,
        key_values,
        offsets,
        log_total,
        grad_mixed,
        Traffic(
            sizes,
            5,
            grads=[parts(pointwise_out_grad, pointwise_out), parts(pointwise_in_grad, pointwise_in)],
            swapped=[activations.reshape(groups, run, D)],
        ),
    )
    table_grad = table_back(near, far_sums, core * (rows // QB)).reshape(H * NB)
    keys_own, keys_other = halves(grad_keys)
    values_own, values_other = halves(grad_values)
    keys_there, values_there = from_other(keys_other), from_other(values_other)
    grad_packed = jnp.concatenate(
        [
            grad_queries,
            (keys_own.astype(jnp.float32) + keys_there.astype(jnp.float32)).astype(jnp.bfloat16),
            (values_own.astype(jnp.float32) + values_there.astype(jnp.float32)).astype(jnp.bfloat16),
        ],
        axis=-1,
    )
    qkv_grad = weight_grad(normed2, grad_packed)
    grad_normed2 = back_product(grad_packed, w_qkv)
    grad_in2, gain_grad1, bias_grad1 = norm_back(hidden1, gains[1], biases[1], grad_normed2)
    grad1 = grad2 + grad_in2
    grad0, early_in_grad, early_out_grad, norm_sums0, *sums_mixer = ffn_back(
        hidden0,
        normed1,
        grad1,
        norms_of(0),
        inner1,
        w_early_in,
        w_early_out,
        Traffic(sizes, 6, grads=[parts(mixer_out_grad, mixer_out), parts(qkv_grad, qkv_weight)]),
    )
    grad_frames = jnp.where(masked, 0.0, grad0).astype(jnp.bfloat16)
    mask_grad = jnp.sum(jnp.where(masked, grad0, 0.0), axis=0)
    gain_stack = jnp.stack([norm_sums0[0], gain_grad1, gain_grad2, norm_sums3[0], gain_grad4])
    bias_stack = jnp.stack([norm_sums0[1], bias_grad1, bias_grad2, norm_sums3[1], bias_grad4])
    small_grads = repack_small(
        [mask_grad, gain_stack, bias_stack, channel_gain_grad, channel_bias_grad, kernel_grad, table_grad],
        small_shapes,
        devices,
    ).astype(jnp.bfloat16)

    sums_early = move(
        Traffic(
            sizes,
            7,
            grads=[
                parts(early_out_grad, early_out),
                parts(early_in_grad, early_in),
                small_grads.reshape((chips, 2, line) + SMALL),
            ],
            swapped=[grad_frames.reshape(groups, run, D)],
        )
    )
    small_sums = sums_early[2].reshape(-1)[:small_size]
    small_out, at = [], 0
    for shape in small_shapes:
        size = math.prod(shape)
        small_out.append(small_sums[at : at + size].reshape(shape))
        at += size
    return (
        sums_depth[2],
        sums_early[3].astype(jnp.float32),
        small_out[0],
        small_out[1],
        small_out[2],
        small_out[3],
        small_out[4],
        sums_early[1].reshape(early_in.shape),
        sums_early[0].reshape(early_out.shape),
        sums_mixer[1].reshape(qkv_weight.shape),
        sums_mixer[0].reshape(mixer_out.shape),
        sums_depth[1].reshape(pointwise_in.shape),
        sums_depth[0].reshape(pointwise_out.shape),
        small_out[5],
        sums_late[1].reshape(late_in.shape),
        sums_late[0].reshape(late_out.shape),
        small_out[6],
    )


def solution(mesh):
    in_specs = (
        P("batch", "frames", None),
        P("batch", None),
        P(("batch", "frames")),
        P(None, ("batch", "frames")),
        P(None, ("batch", "frames")),
        P(("batch", "frames")),
        P(("batch", "frames")),
        P(("batch", "frames"), None),
        P(("batch", "frames"), None),
        P(("batch", "frames"), None),
        P(("batch", "frames"), None),
        P(("batch", "frames"), None),
        P(("batch", "frames"), None),
        P(None, ("batch", "frames")),
        P(("batch", "frames"), None),
        P(("batch", "frames"), None),
        P(("batch", "frames")),
        P("batch", "frames", None),
    )
    out_specs = (
        P("batch", "frames", None),
        P("batch", "frames", None),
        P(("batch", "frames")),
        P(None, ("batch", "frames")),
        P(None, ("batch", "frames")),
        P(("batch", "frames")),
        P(("batch", "frames")),
        P(("batch", "frames"), None),
        P(("batch", "frames"), None),
        P(("batch", "frames"), None),
        P(("batch", "frames"), None),
        P(("batch", "frames"), None),
        P(("batch", "frames"), None),
        P(None, ("batch", "frames")),
        P(("batch", "frames"), None),
        P(("batch", "frames"), None),
        P(("batch", "frames")),
    )
    return jax.shard_map(shards, mesh=mesh, in_specs=in_specs, out_specs=out_specs, check_vma=False)
```

```python
import functools
import math

import jax
import jax.numpy as jnp
from jax import lax
from jax.experimental import pallas as pl
from jax.experimental.pallas import tpu as pltpu
from jax.sharding import PartitionSpec as P

D = 1024
H = 16
DH = 64
C = 2048
KERNEL = 31
HALF = 15
NB = 32
EPS = 1e-05
LIMITS = (8, 12, 16, 24, 32, 48, 64, 96)
BOTH = ("batch", "frames")
SMALL = (16, 512)


MESH = pl.DeviceIdType.MESH
VMEM_BYTES = 58 * 1024 * 1024


def ring_spot(index, count):
    half = count // 2
    return index + (index // half) * (3 * half - 1 - 2 * index)


def places(chips, frames):
    batch, depth = lax.axis_index("batch"), lax.axis_index("frames")
    chip, core = batch // 2, lax.rem(batch, 2)
    spot = ring_spot(chip, chips)

    def chip_at(offset):
        return ring_spot(lax.rem(spot + offset + chips, chips), chips)

    return chip, core, depth, chip_at


def greet(chips, frames, partners):
    chip, core, depth, chip_at = places(chips, frames)
    barrier = pltpu.get_barrier_semaphore()
    for offset in (1, -1):
        pl.semaphore_signal(
            barrier, inc=1, device_id=(chip_at(offset) * 2 + core, depth), device_id_type=MESH
        )
    pl.semaphore_signal(
        barrier, inc=1, device_id=(chip * 2 + 1 - core, depth), device_id_type=MESH
    )

    @pl.when(depth > 0)
    def _():
        pl.semaphore_signal(barrier, inc=1, device_id=(chip * 2 + core, depth - 1), device_id_type=MESH)

    @pl.when(depth < frames - 1)
    def _():
        pl.semaphore_signal(barrier, inc=1, device_id=(chip * 2 + core, depth + 1), device_id_type=MESH)

    count = 3 + jnp.minimum(depth, 1) + jnp.minimum(frames - 1 - depth, 1)
    if partners:
        groups = frames // 2
        for place in range(groups):
            there, side = core * groups + place, depth // groups

            @pl.when(jnp.logical_or(there != depth, side != core))
            def _():
                pl.semaphore_signal(
                    barrier, inc=1, device_id=(chip * 2 + side, there), device_id_type=MESH
                )

        count = count + groups - (1 - jnp.abs(depth // groups - core))
    pl.semaphore_wait(barrier, count)


def swap_frames(chips, frames, sources, targets, send_sems, recv_sems, local_sem):
    chip, core, depth, chip_at = places(chips, frames)
    groups = frames // 2
    starts, ends = [], []
    for at, (source, target) in enumerate(zip(sources, targets)):
        for place in range(groups):
            there, side = core * groups + place, depth // groups
            mine = jnp.logical_and(there == depth, side == core)
            slot = lax.rem(depth, groups)
            remote = pltpu.make_async_remote_copy(
                src_ref=source.at[place],
                dst_ref=target.at[slot],
                send_sem=send_sems.at[at * groups + place],
                recv_sem=recv_sems.at[at * groups + slot],
                device_id=(chip * 2 + side, there),
                device_id_type=MESH,
            )
            arrival = pltpu.make_async_remote_copy(
                src_ref=source.at[place],
                dst_ref=target.at[place],
                send_sem=send_sems.at[at * groups + place],
                recv_sem=recv_sems.at[at * groups + place],
                device_id=(chip * 2 + side, there),
                device_id_type=MESH,
            )
            here = pltpu.make_async_copy(source.at[place], target.at[slot], local_sem.at[at])
            away = jnp.logical_not(mine)
            starts += [gated(away, remote.start), gated(mine, here.start)]
            ends += [
                gated(away, remote.wait_send),
                gated(away, arrival.wait_recv),
                gated(mine, here.wait),
            ]
    return starts, ends


def gated(condition, action):
    if condition is None:
        return action
    return lambda: pl.when(condition)(action)


def shares(columns, split):
    first = columns * split // 8
    if first % 256 or (columns - first) % 256:
        first = columns
    return (0, first), (first, columns - first)


class Timetable:
    def __init__(self, sizes, split):
        chips, frames = sizes
        half = chips // 2
        self.known = chips == 4 and frames == 4
        self.both = split < 8
        self.half, self.frames = half, frames

    def gather(self, distance, step):
        if not self.known:
            return distance + step + 0.1 * bool(step)
        if self.both:
            return ((0, 0.95, 2.45, 3.7), (1.0, 2.6, 3.75, 4.5), (3.0, 4.5, 4.9, 4.9))[step][distance]
        return ((0, 0.95, 1.95, 2.95), (1.0, 3.0, 4.5, 5.0), (3.5, 4.6, 5.6, 6.0))[step][distance]

    def gather_ring(self, distance, step):
        if not self.known:
            return distance + step
        return ((0, 1.0, 3.0), (1.0, 2.5, 4.25), (2.5, 4.25, 5.0), (4.0, 5.0, 5.25))[step][distance]

    def pair(self, distance):
        if not self.known:
            return distance + self.half + 0.5
        if self.both:
            return (3.05, 4.55, 5.05, 5.3)[distance]
        return (3.55, 4.65, 5.65, 6.05)[distance]

    def merge(self, distance):
        if not self.known:
            return 0.01 * (self.frames - distance)
        return (1.3, 1.0, 0.7, 0.35)[distance]

    def scatter(self, distance, step):
        if not self.known:
            return self.frames - 1 - distance + step
        if self.both:
            return ((4.29, 3.49, 2.69, 1.35), (5.1, 4.3, 3.5, 2.7))[step - 1][distance]
        return ((2.6, 2.2, 1.8, 1.4), (6.4, 5.4, 4.4, 3.4))[step - 1][distance]

    def scatter_ring(self, distance, step):
        if not self.known:
            return self.half - distance + step + 0.5
        return ((2.66, 1.33, 0.4), (3.46, 2.67, 1.34), (4.27, 3.47, 2.68), (5.0, 4.28, 3.48))[step][distance]

    def scatter_last(self, distance):
        if not self.known:
            return self.half - distance + self.frames - 1 + 0.5
        return (5.1, 4.29)[distance]


class Mover:
    def __init__(self, spots, sizes, split, send_sems, recv_sems):
        self.time = Timetable(sizes, split)
        self.chips, self.frames = sizes
        self.chip, self.core, self.depth, self.chip_at = spots
        self.send_sems, self.recv_sems = send_sems, recv_sems
        self.used = 0
        self.events = []
        self.departures = []

    def copy(self, source, target, device, condition):
        at = self.used
        self.used += 1
        made = pltpu.make_async_remote_copy(
            src_ref=source,
            dst_ref=target,
            send_sem=self.send_sems.at[at],
            recv_sem=self.recv_sems.at[at],
            device_id=device,
            device_id_type=MESH,
        )
        self.departures.append(gated(condition, made.wait_send))
        return made

    def at(self, time, *actions):
        self.events += [(time, action) for action in actions]

    def other_core(self):
        return (self.chip * 2 + 1 - self.core, self.depth)

    def group(self, offset):
        at = self.depth + offset
        if offset == 0:
            return at, None
        return jnp.clip(at, 0, self.frames - 1), jnp.logical_and(at >= 0, at < self.frames)

    def chips_at(self, distance):
        if distance == 0:
            return (self.chip,)
        if distance == self.chips // 2:
            return (self.chip_at(distance),)
        return (self.chip_at(distance), self.chip_at(-distance))

    def offsets(self, distance):
        return (0,) if distance == 0 else (-distance, distance)


class Gather(Mover):
    def __init__(self, spots, sizes, shard, whole, split, send_sems, recv_sems, local_sems):
        super().__init__(spots, sizes, split, send_sems, recv_sems)
        self.shard, self.whole = shard, whole
        self.first, self.last = shares(shard.shape[1], split)
        self.local = pltpu.make_async_copy(
            shard, whole.at[self.chip, self.core, self.depth], local_sems.at[0]
        )
        self.at(0, self.local.start)
        for distance in range(self.frames):
            self.spread(distance)
        if self.last[1]:
            for distance in range(self.chips // 2 + 1):
                self.spread_ring(distance)
        for distance in range(self.frames):
            self.hand_over(distance)
        self.ends = self.departures

    def spread(self, distance):
        chip, core, depth, half = self.chip, self.core, self.depth, self.chips // 2
        for offset in self.offsets(distance):
            held, valid = self.group(offset)
            start, columns = self.first
            block = self.whole.at[chip, core, held, :, pl.ds(start, columns)]
            source = block if distance else self.shard.at[:, pl.ds(start, columns)]
            for way in (1, -1):
                if distance + 1 == self.frames or offset * way > 0:
                    continue
                into, there = self.group(way)
                condition = there if valid is None else jnp.logical_and(valid, there)
                made = self.copy(source, block, (chip * 2 + core, into), condition)
                self.at(self.time.gather(distance, 0), gated(condition, made.start))
                comes = self.group(offset - way)[1]
                self.at(self.time.gather(distance + 1, 0), gated(comes, made.wait_recv))
            for step in range(1, half + 1):
                for side, way in enumerate((1, -1)):
                    part = pl.ds(start, columns)
                    if step == half:
                        part = pl.ds(start + side * columns // 2, columns // 2)
                    origin = self.chip_at(-way * (step - 1))
                    target = self.whole.at[origin, core, held, :, part]
                    given = self.shard.at[:, part] if distance == 0 and step == 1 else target
                    made = self.copy(given, target, (self.chip_at(way) * 2 + core, depth), valid)
                    self.at(self.time.gather(distance, step - 1), gated(valid, made.start))
                    self.at(self.time.gather(distance, step), gated(valid, made.wait_recv))

    def hand_over(self, distance):
        for offset in self.offsets(distance):
            held, valid = self.group(offset)
            line = self.whole.at[:, self.core, held]
            pair = self.copy(line, line, self.other_core(), valid)
            if distance == 0:
                self.at(self.time.pair(0), self.local.wait)
            self.at(self.time.pair(distance), gated(valid, pair.start))
            self.departures.append(gated(valid, pair.wait_recv))

    def spread_ring(self, distance):
        core, depth, half = self.core, self.depth, self.chips // 2
        start, columns = self.last
        everything = pl.ds(start, columns)
        if distance < half:
            step = distance + 1
            for side, way in enumerate((1, -1)):
                part = everything
                if step == half:
                    part = pl.ds(start + side * columns // 2, columns // 2)
                target = self.whole.at[self.chip_at(-way * distance), core, depth, :, part]
                given = target if distance else self.shard.at[:, part]
                made = self.copy(given, target, (self.chip_at(way) * 2 + core, depth), None)
                self.at(self.time.gather_ring(distance, 0), made.start)
                self.at(self.time.gather_ring(distance + 1, 0), made.wait_recv)
        for place, chip in enumerate(self.chips_at(distance)):
            for step in range(1, self.frames):
                for way in (1, -1):
                    held, there = self.group(-way * (step - 1))
                    into, beside = self.group(way)
                    valid = beside if there is None else jnp.logical_and(there, beside)
                    block = self.whole.at[chip, core, held, :, everything]
                    given = block if distance or step > 1 else self.shard.at[:, everything]
                    made = self.copy(given, block, (self.chip * 2 + core, into), valid)
                    self.at(self.time.gather_ring(distance, step - 1), gated(valid, made.start))
                    comes = self.group(-way * step)[1]
                    self.at(self.time.gather_ring(distance, step), gated(comes, made.wait_recv))


class Scatter(Mover):
    def __init__(
        self, spots, sizes, grads, out, total, stage, landings, split, send_sems, recv_sems, local_sems
    ):
        super().__init__(spots, sizes, split, send_sems, recv_sems)
        self.grads, self.out, self.total, self.stage = grads, out, total, stage
        (self.halves, self.fulls, self.lines), self.landings = landings[:3], list(landings[3:])
        self.local_sems = local_sems
        self.first, self.last = shares(out.shape[1], split)
        self.merges = 0
        for distance in reversed(range(self.frames)):
            self.collect(distance)
        if self.last[1]:
            for distance in reversed(range(self.chips // 2 + 1)):
                self.collect_ring(distance)
        self.ends = [self.finish] + self.departures

    def add(self, where, piece):
        total = self.total
        total[where] = total[where] + piece

    def merge(self, held, pair, load, stage):
        load.wait()
        pair.wait_recv()

        @pl.loop(0, self.chips)
        def _(chip):
            self.add((chip, held), stage[chip])

    def settle(self, made, where, landed):
        made.wait_recv()
        self.add(where, landed[...])

    def collect(self, distance):
        core, depth, half = self.core, self.depth, self.chips // 2
        for offset in self.offsets(distance):
            held, valid = self.group(offset)
            pair = self.copy(
                self.grads.at[:, 1 - core, held], self.total.at[:, held], self.other_core(), valid
            )
            stage = self.stage.at[held]
            load = pltpu.make_async_copy(
                self.grads.at[:, core, held], stage, self.local_sems.at[self.merges]
            )
            self.merges += 1
            begin = -0.01 * (distance + 1)
            self.at(begin, gated(valid, pair.start), gated(valid, load.start))
            self.at(
                self.time.merge(distance),
                gated(valid, functools.partial(self.merge, held, pair, load, stage)),
            )
            start, columns = self.first
            everything = pl.ds(start, columns)
            for step in range(1, half + 1):
                for side, way in enumerate((1, -1)):
                    part = everything
                    if step == 1:
                        part = pl.ds(start + side * columns // 2, columns // 2)
                    reach = half - step + 1
                    goal = self.chip_at(way * reach)
                    if step == 1:
                        landed = self.halves.at[held, side]
                    else:
                        landed = self.fulls.at[held, 2 * (step - 2) + side]
                    made = self.copy(
                        self.total.at[goal, held, :, part],
                        landed,
                        (self.chip_at(way) * 2 + core, depth),
                        valid,
                    )
                    ready = self.time.scatter(distance, step - 1) if step > 1 else self.time.merge(distance)
                    self.at(ready, gated(valid, made.start))
                    where = (self.chip_at(way * (reach - 1)), held, slice(None), part)
                    self.at(
                        self.time.scatter(distance, step),
                        gated(valid, functools.partial(self.settle, made, where, landed)),
                    )
            if distance == 0:
                continue
            way = 1 if offset > 0 else -1
            landed = self.lines.at[0 if way > 0 else 1, held]
            made = self.copy(
                self.total.at[self.chip, held, :, everything],
                landed,
                (self.chip * 2 + core, self.group(way)[0]),
                valid,
            )
            self.at(self.time.scatter(distance, half), gated(valid, made.start))
            before = self.group(-way)[1]
            goes, there = self.group(offset - way)
            comes = before if there is None else jnp.logical_and(before, there)
            where = (self.chip, goes, slice(None), everything)
            arrived = self.lines.at[0 if way > 0 else 1, goes]
            self.at(
                self.time.scatter(distance - 1, half) - 0.01,
                gated(comes, functools.partial(self.settle, made, where, arrived)),
            )

    def collect_ring(self, distance):
        core, depth, half = self.core, self.depth, self.chips // 2
        start, columns = self.last
        everything = pl.ds(start, columns)
        for chip in self.chips_at(distance):
            for step in range(1, self.frames):
                for way in (1, -1):
                    reach = way * (self.frames - step)
                    held, valid = self.group(reach)
                    landed = self.landings.pop(0)
                    made = self.copy(
                        self.total.at[chip, held, :, everything],
                        landed,
                        (self.chip * 2 + core, self.group(way)[0]),
                        valid,
                    )
                    self.at(self.time.scatter_ring(distance, step - 1), gated(valid, made.start))
                    before = self.group(-way)[1]
                    goes, there = self.group(reach - way)
                    comes = before if there is None else jnp.logical_and(before, there)
                    where = (chip, goes, slice(None), everything)
                    self.at(
                        self.time.scatter_ring(distance, step),
                        gated(comes, functools.partial(self.settle, made, where, landed)),
                    )
        if distance == 0:
            return
        whole = max(
            self.time.scatter_ring(distance, self.frames - 1),
            self.time.scatter_last(distance) if distance < half else 0,
        )
        for side, way in enumerate((1, -1)):
            part = everything
            if distance == half:
                part = pl.ds(start + side * columns // 2, columns // 2)
            goal = self.chip_at(way * distance)
            landed = self.landings.pop(0)
            made = self.copy(
                self.total.at[goal, depth, :, part],
                landed,
                (self.chip_at(way) * 2 + core, depth),
                None,
            )
            self.at(whole + 0.01, made.start)
            where = (self.chip_at(way * (distance - 1)), depth, slice(None), part)
            self.at(
                self.time.scatter_last(distance - 1),
                functools.partial(self.settle, made, where, landed),
            )

    def finish(self):
        self.out[...] = self.total[self.chip, self.depth].astype(self.out.dtype)


def landing_shapes(sizes, rows, columns, split):
    chips, frames = sizes
    (_, first), (_, last) = shares(columns, split)
    half = chips // 2
    shapes = [
        (frames, 2, rows, first // 2),
        (frames, max(2 * (half - 1), 1), rows, first),
        (2, frames, rows, first),
    ]
    if last:
        for distance in reversed(range(half + 1)):
            many = 1 if distance in (0, half) else 2
            shapes += [(rows, last)] * (many * 2 * (frames - 1))
            if distance:
                shapes += [(rows, last // 2 if distance == half else last)] * 2
    return shapes


class Traffic:
    def __init__(
        self, sizes, identity, shards=(), grads=(), swapped=(), swap_at=0, split=8, pace=1.0
    ):
        self.sizes, self.identity = sizes, identity
        self.shards, self.grads, self.swapped = list(shards), list(grads), list(swapped)
        self.swap_at, self.split, self.pace = swap_at, split, pace
        self.active = bool(self.shards or self.grads or self.swapped)

    def operands(self):
        return self.shards + self.grads + self.swapped

    def in_specs(self):
        return [pl.BlockSpec(memory_space=pl.ANY)] * len(self.operands())

    def out_shapes(self):
        chips, frames = self.sizes
        return (
            [jax.ShapeDtypeStruct((chips, 2, frames) + s.shape, s.dtype) for s in self.shards]
            + [jax.ShapeDtypeStruct(g.shape[3:], jnp.float32) for g in self.grads]
            + [jax.ShapeDtypeStruct(s.shape, s.dtype) for s in self.swapped]
        )

    def out_specs(self):
        anywhere = pl.BlockSpec(memory_space=pl.ANY)
        return (
            [anywhere] * len(self.shards)
            + [pl.BlockSpec(memory_space=pltpu.VMEM)] * len(self.grads)
            + [anywhere] * len(self.swapped)
        )

    def scratch(self):
        if not self.active:
            return []
        chips, frames = self.sizes
        shapes = []
        for grad in self.grads:
            shard = grad.shape[3:]
            shapes += [
                pltpu.VMEM((chips, frames) + shard, grad.dtype),
                pltpu.VMEM((frames, chips) + shard, grad.dtype),
            ]
            shapes += [pltpu.VMEM(shape, grad.dtype) for shape in landing_shapes(self.sizes, *shard, self.split)]
        copies = (2 * frames - 1) * (3 + chips) + chips * (2 * frames - 1)
        arrays = max(len(self.shards) + len(self.grads), 1)
        swaps = max(len(self.swapped), 1)
        return shapes + [
            pltpu.SemaphoreType.DMA((arrays, copies)),
            pltpu.SemaphoreType.DMA((arrays, copies)),
            pltpu.SemaphoreType.DMA((arrays, 2 * frames - 1)),
            pltpu.SemaphoreType.DMA((swaps * (frames // 2),)),
            pltpu.SemaphoreType.DMA((swaps * (frames // 2),)),
            pltpu.SemaphoreType.DMA((swaps,)),
        ]

    def plan(self, ins, outs, scratch):
        if not self.active:
            return []
        chips, frames = self.sizes
        scratch = list(scratch)
        send_sems, recv_sems, local_sems, swap_send, swap_recv, swap_local = scratch[-6:]
        spots = places(chips, frames)
        gathers, scatters = len(self.shards), len(self.grads)
        parts = []
        for at in range(gathers + scatters):
            sems = (send_sems.at[at], recv_sems.at[at], local_sems.at[at])
            if at < gathers:
                parts.append(Gather(spots, self.sizes, ins[at], outs[at], self.split, *sems))
                continue
            total, stage = scratch.pop(0), scratch.pop(0)
            many = len(landing_shapes(self.sizes, *outs[at].shape, self.split))
            landings = [scratch.pop(0) for _ in range(many)]
            parts.append(
                Scatter(
                    spots, self.sizes, ins[at], outs[at], total, stage, landings, self.split, *sems
                )
            )
        events = [event for part in parts for event in part.events]
        last = max([time for time, _ in events], default=1.0)
        ends = sum([part.ends for part in parts], [])
        if self.swapped:
            starts, waits = swap_frames(
                chips,
                frames,
                ins[gathers + scatters :],
                outs[gathers + scatters :],
                swap_send,
                swap_recv,
                swap_local,
            )
            events += [(self.swap_at, action) for action in starts]
            ends += waits
        events.append((-1, functools.partial(greet, chips, frames, bool(self.swapped))))
        events = sorted(events, key=lambda event: event[0])
        return [(max(time / last, 0.0) * 0.97, action) for time, action in events] + [
            (1.0, action) for action in ends
        ]


def run_plan(traffic, ins, outs, scratch, step, steps, late=False):
    if not traffic.active:
        return
    whens = [when for when, _ in traffic.plan(ins, outs, scratch)]
    due = [min(int(when * traffic.pace * steps), steps) for when in whens]

    def run(place):
        for at, (_, action) in zip(due, traffic.plan(ins, outs, scratch)):
            if at == place:
                action()

    if late:
        pl.when(step == steps - 1)(functools.partial(run, steps))
        return
    for place in sorted(set(due) - {steps}):
        pl.when(step == place)(functools.partial(run, place))


def traffic_kernel(traffic, *refs):
    count = len(traffic.operands())
    for _, action in traffic.plan(refs[:count], refs[count : 2 * count], refs[2 * count :]):
        action()


def move(traffic):
    return pl.pallas_call(
        functools.partial(traffic_kernel, traffic),
        out_shape=traffic.out_shapes(),
        in_specs=traffic.in_specs(),
        out_specs=traffic.out_specs(),
        scratch_shapes=traffic.scratch(),
        compiler_params=traffic_params(traffic),
    )(*traffic.operands())


def traffic_params(traffic):
    if not traffic.active:
        return pltpu.CompilerParams(vmem_limit_bytes=VMEM_BYTES)
    return pltpu.CompilerParams(
        collective_id=traffic.identity, has_side_effects=True, vmem_limit_bytes=VMEM_BYTES
    )


def layer_norm(values, norm_gain, norm_shift):
    centred = values - jnp.mean(values, axis=-1, keepdims=True)
    spread = jnp.mean(centred * centred, axis=-1, keepdims=True)
    return centred * lax.rsqrt(spread + EPS) * norm_gain + norm_shift


def bucket_of(relative):
    magnitude = jnp.abs(relative)
    above = jnp.zeros_like(relative)
    for threshold in LIMITS:
        above = above + (magnitude >= threshold).astype(jnp.int32)
    inner_bucket = jnp.where(magnitude < 8, magnitude, 7 + above)
    return inner_bucket + NB // 2 * (relative > 0).astype(jnp.int32)


def product(operand_a, operand_b):
    return jnp.dot(operand_a, operand_b, preferred_element_type=jnp.float32)


def weight_grad(operand_a, operand_b):
    return lax.dot_general(
        operand_a, operand_b, (((0,), (0,)), ((), ())), preferred_element_type=jnp.float32
    ).astype(jnp.bfloat16)


def back_product(operand_a, operand_b):
    return lax.dot_general(
        operand_a, operand_b, (((1,), (1,)), ((), ())), preferred_element_type=jnp.float32
    )


def gated_unit(paired):
    return paired[:, :C] * jax.nn.sigmoid(paired[:, C:])


def depth_post(depth_values, norm_gain, norm_shift):
    return jax.nn.silu(layer_norm(depth_values, norm_gain, norm_shift))


def norm_back(hidden, norm_gain, norm_shift, upstream):
    normed_unused, pull_back = jax.vjp(layer_norm, hidden, norm_gain, norm_shift)
    return pull_back(upstream)


TILE = 512
CHUNK = 64


def dot_nt(left, right):
    return lax.dot_general(left, right, (((1,), (1,)), ((), ())), preferred_element_type=jnp.float32)


def dot_nn(left, right):
    return lax.dot_general(left, right, (((1,), (0,)), ((), ())), preferred_element_type=jnp.float32)


def sigmoid(values):
    return 0.5 * jnp.tanh(0.5 * values) + 0.5


def norm_parts(values):
    centred = values - jnp.mean(values, axis=-1, keepdims=True)
    rstd = lax.rsqrt(jnp.mean(centred * centred, axis=-1, keepdims=True) + EPS)
    return centred * rstd, rstd


def norm_chunk(values, norms_ref, which):
    scaled, _ = norm_parts(values)
    return scaled * norms_ref[2 * which : 2 * which + 1, :] + norms_ref[2 * which + 1 : 2 * which + 2, :]


def chunks(rows):
    def each(body):
        @pl.loop(0, rows // CHUNK)
        def _(at):
            body(pl.ds(pl.multiple_of(at * CHUNK, CHUNK), CHUNK))

    return each


def ffn_kernel(traffic, hidden_ref, norms_ref, w_in_ref, w_out_ref, *refs):
    moved = len(traffic.operands())
    ins, refs = refs[:moved], refs[moved:]
    out_ref, inner_ref, normed_ref, next_ref = refs[:4]
    outs, refs = refs[4 : 4 + moved], refs[4 + moved :]
    total, refs = refs[0], refs[1:]
    step, steps = pl.program_id(0), pl.num_programs(0)
    run_plan(traffic, ins, outs, refs, step, FFN_STEPS)
    each = chunks(hidden_ref.shape[0])

    @pl.when(step == 0)
    def _():
        def body(here):
            normed_ref[here, :] = norm_chunk(hidden_ref[here, :], norms_ref, 0).astype(jnp.bfloat16)
            total[here, :] = jnp.zeros((CHUNK, total.shape[1]), jnp.float32)

        each(body)

    inner = dot_nn(normed_ref[...], w_in_ref[...])
    inner_ref[...] = inner.astype(jnp.bfloat16)
    total[...] += dot_nn((inner * sigmoid(inner)).astype(jnp.bfloat16), w_out_ref[...])

    @pl.when(step == steps - 1)
    def _():
        def body(here):
            hidden = hidden_ref[here, :] + 0.5 * total[here, :]
            out_ref[here, :] = hidden
            next_ref[here, :] = norm_chunk(hidden, norms_ref, 1).astype(jnp.bfloat16)

        each(body)

    run_plan(traffic, ins, outs, refs, step, FFN_STEPS, late=True)


FFN_STEPS = 8


def resident(shape):
    return pl.BlockSpec(shape, lambda step: (0,) * len(shape))


def ffn(hidden, norms, weight_in, weight_out, traffic):
    rows, width = hidden.shape
    tile = weight_in.shape[1] // FFN_STEPS
    return pl.pallas_call(
        functools.partial(ffn_kernel, traffic),
        grid=(FFN_STEPS,),
        out_shape=[
            jax.ShapeDtypeStruct((rows, width), jnp.float32),
            jax.ShapeDtypeStruct((rows, weight_in.shape[1]), jnp.bfloat16),
            jax.ShapeDtypeStruct((rows, width), jnp.bfloat16),
            jax.ShapeDtypeStruct((rows, width), jnp.bfloat16),
        ]
        + traffic.out_shapes(),
        in_specs=[
            resident((rows, width)),
            resident(norms.shape),
            pl.BlockSpec((width, tile), lambda step: (0, step)),
            pl.BlockSpec((tile, width), lambda step: (step, 0)),
        ]
        + traffic.in_specs(),
        out_specs=[
            resident((rows, width)),
            pl.BlockSpec((rows, tile), lambda step: (0, step)),
            resident((rows, width)),
            resident((rows, width)),
        ]
        + traffic.out_specs(),
        scratch_shapes=[pltpu.VMEM((rows, width), jnp.float32)] + traffic.scratch(),
        compiler_params=traffic_params(traffic),
    )(hidden, norms, weight_in, weight_out, *traffic.operands())


def ffn_back_kernel(
    traffic, hidden_ref, normed_ref, grad_ref, norms_ref, inner_ref, w_in_ref, w_out_ref, *refs
):
    moved = len(traffic.operands())
    ins, refs = refs[:moved], refs[moved:]
    out_ref, g_in_ref, g_out_ref, sums_ref = refs[:4]
    outs, refs = refs[4 : 4 + moved], refs[4 + moved :]
    (half_grad, turned, total), refs = refs[:3], refs[3:]
    step, steps = pl.program_id(0), pl.num_programs(0)
    run_plan(traffic, ins, outs, refs, step, FFN_STEPS)
    each = chunks(hidden_ref.shape[0])

    @pl.when(step == 0)
    def _():
        def body(here):
            half_grad[here, :] = (0.5 * grad_ref[here, :]).astype(jnp.bfloat16)
            total[here, :] = jnp.zeros((CHUNK, total.shape[1]), jnp.float32)

        each(body)
        turned[...] = normed_ref[...].T
        sums_ref[...] = jnp.zeros_like(sums_ref)

    inner = inner_ref[...].astype(jnp.float32)
    gate = sigmoid(inner)
    active = (inner * gate).astype(jnp.bfloat16)
    g_out_ref[...] = dot_nn(active.T, half_grad[...]).astype(jnp.bfloat16)
    slope = gate * (1.0 + inner * (1.0 - gate))
    grad_inner = (dot_nt(half_grad[...], w_out_ref[...]) * slope).astype(jnp.bfloat16)
    g_in_ref[...] = dot_nn(turned[...], grad_inner).astype(jnp.bfloat16)
    total[...] += dot_nt(grad_inner, w_in_ref[...])

    @pl.when(step == steps - 1)
    def _():
        def body(here):
            scaled, rstd = norm_parts(hidden_ref[here, :])
            upstream = total[here, :]
            sums_ref[0:1, :] += jnp.sum(upstream * scaled, axis=0, keepdims=True)
            sums_ref[1:2, :] += jnp.sum(upstream, axis=0, keepdims=True)
            weighted = upstream * norms_ref[0:1, :]
            back = weighted - jnp.mean(weighted, axis=-1, keepdims=True)
            back = back - scaled * jnp.mean(weighted * scaled, axis=-1, keepdims=True)
            out_ref[here, :] = grad_ref[here, :] + rstd * back

        each(body)

    run_plan(traffic, ins, outs, refs, step, FFN_STEPS, late=True)


def ffn_back(hidden, normed, grad, norms, inner, weight_in, weight_out, traffic):
    rows, width = hidden.shape
    tile = weight_in.shape[1] // FFN_STEPS
    return pl.pallas_call(
        functools.partial(ffn_back_kernel, traffic),
        grid=(FFN_STEPS,),
        out_shape=[
            jax.ShapeDtypeStruct((rows, width), jnp.float32),
            jax.ShapeDtypeStruct(weight_in.shape, jnp.bfloat16),
            jax.ShapeDtypeStruct(weight_out.shape, jnp.bfloat16),
            jax.ShapeDtypeStruct((8, width), jnp.float32),
        ]
        + traffic.out_shapes(),
        in_specs=[
            resident((rows, width)),
            resident((rows, width)),
            resident((rows, width)),
            resident(norms.shape),
            pl.BlockSpec((rows, tile), lambda step: (0, step)),
            pl.BlockSpec((width, tile), lambda step: (0, step)),
            pl.BlockSpec((tile, width), lambda step: (step, 0)),
        ]
        + traffic.in_specs(),
        out_specs=[
            resident((rows, width)),
            pl.BlockSpec((width, tile), lambda step: (0, step)),
            pl.BlockSpec((tile, width), lambda step: (step, 0)),
            resident((8, width)),
        ]
        + traffic.out_specs(),
        scratch_shapes=[
            pltpu.VMEM((rows, width), jnp.bfloat16),
            pltpu.VMEM((width, rows), jnp.bfloat16),
            pltpu.VMEM((rows, width), jnp.float32),
        ]
        + traffic.scratch(),
        compiler_params=traffic_params(traffic),
    )(hidden, normed, grad, norms, inner, weight_in, weight_out, *traffic.operands())


QB = 128
PAIRS = H // 2
BAND = 3 * QB


def stacked(block):
    lanes = lax.broadcasted_iota(jnp.int32, block.shape, 1)
    nothing = jnp.zeros_like(block)
    return jnp.concatenate(
        [jnp.where(lanes < DH, block, nothing), jnp.where(lanes >= DH, block, nothing)], axis=0
    )


def own_halves(both):
    channels = lax.broadcasted_iota(jnp.int32, (2 * DH, QB), 0)
    return jnp.where(channels < DH, both[:, :QB], both[:, QB:]).T


def offset_rows(table):
    offsets = (jnp.arange(4, dtype=jnp.int32)[:, None] - 1) * QB - jnp.arange(QB, dtype=jnp.int32)
    onehot = (jnp.arange(NB)[:, None, None] == bucket_of(offsets)[None]).astype(jnp.float32)
    rows = jnp.dot(table, onehot.reshape(NB, 4 * QB), precision=lax.Precision.HIGHEST)
    return rows.reshape(PAIRS, 8, QB)


def fill_strip(strip, rows_ref, length):
    far = length - 2 * QB
    rows_of = lax.broadcasted_iota(jnp.int32, (QB, QB), 0)
    lanes_of = lax.broadcasted_iota(jnp.int32, (QB, QB), 1)
    for head in range(2):
        columns = slice(head * QB, (head + 1) * QB)
        turned = []
        for at in range(4):
            row = jnp.broadcast_to(rows_ref[0, head * 4 + at : head * 4 + at + 1, :], (QB, QB))
            turned.append(pltpu.roll(row, 0, 1, stride=1, stride_axis=0))
        for tile in range(3):
            strip[far + tile * QB : far + (tile + 1) * QB, columns] = jnp.where(
                lanes_of >= rows_of, turned[tile], turned[tile + 1]
            )

        @pl.loop(0, far // QB)
        def _(at):
            before, after = pl.multiple_of(at * QB, QB), pl.multiple_of(far + BAND + at * QB, QB)
            strip[pl.ds(before, QB), columns] = turned[0]
            strip[pl.ds(after, QB), columns] = turned[3]


def strip_start(rows, length):
    first = lax.rem(lax.axis_index("batch"), 2) * rows + pl.program_id(1) * QB
    return pl.multiple_of(length - QB - first, QB), first


def in_order(whole, own_ref, far_ref):
    rows = own_ref.shape[0]
    core = lax.rem(lax.axis_index("batch"), 2)
    whole[pl.ds(pl.multiple_of(core * rows, QB), rows), :] = own_ref[...]
    whole[pl.ds(pl.multiple_of((1 - core) * rows, QB), rows), :] = far_ref[...]


def attend_kernel(
    rows, length, traffic, rows_ref, q_ref, k_own_ref, v_own_ref, k_far_ref, v_far_ref, *refs
):
    moved = len(traffic.operands())
    ins, refs = refs[:moved], refs[moved:]
    (out_ref, log_ref), refs = refs[:2], refs[2:]
    outs, refs = refs[:moved], refs[moved:]
    (strip, score, prob, vt, k_all, v_all), refs = refs[:6], refs[6:]
    blocks = rows // QB
    step = pl.program_id(0) * blocks + pl.program_id(1)
    run_plan(traffic, ins, outs, refs, step, PAIRS * blocks)

    @pl.when(pl.program_id(1) == 0)
    def _():
        fill_strip(strip, rows_ref, length)
        in_order(k_all, k_own_ref, k_far_ref)
        in_order(v_all, v_own_ref, v_far_ref)
        vt[...] = v_all[...].T

    start, _ = strip_start(rows, length)
    score[...] = dot_nt(k_all[...], stacked(q_ref[...] * 0.125))

    def highest(at, most):
        here = pl.ds(pl.multiple_of(at * QB, QB), QB)
        values = score[here, :] + strip[pl.ds(pl.multiple_of(start + at * QB, QB), QB), :]
        score[here, :] = values
        return jnp.maximum(most, jnp.max(values.reshape(QB // 8, 8, 2 * QB), axis=0))

    most = lax.fori_loop(
        0, length // QB, highest, jnp.full((8, 2 * QB), -jnp.inf, jnp.float32), unroll=True
    )
    most = jnp.max(most, axis=0, keepdims=True)

    def weigh(at, total):
        here = pl.ds(pl.multiple_of(at * QB, QB), QB)
        values = jnp.exp(score[here, :] - most)
        prob[here, :] = values.astype(jnp.bfloat16)
        return total + jnp.sum(values.reshape(QB // 8, 8, 2 * QB), axis=0)

    total = lax.fori_loop(
        0, length // QB, weigh, jnp.zeros((8, 2 * QB), jnp.float32), unroll=True
    )
    total = jnp.sum(total, axis=0, keepdims=True)
    mixed = dot_nn(vt[...], prob[...]) / total
    out_ref[...] = own_halves(mixed).astype(out_ref.dtype)
    log_ref[0] = most + jnp.log(total)
    run_plan(traffic, ins, outs, refs, step, PAIRS * blocks, late=True)


def attend(packed, far, offsets, traffic):
    rows = packed.shape[0]
    length = 2 * rows
    blocks = rows // QB
    return pl.pallas_call(
        functools.partial(attend_kernel, rows, length, traffic),
        grid=(PAIRS, blocks),
        out_shape=[
            jax.ShapeDtypeStruct((rows, D), jnp.bfloat16),
            jax.ShapeDtypeStruct((PAIRS * blocks, 1, 2 * QB), jnp.float32),
        ]
        + traffic.out_shapes(),
        in_specs=[
            pl.BlockSpec((1, 8, QB), lambda p, b: (p, 0, 0)),
            pl.BlockSpec((QB, 2 * DH), lambda p, b: (b, p)),
            pl.BlockSpec((rows, 2 * DH), lambda p, b: (0, PAIRS + p)),
            pl.BlockSpec((rows, 2 * DH), lambda p, b: (0, 2 * PAIRS + p)),
            pl.BlockSpec((rows, 2 * DH), lambda p, b: (0, p)),
            pl.BlockSpec((rows, 2 * DH), lambda p, b: (0, PAIRS + p)),
        ]
        + traffic.in_specs(),
        out_specs=[
            pl.BlockSpec((QB, 2 * DH), lambda p, b: (b, p)),
            pl.BlockSpec((1, 1, 2 * QB), lambda p, b: (p * blocks + b, 0, 0)),
        ]
        + traffic.out_specs(),
        scratch_shapes=[
            pltpu.VMEM((2 * length - QB, 2 * QB), jnp.float32),
            pltpu.VMEM((length, 2 * QB), jnp.float32),
            pltpu.VMEM((length, 2 * QB), jnp.bfloat16),
            pltpu.VMEM((2 * DH, length), jnp.bfloat16),
            pltpu.VMEM((length, 2 * DH), jnp.bfloat16),
            pltpu.VMEM((length, 2 * DH), jnp.bfloat16),
        ]
        + traffic.scratch(),
        compiler_params=traffic_params(traffic),
    )(offsets, packed, packed, packed, far, far, *traffic.operands())


def attend_back_kernel(
    rows,
    length,
    traffic,
    rows_ref,
    q_ref,
    k_own_ref,
    v_own_ref,
    k_far_ref,
    v_far_ref,
    g_ref,
    log_ref,
    *refs,
):
    moved = len(traffic.operands())
    ins, refs = refs[:moved], refs[moved:]
    (dq_ref, dk_own_ref, dv_own_ref, dk_far_ref, dv_far_ref), refs = refs[:5], refs[5:]
    (near_ref, sums_ref), refs = refs[:2], refs[2:]
    outs, refs = refs[:moved], refs[moved:]
    (strip, score, slope, prob, change, kt, dk_sum, dv_sum, near), refs = refs[:9], refs[9:]
    (k_all, v_all), refs = refs[:2], refs[2:]
    block, blocks = pl.program_id(1), rows // QB
    step = pl.program_id(0) * blocks + block
    run_plan(traffic, ins, outs, refs, step, PAIRS * blocks)

    @pl.when(block == 0)
    def _():
        fill_strip(strip, rows_ref, length)
        in_order(k_all, k_own_ref, k_far_ref)
        in_order(v_all, v_own_ref, v_far_ref)
        kt[...] = k_all[...].T
        dk_sum[...] = jnp.zeros_like(dk_sum)
        dv_sum[...] = jnp.zeros_like(dv_sum)
        near[...] = jnp.zeros_like(near)
        change[0:QB, :] = jnp.zeros((QB, 2 * QB), jnp.bfloat16)
        change[length + QB : length + 2 * QB, :] = jnp.zeros((QB, 2 * QB), jnp.bfloat16)

    start, first = strip_start(rows, length)
    q_both = stacked(q_ref[...] * 0.125)
    g_both = stacked(g_ref[...])
    score[...] = dot_nt(k_all[...], q_both)
    slope[...] = dot_nt(v_all[...], g_both)
    log_total = log_ref[0]

    def weigh(at, total):
        here = pl.ds(pl.multiple_of(at * QB, QB), QB)
        values = jnp.exp(
            score[here, :] + strip[pl.ds(pl.multiple_of(start + at * QB, QB), QB), :] - log_total
        )
        score[here, :] = values
        prob[here, :] = values.astype(jnp.bfloat16)
        return total + jnp.sum((values * slope[here, :]).reshape(QB // 8, 8, 2 * QB), axis=0)

    centre = lax.fori_loop(
        0, length // QB, weigh, jnp.zeros((8, 2 * QB), jnp.float32), unroll=True
    )
    centre = jnp.sum(centre, axis=0, keepdims=True)

    for at in range(length // QB):
        here = pl.ds(at * QB, QB)
        values = score[here, :] * (slope[here, :] - centre)
        change[pl.ds(at * QB + QB, QB), :] = values.astype(jnp.bfloat16)
        sums_ref[0, at : at + 1, :] = jnp.sum(values, axis=0, keepdims=True)

    dv_sum[...] += dot_nn(prob[...], g_both)
    moved = change[QB : QB + length, :]
    dk_sum[...] += dot_nn(moved, q_both)
    dq_ref[...] = (own_halves(dot_nn(kt[...], moved)) * 0.125).astype(dq_ref.dtype)
    near[...] += change[pl.ds(pl.multiple_of(first, QB), BAND), :].astype(jnp.float32)

    @pl.when(block == pl.num_programs(1) - 1)
    def _():
        core = lax.rem(lax.axis_index("batch"), 2)
        own = pl.ds(pl.multiple_of(core * rows, QB), rows)
        far = pl.ds(pl.multiple_of((1 - core) * rows, QB), rows)
        dk_own_ref[...] = dk_sum[own, :].astype(jnp.bfloat16)
        dv_own_ref[...] = dv_sum[own, :].astype(jnp.bfloat16)
        dk_far_ref[...] = dk_sum[far, :].astype(jnp.bfloat16)
        dv_far_ref[...] = dv_sum[far, :].astype(jnp.bfloat16)
        rows_of = lax.broadcasted_iota(jnp.int32, (QB, QB), 0)
        lanes_of = lax.broadcasted_iota(jnp.int32, (QB, QB), 1)
        for head in range(2):
            for tile in range(3):
                turned = near[tile * QB : (tile + 1) * QB, head * QB : (head + 1) * QB]
                step = 1
                while step < QB:
                    turned = jnp.where(
                        lax.rem(rows_of // step, 2) == 1, pltpu.roll(turned, QB - step, 1), turned
                    )
                    step *= 2
                upper = jnp.where((lanes_of >= 1) & (lanes_of + rows_of < QB), turned, 0.0)
                for half, piece in enumerate((upper, turned - upper)):
                    at = head * 6 + tile * 2 + half
                    near_ref[0, at : at + 1, :] = jnp.sum(piece, axis=0, keepdims=True)

    run_plan(traffic, ins, outs, refs, step, PAIRS * blocks, late=True)


def attend_back(packed, far, offsets, log_total, grads, traffic):
    rows = packed.shape[0]
    length = 2 * rows
    blocks = rows // QB
    big = (length, 2 * QB)
    return pl.pallas_call(
        functools.partial(attend_back_kernel, rows, length, traffic),
        grid=(PAIRS, blocks),
        out_shape=[
            jax.ShapeDtypeStruct((rows, D), jnp.bfloat16),
            jax.ShapeDtypeStruct((rows, D), jnp.bfloat16),
            jax.ShapeDtypeStruct((rows, D), jnp.bfloat16),
            jax.ShapeDtypeStruct((rows, D), jnp.bfloat16),
            jax.ShapeDtypeStruct((rows, D), jnp.bfloat16),
            jax.ShapeDtypeStruct((PAIRS, 12, QB), jnp.float32),
            jax.ShapeDtypeStruct((PAIRS * blocks, length // QB, 2 * QB), jnp.float32),
        ]
        + traffic.out_shapes(),
        in_specs=[
            pl.BlockSpec((1, 8, QB), lambda p, b: (p, 0, 0)),
            pl.BlockSpec((QB, 2 * DH), lambda p, b: (b, p)),
            pl.BlockSpec((rows, 2 * DH), lambda p, b: (0, PAIRS + p)),
            pl.BlockSpec((rows, 2 * DH), lambda p, b: (0, 2 * PAIRS + p)),
            pl.BlockSpec((rows, 2 * DH), lambda p, b: (0, p)),
            pl.BlockSpec((rows, 2 * DH), lambda p, b: (0, PAIRS + p)),
            pl.BlockSpec((QB, 2 * DH), lambda p, b: (b, p)),
            pl.BlockSpec((1, 1, 2 * QB), lambda p, b: (p * blocks + b, 0, 0)),
        ]
        + traffic.in_specs(),
        out_specs=[
            pl.BlockSpec((QB, 2 * DH), lambda p, b: (b, p)),
            pl.BlockSpec((rows, 2 * DH), lambda p, b: (0, p)),
            pl.BlockSpec((rows, 2 * DH), lambda p, b: (0, p)),
            pl.BlockSpec((rows, 2 * DH), lambda p, b: (0, p)),
            pl.BlockSpec((rows, 2 * DH), lambda p, b: (0, p)),
            pl.BlockSpec((1, 12, QB), lambda p, b: (p, 0, 0)),
            pl.BlockSpec((1, length // QB, 2 * QB), lambda p, b: (p * blocks + b, 0, 0)),
        ]
        + traffic.out_specs(),
        scratch_shapes=[
            pltpu.VMEM((2 * length - QB, 2 * QB), jnp.float32),
            pltpu.VMEM(big, jnp.float32),
            pltpu.VMEM(big, jnp.float32),
            pltpu.VMEM(big, jnp.bfloat16),
            pltpu.VMEM((length + 2 * QB, 2 * QB), jnp.bfloat16),
            pltpu.VMEM((2 * DH, length), jnp.bfloat16),
            pltpu.VMEM((length, 2 * DH), jnp.float32),
            pltpu.VMEM((length, 2 * DH), jnp.float32),
            pltpu.VMEM((BAND, 2 * QB), jnp.float32),
            pltpu.VMEM((length, 2 * DH), jnp.bfloat16),
            pltpu.VMEM((length, 2 * DH), jnp.bfloat16),
        ]
        + traffic.scratch(),
        compiler_params=traffic_params(traffic),
    )(offsets, packed, packed, packed, far, far, grads, log_total, *traffic.operands())


def table_back(near, sums, first_block):
    blocks = sums.shape[0] // PAIRS
    count = sums.shape[1]
    lane = jnp.arange(QB, dtype=jnp.int32)[None, None, :]
    tile = jnp.arange(3, dtype=jnp.int32)[:, None, None]
    half = jnp.arange(2, dtype=jnp.int32)[None, :, None]
    behind = jnp.where(half == 0, jnp.where(lane == 0, QB, lane), jnp.where(lane == 0, 0, lane - QB))
    offsets = (tile - 1) * QB - behind
    onehot = (bucket_of(offsets)[..., None] == jnp.arange(NB)).astype(jnp.float32)
    close = jnp.einsum(
        "zthl,thlb->zb",
        near.reshape(H, 3, 2, QB),
        onehot,
        precision=lax.Precision.HIGHEST,
    )
    by_block = sums.reshape(PAIRS, blocks, count, 2, QB).sum(axis=4)
    here = first_block + jnp.arange(blocks, dtype=jnp.int32)[:, None]
    there = jnp.arange(count, dtype=jnp.int32)[None, :]
    below = jnp.einsum(
        "pbch,bc->ph", by_block, (there < here - 1).astype(jnp.float32), precision=lax.Precision.HIGHEST
    ).reshape(H)
    above = jnp.einsum(
        "pbch,bc->ph", by_block, (there > here + 1).astype(jnp.float32), precision=lax.Precision.HIGHEST
    ).reshape(H)
    spread = jnp.arange(NB)[None, :]
    close = close + jnp.where(spread == NB // 2 - 1, below[:, None], 0.0)
    return close + jnp.where(spread == NB - 1, above[:, None], 0.0)


EDGE = 16
LANES = 128
BLOCK = 128


def shifted_rows(window):
    for low in range(8):
        turned = pltpu.roll(window, window.shape[0] - low, 0) if low else window
        for high in range(4):
            offset = 8 * high + low
            if 1 <= offset <= KERNEL:
                yield offset, turned[8 * high : 8 * high + BLOCK, :]


def conv_kernel(traffic, padded_ref, taps_ref, norms_ref, *refs):
    moved = len(traffic.operands())
    ins, refs = refs[:moved], refs[moved:]
    (depth_ref, post_ref, mean_ref, rstd_ref), refs = refs[:4], refs[4:]
    outs, refs = refs[:moved], refs[moved:]
    step = pl.program_id(0)
    run_plan(traffic, ins, outs, refs, step, CONV_BLOCKS)
    first = pl.multiple_of(step * BLOCK, BLOCK)

    @pl.loop(0, C // LANES)
    def _(at):
        lanes = pl.ds(pl.multiple_of(at * LANES, LANES), LANES)
        window = padded_ref[pl.ds(first, BLOCK + 2 * EDGE), lanes].astype(jnp.float32)
        total = jnp.zeros((BLOCK, LANES), jnp.float32)
        for offset, rows in shifted_rows(window):
            total = total + rows * taps_ref[offset - 1 : offset, lanes]
        depth_ref[:, lanes] = total

    @pl.loop(0, BLOCK // 16)
    def _(at):
        here = pl.ds(pl.multiple_of(at * 16, 16), 16)
        scaled, rstd = norm_parts(depth_ref[here, :])
        mean_ref[here, :] = jnp.mean(depth_ref[here, :], axis=-1, keepdims=True)
        rstd_ref[here, :] = rstd
        normed = scaled * norms_ref[0:1, :] + norms_ref[1:2, :]
        post_ref[here, :] = (normed * sigmoid(normed)).astype(jnp.bfloat16)

    run_plan(traffic, ins, outs, refs, step, CONV_BLOCKS, late=True)


CONV_BLOCKS = 5


def convolve(padded, taps, norms, traffic):
    rows = padded.shape[0] - 2 * EDGE
    return pl.pallas_call(
        functools.partial(conv_kernel, traffic),
        grid=(CONV_BLOCKS,),
        out_shape=[
            jax.ShapeDtypeStruct((rows, C), jnp.float32),
            jax.ShapeDtypeStruct((rows, C), jnp.bfloat16),
            jax.ShapeDtypeStruct((rows, 1), jnp.float32),
            jax.ShapeDtypeStruct((rows, 1), jnp.float32),
        ]
        + traffic.out_shapes(),
        in_specs=[resident(padded.shape), resident(taps.shape), resident(norms.shape)]
        + traffic.in_specs(),
        out_specs=[
            pl.BlockSpec((BLOCK, C), lambda step: (step, 0)),
            pl.BlockSpec((BLOCK, C), lambda step: (step, 0)),
            pl.BlockSpec((BLOCK, 1), lambda step: (step, 0)),
            pl.BlockSpec((BLOCK, 1), lambda step: (step, 0)),
        ]
        + traffic.out_specs(),
        scratch_shapes=traffic.scratch(),
        compiler_params=traffic_params(traffic),
    )(padded, taps, norms, *traffic.operands())


def conv_back_kernel(traffic, change_ref, gated_ref, first_ref, second_ref, taps_ref, *refs):
    moved = len(traffic.operands())
    ins, refs = refs[:moved], refs[moved:]
    (g_first_ref, g_second_ref, g_taps_ref), refs = refs[:3], refs[3:]
    outs, refs = refs[:moved], refs[moved:]
    sums, refs = refs[0], refs[1:]
    step = pl.program_id(0)
    run_plan(traffic, ins, outs, refs, step, C // LANES)
    sums[...] = jnp.zeros_like(sums)

    @pl.loop(0, CONV_BLOCKS)
    def _(block):
        first = pl.multiple_of(block * BLOCK, BLOCK)
        here = pl.ds(first, BLOCK)
        around = pl.ds(first, BLOCK + 2 * EDGE)
        window = change_ref[around, :].astype(jnp.float32)
        total = jnp.zeros((BLOCK, LANES), jnp.float32)
        for offset, rows in shifted_rows(window):
            total = total + rows * taps_ref[KERNEL - offset : KERNEL - offset + 1, :]
        gate = sigmoid(second_ref[here, :].astype(jnp.float32))
        through = total * gate
        g_first_ref[here, :] = through.astype(jnp.bfloat16)
        g_second_ref[here, :] = (
            through * first_ref[here, :].astype(jnp.float32) * (1.0 - gate)
        ).astype(jnp.bfloat16)

        change = change_ref[pl.ds(pl.multiple_of(first + EDGE, EDGE), BLOCK), :].astype(jnp.float32)
        window = gated_ref[around, :].astype(jnp.float32)
        for offset, rows in shifted_rows(window):
            part = jnp.sum((rows * change).reshape(BLOCK // 8, 8, LANES), axis=0)
            sums[8 * (offset - 1) : 8 * offset, :] += part

    for tap in range(KERNEL):
        g_taps_ref[tap : tap + 1, :] = jnp.sum(sums[8 * tap : 8 * tap + 8, :], axis=0, keepdims=True)

    run_plan(traffic, ins, outs, refs, step, C // LANES, late=True)


def convolve_back(change, gated, paired, taps, traffic):
    rows = change.shape[0] - 2 * EDGE
    half = C // LANES
    column = pl.BlockSpec((rows, LANES), lambda step: (0, step))
    edged = pl.BlockSpec((rows + 2 * EDGE, LANES), lambda step: (0, step))
    return pl.pallas_call(
        functools.partial(conv_back_kernel, traffic),
        grid=(half,),
        out_shape=[
            jax.ShapeDtypeStruct((rows, C), jnp.bfloat16),
            jax.ShapeDtypeStruct((rows, C), jnp.bfloat16),
            jax.ShapeDtypeStruct((KERNEL + 1, C), jnp.float32),
        ]
        + traffic.out_shapes(),
        in_specs=[
            edged,
            edged,
            column,
            pl.BlockSpec((rows, LANES), lambda step: (0, half + step)),
            pl.BlockSpec((KERNEL + 1, LANES), lambda step: (0, step)),
        ]
        + traffic.in_specs(),
        out_specs=[column, column, pl.BlockSpec((KERNEL + 1, LANES), lambda step: (0, step))]
        + traffic.out_specs(),
        scratch_shapes=[pltpu.VMEM((8 * KERNEL, LANES), jnp.float32)] + traffic.scratch(),
        compiler_params=traffic_params(traffic),
    )(change, gated, paired, paired, taps, *traffic.operands())


def as_shard(array):
    rows = array.shape[0]
    return array if rows % 16 == 0 else array.reshape(16, rows * array.shape[1] // 16)


def as_weight(whole, like):
    devices = math.prod(whole.shape[:3])
    return whole.reshape(devices * like.shape[0], like.shape[1])


def as_parts(grad, sizes, like):
    chips, frames = sizes
    shard = as_shard(jnp.zeros(like.shape, jnp.bfloat16)).shape
    return grad.reshape((chips, 2, frames) + shard)


def pack_small(values, small_shapes):
    flat = jnp.concatenate([value.reshape(-1) for value in values])
    return jnp.pad(flat, (0, SMALL[0] * SMALL[1] - flat.shape[0])).reshape(SMALL)


def unpack_small(packed, shapes):
    devices = packed.shape[0]
    at, out = 0, []
    for shape in shapes:
        size = math.prod(shape)
        piece = packed[:, at : at + size].reshape((devices,) + shape)
        at += size
        piece = jnp.moveaxis(piece, 0, -2)
        out.append(piece.reshape(shape[:-1] + (devices * shape[-1],)))
    return out


def repack_small(values, shapes, devices):
    pieces = []
    for value, shape in zip(values, shapes):
        piece = value.reshape(shape[:-1] + (devices, shape[-1]))
        pieces.append(jnp.moveaxis(piece, -2, 0).reshape(devices, -1))
    flat = jnp.concatenate(pieces, axis=1)
    return jnp.pad(flat, ((0, 0), (0, SMALL[0] * SMALL[1] - flat.shape[1])))


def shards(
    frames_in,
    positions,
    mask_vector,
    norm_gains,
    norm_biases,
    depth_gain,
    depth_bias,
    early_in,
    early_out,
    qkv_weight,
    mixer_out,
    pointwise_in,
    pointwise_out,
    depth_kernel,
    late_in,
    late_out,
    position_bias,
    cotangent,
):
    groups, run, model_width = frames_in.shape
    line = lax.axis_size("frames")
    chips = lax.axis_size("batch") // 2
    sizes = (chips, line)
    devices = 2 * chips * line
    length = run * line
    rows = groups * run
    batch, depth = lax.axis_index("batch"), lax.axis_index("frames")
    core = lax.rem(batch, 2)
    first_frame = core * rows
    partner = [(at, at + 1 - 2 * (at % 2)) for at in range(2 * chips)]

    def from_other(array):
        return lax.ppermute(array, "batch", partner)

    big = [early_in, early_out, qkv_weight, mixer_out, pointwise_in, pointwise_out, late_in, late_out]
    small = [mask_vector, norm_gains, norm_biases, depth_gain, depth_bias, depth_kernel, position_bias]
    small_shapes = [value.shape for value in small]
    small_size = sum(math.prod(shape) for shape in small_shapes)
    shard_of = [as_shard(value) for value in big]
    gathered = move(
        Traffic(
            sizes,
            0,
            shards=shard_of[:2] + [pack_small(small, small_shapes)],
            swapped=[frames_in],
            swap_at=3.0,
        )
    )
    w_early_in, w_early_out = as_weight(gathered[0], early_in), as_weight(gathered[1], early_out)
    small_whole = gathered[2].reshape(devices, SMALL[0] * SMALL[1])
    mask_full, gains, biases, channel_gain, channel_bias, kernel_full, table = [
        value.astype(jnp.float32) for value in unpack_small(small_whole, small_shapes)
    ]
    table = table.reshape(H, NB)
    frames_here = gathered[3].reshape(rows, D)

    both = jnp.where(core == 0, 0, 1)
    other_positions = from_other(positions)
    owner = depth // groups
    listed = jnp.where(owner == both, positions, other_positions)
    listed = lax.dynamic_index_in_dim(listed, lax.rem(depth, groups), 0, keepdims=False)
    frame_ids = first_frame + jnp.arange(rows, dtype=jnp.int32)
    masked = jnp.any(listed[:, None] == frame_ids[None, :], axis=0).reshape(rows, 1)

    offsets = offset_rows(table)

    def norms_of(*which):
        rows_of = [row for at in which for row in (gains[at], biases[at])]
        return jnp.stack(rows_of + [jnp.zeros((D,), jnp.float32)] * (8 - len(rows_of)))

    def parts(grad, like):
        return as_parts(grad, sizes, like)

    hidden0 = jnp.where(masked, mask_full[None, :], frames_here.astype(jnp.float32))
    hidden1, inner1, normed1, normed2, *gathered = ffn(
        hidden0,
        norms_of(0, 1),
        w_early_in,
        w_early_out,
        Traffic(sizes, 1, shards=shard_of[2:4], swapped=[cotangent], swap_at=3.0, pace=2.0),
    )
    w_qkv, w_mixer = as_weight(gathered[0], qkv_weight), as_weight(gathered[1], mixer_out)
    upstream = gathered[2].reshape(rows, D).astype(jnp.float32)
    packed = product(normed2, w_qkv).astype(jnp.bfloat16)
    far = from_other(packed[:, D:])
    mixed_rows, log_total, *gathered = attend(
        packed, far, offsets, Traffic(sizes, 2, shards=shard_of[4:6], split=6, pace=1.15)
    )
    w_point_in = as_weight(gathered[0], pointwise_in)
    w_point_out = as_weight(gathered[1], pointwise_out)
    hidden2 = hidden1 + product(mixed_rows, w_mixer)

    normed3 = layer_norm(hidden2, gains[2], biases[2]).astype(jnp.bfloat16)
    paired = product(normed3, w_point_in).astype(jnp.bfloat16)
    gated = gated_unit(paired.astype(jnp.float32)).astype(jnp.bfloat16)

    def with_edges(array):
        sent = jnp.where(core == 0, array[rows - EDGE :], array[:EDGE])
        edge = from_other(sent)
        nothing = jnp.zeros_like(edge)
        return jnp.concatenate(
            [jnp.where(core == 0, nothing, edge), array, jnp.where(core == 0, edge, nothing)], axis=0
        )

    padded = with_edges(gated)
    taps = jnp.pad(kernel_full, ((0, 1), (0, 0)))
    channel_norms = jnp.pad(jnp.stack([channel_gain, channel_bias]), ((0, 6), (0, 0)))
    depth_values, post, depth_mean, depth_rstd, *gathered = convolve(
        padded, taps, channel_norms, Traffic(sizes, 3, shards=shard_of[6:], split=6, pace=2.4)
    )
    w_late_in, w_late_out = as_weight(gathered[0], late_in), as_weight(gathered[1], late_out)
    hidden3 = hidden2 + product(post, w_point_out)
    hidden4, inner5, normed5, activations = ffn(
        hidden3, norms_of(3, 4), w_late_in, w_late_out, Traffic(sizes, None)
    )

    grad4, gain_grad4, bias_grad4 = norm_back(hidden4, gains[4], biases[4], upstream)
    grad3, late_in_grad, late_out_grad, norm_sums3 = ffn_back(
        hidden3, normed5, grad4, norms_of(3), inner5, w_late_in, w_late_out, Traffic(sizes, None)
    )
    grad_out3 = grad3.astype(jnp.bfloat16)
    pointwise_out_grad = weight_grad(post, grad_out3)
    grad_post = back_product(grad_out3, w_point_out)
    scaled = (depth_values - depth_mean) * depth_rstd
    shifted = scaled * channel_gain + channel_bias
    gate = jax.nn.sigmoid(shifted)
    grad_shifted = grad_post * gate * (1.0 + shifted * (1.0 - gate))
    channel_gain_grad = jnp.sum(grad_shifted * scaled, axis=0)
    channel_bias_grad = jnp.sum(grad_shifted, axis=0)
    weighted = grad_shifted * channel_gain
    grad_depth = depth_rstd * (
        weighted
        - jnp.mean(weighted, axis=-1, keepdims=True)
        - scaled * jnp.mean(weighted * scaled, axis=-1, keepdims=True)
    )
    grad_depth_low = grad_depth.astype(jnp.bfloat16)
    grad_first, grad_second, taps_grad, *sums_late = convolve_back(
        with_edges(grad_depth_low),
        padded,
        paired,
        taps,
        Traffic(
            sizes,
            4,
            grads=[parts(late_out_grad, late_out), parts(late_in_grad, late_in)],
            split=6,
        ),
    )
    kernel_grad = taps_grad[:KERNEL]
    grad_paired = jnp.concatenate([grad_first, grad_second], axis=1)
    pointwise_in_grad = weight_grad(normed3, grad_paired)
    grad_normed3 = back_product(grad_paired, w_point_in)
    grad_in3, gain_grad2, bias_grad2 = norm_back(hidden2, gains[2], biases[2], grad_normed3)
    grad2 = grad3 + grad_in3

    grad_out2 = grad2.astype(jnp.bfloat16)
    mixer_out_grad = weight_grad(mixed_rows, grad_out2)
    grad_mixed = back_product(grad_out2, w_mixer).astype(jnp.bfloat16)
    grad_queries, keys_own, values_own, keys_far, values_far, near, far_sums, *sums_depth = attend_back(
        packed,
        far,
        offsets,
        log_total,
        grad_mixed,
        Traffic(
            sizes,
            5,
            grads=[parts(pointwise_out_grad, pointwise_out), parts(pointwise_in_grad, pointwise_in)],
            split=6,
        ),
    )
    table_grad = table_back(near, far_sums, core * (rows // QB)).reshape(H * NB)
    keys_there, values_there = from_other(keys_far), from_other(values_far)
    grad_packed = jnp.concatenate(
        [
            grad_queries,
            (keys_own.astype(jnp.float32) + keys_there.astype(jnp.float32)).astype(jnp.bfloat16),
            (values_own.astype(jnp.float32) + values_there.astype(jnp.float32)).astype(jnp.bfloat16),
        ],
        axis=-1,
    )
    qkv_grad = weight_grad(normed2, grad_packed)
    grad_normed2 = back_product(grad_packed, w_qkv)
    grad_in2, gain_grad1, bias_grad1 = norm_back(hidden1, gains[1], biases[1], grad_normed2)
    grad1 = grad2 + grad_in2
    grad0, early_in_grad, early_out_grad, norm_sums0, *sums_mixer = ffn_back(
        hidden0,
        normed1,
        grad1,
        norms_of(0),
        inner1,
        w_early_in,
        w_early_out,
        Traffic(
            sizes,
            6,
            grads=[parts(mixer_out_grad, mixer_out), parts(qkv_grad, qkv_weight)],
            swapped=[activations.reshape(groups, run, D)],
            pace=1.3,
        ),
    )
    grad_frames = jnp.where(masked, 0.0, grad0).astype(jnp.bfloat16)
    mask_grad = jnp.sum(jnp.where(masked, grad0, 0.0), axis=0)
    gain_stack = jnp.stack([norm_sums0[0], gain_grad1, gain_grad2, norm_sums3[0], gain_grad4])
    bias_stack = jnp.stack([norm_sums0[1], bias_grad1, bias_grad2, norm_sums3[1], bias_grad4])
    small_grads = repack_small(
        [mask_grad, gain_stack, bias_stack, channel_gain_grad, channel_bias_grad, kernel_grad, table_grad],
        small_shapes,
        devices,
    ).astype(jnp.bfloat16)

    sums_early = move(
        Traffic(
            sizes,
            7,
            grads=[
                parts(early_out_grad, early_out),
                parts(early_in_grad, early_in),
                small_grads.reshape((chips, 2, line) + SMALL),
            ],
            swapped=[grad_frames.reshape(groups, run, D)],
        )
    )
    small_sums = sums_early[2].reshape(-1)[:small_size]
    small_out, at = [], 0
    for shape in small_shapes:
        size = math.prod(shape)
        small_out.append(small_sums[at : at + size].reshape(shape))
        at += size
    return (
        sums_mixer[2],
        sums_early[3].astype(jnp.float32),
        small_out[0],
        small_out[1],
        small_out[2],
        small_out[3],
        small_out[4],
        sums_early[1].reshape(early_in.shape),
        sums_early[0].reshape(early_out.shape),
        sums_mixer[1].reshape(qkv_weight.shape),
        sums_mixer[0].reshape(mixer_out.shape),
        sums_depth[1].reshape(pointwise_in.shape),
        sums_depth[0].reshape(pointwise_out.shape),
        small_out[5],
        sums_late[1].reshape(late_in.shape),
        sums_late[0].reshape(late_out.shape),
        small_out[6],
    )


def solution(mesh):
    in_specs = (
        P("batch", "frames", None),
        P("batch", None),
        P(("batch", "frames")),
        P(None, ("batch", "frames")),
        P(None, ("batch", "frames")),
        P(("batch", "frames")),
        P(("batch", "frames")),
        P(("batch", "frames"), None),
        P(("batch", "frames"), None),
        P(("batch", "frames"), None),
        P(("batch", "frames"), None),
        P(("batch", "frames"), None),
        P(("batch", "frames"), None),
        P(None, ("batch", "frames")),
        P(("batch", "frames"), None),
        P(("batch", "frames"), None),
        P(("batch", "frames")),
        P("batch", "frames", None),
    )
    out_specs = (
        P("batch", "frames", None),
        P("batch", "frames", None),
        P(("batch", "frames")),
        P(None, ("batch", "frames")),
        P(None, ("batch", "frames")),
        P(("batch", "frames")),
        P(("batch", "frames")),
        P(("batch", "frames"), None),
        P(("batch", "frames"), None),
        P(("batch", "frames"), None),
        P(("batch", "frames"), None),
        P(("batch", "frames"), None),
        P(("batch", "frames"), None),
        P(None, ("batch", "frames")),
        P(("batch", "frames"), None),
        P(("batch", "frames"), None),
        P(("batch", "frames")),
    )
    return jax.shard_map(shards, mesh=mesh, in_specs=in_specs, out_specs=out_specs, check_vma=False)
```

```python
import functools
import math

import jax
import jax.numpy as jnp
from jax import lax
from jax.experimental import pallas as pl
from jax.experimental.pallas import tpu as pltpu
from jax.sharding import PartitionSpec as P

D = 1024
H = 16
DH = 64
C = 2048
KERNEL = 31
HALF = 15
NB = 32
EPS = 1e-05
LIMITS = (8, 12, 16, 24, 32, 48, 64, 96)
BOTH = ("batch", "frames")
SMALL = (16, 512)


MESH = pl.DeviceIdType.MESH
VMEM_BYTES = 58 * 1024 * 1024


def ring_spot(index, count):
    half = count // 2
    return index + (index // half) * (3 * half - 1 - 2 * index)


def places(chips, frames):
    batch, depth = lax.axis_index("batch"), lax.axis_index("frames")
    chip, core = batch // 2, lax.rem(batch, 2)
    spot = ring_spot(chip, chips)

    def chip_at(offset):
        return ring_spot(lax.rem(spot + offset + chips, chips), chips)

    return chip, core, depth, chip_at


def greet(chips, frames, partners):
    chip, core, depth, chip_at = places(chips, frames)
    barrier = pltpu.get_barrier_semaphore()
    for offset in (1, -1):
        pl.semaphore_signal(
            barrier, inc=1, device_id=(chip_at(offset) * 2 + core, depth), device_id_type=MESH
        )
    pl.semaphore_signal(
        barrier, inc=1, device_id=(chip * 2 + 1 - core, depth), device_id_type=MESH
    )

    @pl.when(depth > 0)
    def _():
        pl.semaphore_signal(barrier, inc=1, device_id=(chip * 2 + core, depth - 1), device_id_type=MESH)

    @pl.when(depth < frames - 1)
    def _():
        pl.semaphore_signal(barrier, inc=1, device_id=(chip * 2 + core, depth + 1), device_id_type=MESH)

    count = 3 + jnp.minimum(depth, 1) + jnp.minimum(frames - 1 - depth, 1)
    if partners:
        groups = frames // 2
        for place in range(groups):
            there, side = core * groups + place, depth // groups

            @pl.when(jnp.logical_or(there != depth, side != core))
            def _():
                pl.semaphore_signal(
                    barrier, inc=1, device_id=(chip * 2 + side, there), device_id_type=MESH
                )

        count = count + groups - (1 - jnp.abs(depth // groups - core))
    pl.semaphore_wait(barrier, count)


def swap_frames(chips, frames, sources, targets, send_sems, recv_sems, local_sem):
    chip, core, depth, chip_at = places(chips, frames)
    groups = frames // 2
    starts, ends = [], []
    for at, (source, target) in enumerate(zip(sources, targets)):
        for place in range(groups):
            there, side = core * groups + place, depth // groups
            mine = jnp.logical_and(there == depth, side == core)
            slot = lax.rem(depth, groups)
            remote = pltpu.make_async_remote_copy(
                src_ref=source.at[place],
                dst_ref=target.at[slot],
                send_sem=send_sems.at[at * groups + place],
                recv_sem=recv_sems.at[at * groups + slot],
                device_id=(chip * 2 + side, there),
                device_id_type=MESH,
            )
            arrival = pltpu.make_async_remote_copy(
                src_ref=source.at[place],
                dst_ref=target.at[place],
                send_sem=send_sems.at[at * groups + place],
                recv_sem=recv_sems.at[at * groups + place],
                device_id=(chip * 2 + side, there),
                device_id_type=MESH,
            )
            here = pltpu.make_async_copy(source.at[place], target.at[slot], local_sem.at[at])
            away = jnp.logical_not(mine)
            starts += [gated(away, remote.start), gated(mine, here.start)]
            ends += [
                gated(away, remote.wait_send),
                gated(away, arrival.wait_recv),
                gated(mine, here.wait),
            ]
    return starts, ends


def gated(condition, action):
    if condition is None:
        return action
    return lambda: pl.when(condition)(action)


def shares(columns, split):
    first = columns * split // 8
    if first % 256 or (columns - first) % 256:
        first = columns
    return (0, first), (first, columns - first)


class Timetable:
    def __init__(self, sizes, split):
        chips, frames = sizes
        half = chips // 2
        self.known = chips == 4 and frames == 4
        self.both = split < 8
        self.half, self.frames = half, frames

    def gather(self, distance, step):
        if not self.known:
            return distance + step + 0.1 * bool(step)
        if self.both:
            return ((0, 0.95, 2.45, 3.7), (1.0, 2.6, 3.75, 4.5), (3.0, 4.5, 4.9, 4.9))[step][distance]
        return ((0, 0.95, 1.95, 2.95), (1.0, 3.0, 4.5, 5.0), (3.5, 4.6, 5.6, 6.0))[step][distance]

    def gather_ring(self, distance, step):
        if not self.known:
            return distance + step
        return ((0, 1.0, 3.0), (1.0, 2.5, 4.25), (2.5, 4.25, 5.0), (4.0, 5.0, 5.25))[step][distance]

    def pair(self, distance):
        if not self.known:
            return distance + self.half + 0.5
        if self.both:
            return (3.05, 4.55, 5.05, 5.3)[distance]
        return (3.55, 4.65, 5.65, 6.05)[distance]

    def merge(self, distance):
        if not self.known:
            return 0.01 * (self.frames - distance)
        return (1.3, 1.0, 0.7, 0.35)[distance]

    def scatter(self, distance, step):
        if not self.known:
            return self.frames - 1 - distance + step
        if self.both:
            return ((4.29, 3.49, 2.69, 1.35), (5.1, 4.3, 3.5, 2.7))[step - 1][distance]
        return ((2.6, 2.2, 1.8, 1.4), (6.4, 5.4, 4.4, 3.4))[step - 1][distance]

    def scatter_ring(self, distance, step):
        if not self.known:
            return self.half - distance + step + 0.5
        return ((2.66, 1.33, 0.4), (3.46, 2.67, 1.34), (4.27, 3.47, 2.68), (5.0, 4.28, 3.48))[step][distance]

    def scatter_last(self, distance):
        if not self.known:
            return self.half - distance + self.frames - 1 + 0.5
        return (5.1, 4.29)[distance]


class Mover:
    def __init__(self, spots, sizes, split, send_sems, recv_sems):
        self.time = Timetable(sizes, split)
        self.chips, self.frames = sizes
        self.chip, self.core, self.depth, self.chip_at = spots
        self.send_sems, self.recv_sems = send_sems, recv_sems
        self.used = 0
        self.events = []
        self.departures = []

    def copy(self, source, target, device, condition):
        at = self.used
        self.used += 1
        made = pltpu.make_async_remote_copy(
            src_ref=source,
            dst_ref=target,
            send_sem=self.send_sems.at[at],
            recv_sem=self.recv_sems.at[at],
            device_id=device,
            device_id_type=MESH,
        )
        self.departures.append(gated(condition, made.wait_send))
        return made

    def at(self, time, *actions):
        self.events += [(time, action) for action in actions]

    def other_core(self):
        return (self.chip * 2 + 1 - self.core, self.depth)

    def group(self, offset):
        at = self.depth + offset
        if offset == 0:
            return at, None
        return jnp.clip(at, 0, self.frames - 1), jnp.logical_and(at >= 0, at < self.frames)

    def chips_at(self, distance):
        if distance == 0:
            return (self.chip,)
        if distance == self.chips // 2:
            return (self.chip_at(distance),)
        return (self.chip_at(distance), self.chip_at(-distance))

    def offsets(self, distance):
        return (0,) if distance == 0 else (-distance, distance)


class Gather(Mover):
    def __init__(self, spots, sizes, shard, whole, split, send_sems, recv_sems, local_sems):
        super().__init__(spots, sizes, split, send_sems, recv_sems)
        self.shard, self.whole = shard, whole
        self.first, self.last = shares(shard.shape[1], split)
        self.local = pltpu.make_async_copy(
            shard, whole.at[self.chip, self.core, self.depth], local_sems.at[0]
        )
        self.at(0, self.local.start)
        for distance in range(self.frames):
            self.spread(distance)
        if self.last[1]:
            for distance in range(self.chips // 2 + 1):
                self.spread_ring(distance)
        for distance in range(self.frames):
            self.hand_over(distance)
        self.ends = self.departures

    def spread(self, distance):
        chip, core, depth, half = self.chip, self.core, self.depth, self.chips // 2
        for offset in self.offsets(distance):
            held, valid = self.group(offset)
            start, columns = self.first
            block = self.whole.at[chip, core, held, :, pl.ds(start, columns)]
            source = block if distance else self.shard.at[:, pl.ds(start, columns)]
            for way in (1, -1):
                if distance + 1 == self.frames or offset * way > 0:
                    continue
                into, there = self.group(way)
                condition = there if valid is None else jnp.logical_and(valid, there)
                made = self.copy(source, block, (chip * 2 + core, into), condition)
                self.at(self.time.gather(distance, 0), gated(condition, made.start))
                comes = self.group(offset - way)[1]
                self.at(self.time.gather(distance + 1, 0), gated(comes, made.wait_recv))
            for step in range(1, half + 1):
                for side, way in enumerate((1, -1)):
                    part = pl.ds(start, columns)
                    if step == half:
                        part = pl.ds(start + side * columns // 2, columns // 2)
                    origin = self.chip_at(-way * (step - 1))
                    target = self.whole.at[origin, core, held, :, part]
                    given = self.shard.at[:, part] if distance == 0 and step == 1 else target
                    made = self.copy(given, target, (self.chip_at(way) * 2 + core, depth), valid)
                    self.at(self.time.gather(distance, step - 1), gated(valid, made.start))
                    self.at(self.time.gather(distance, step), gated(valid, made.wait_recv))

    def hand_over(self, distance):
        for offset in self.offsets(distance):
            held, valid = self.group(offset)
            line = self.whole.at[:, self.core, held]
            pair = self.copy(line, line, self.other_core(), valid)
            if distance == 0:
                self.at(self.time.pair(0), self.local.wait)
            self.at(self.time.pair(distance), gated(valid, pair.start))
            self.departures.append(gated(valid, pair.wait_recv))

    def spread_ring(self, distance):
        core, depth, half = self.core, self.depth, self.chips // 2
        start, columns = self.last
        everything = pl.ds(start, columns)
        if distance < half:
            step = distance + 1
            for side, way in enumerate((1, -1)):
                part = everything
                if step == half:
                    part = pl.ds(start + side * columns // 2, columns // 2)
                target = self.whole.at[self.chip_at(-way * distance), core, depth, :, part]
                given = target if distance else self.shard.at[:, part]
                made = self.copy(given, target, (self.chip_at(way) * 2 + core, depth), None)
                self.at(self.time.gather_ring(distance, 0), made.start)
                self.at(self.time.gather_ring(distance + 1, 0), made.wait_recv)
        for place, chip in enumerate(self.chips_at(distance)):
            for step in range(1, self.frames):
                for way in (1, -1):
                    held, there = self.group(-way * (step - 1))
                    into, beside = self.group(way)
                    valid = beside if there is None else jnp.logical_and(there, beside)
                    block = self.whole.at[chip, core, held, :, everything]
                    given = block if distance or step > 1 else self.shard.at[:, everything]
                    made = self.copy(given, block, (self.chip * 2 + core, into), valid)
                    self.at(self.time.gather_ring(distance, step - 1), gated(valid, made.start))
                    comes = self.group(-way * step)[1]
                    self.at(self.time.gather_ring(distance, step), gated(comes, made.wait_recv))


class Scatter(Mover):
    def __init__(
        self, spots, sizes, grads, out, total, stage, landings, split, send_sems, recv_sems, local_sems
    ):
        super().__init__(spots, sizes, split, send_sems, recv_sems)
        self.grads, self.out, self.total, self.stage = grads, out, total, stage
        (self.halves, self.fulls, self.lines), self.landings = landings[:3], list(landings[3:])
        self.local_sems = local_sems
        self.first, self.last = shares(out.shape[1], split)
        self.merges = 0
        for distance in reversed(range(self.frames)):
            self.collect(distance)
        if self.last[1]:
            for distance in reversed(range(self.chips // 2 + 1)):
                self.collect_ring(distance)
        self.ends = [self.finish] + self.departures

    def add(self, where, piece):
        total = self.total
        total[where] = total[where] + piece

    def merge(self, held, pair, load, stage):
        load.wait()
        pair.wait_recv()

        @pl.loop(0, self.chips)
        def _(chip):
            self.add((chip, held), stage[chip])

    def settle(self, made, where, landed):
        made.wait_recv()
        self.add(where, landed[...])

    def collect(self, distance):
        core, depth, half = self.core, self.depth, self.chips // 2
        for offset in self.offsets(distance):
            held, valid = self.group(offset)
            pair = self.copy(
                self.grads.at[:, 1 - core, held], self.total.at[:, held], self.other_core(), valid
            )
            stage = self.stage.at[held]
            load = pltpu.make_async_copy(
                self.grads.at[:, core, held], stage, self.local_sems.at[self.merges]
            )
            self.merges += 1
            begin = -0.01 * (distance + 1)
            self.at(begin, gated(valid, pair.start), gated(valid, load.start))
            self.at(
                self.time.merge(distance),
                gated(valid, functools.partial(self.merge, held, pair, load, stage)),
            )
            start, columns = self.first
            everything = pl.ds(start, columns)
            for step in range(1, half + 1):
                for side, way in enumerate((1, -1)):
                    part = everything
                    if step == 1:
                        part = pl.ds(start + side * columns // 2, columns // 2)
                    reach = half - step + 1
                    goal = self.chip_at(way * reach)
                    if step == 1:
                        landed = self.halves.at[held, side]
                    else:
                        landed = self.fulls.at[held, 2 * (step - 2) + side]
                    made = self.copy(
                        self.total.at[goal, held, :, part],
                        landed,
                        (self.chip_at(way) * 2 + core, depth),
                        valid,
                    )
                    ready = self.time.scatter(distance, step - 1) if step > 1 else self.time.merge(distance)
                    self.at(ready, gated(valid, made.start))
                    where = (self.chip_at(way * (reach - 1)), held, slice(None), part)
                    self.at(
                        self.time.scatter(distance, step),
                        gated(valid, functools.partial(self.settle, made, where, landed)),
                    )
            if distance == 0:
                continue
            way = 1 if offset > 0 else -1
            landed = self.lines.at[0 if way > 0 else 1, held]
            made = self.copy(
                self.total.at[self.chip, held, :, everything],
                landed,
                (self.chip * 2 + core, self.group(way)[0]),
                valid,
            )
            self.at(self.time.scatter(distance, half), gated(valid, made.start))
            before = self.group(-way)[1]
            goes, there = self.group(offset - way)
            comes = before if there is None else jnp.logical_and(before, there)
            where = (self.chip, goes, slice(None), everything)
            arrived = self.lines.at[0 if way > 0 else 1, goes]
            self.at(
                self.time.scatter(distance - 1, half) - 0.01,
                gated(comes, functools.partial(self.settle, made, where, arrived)),
            )

    def collect_ring(self, distance):
        core, depth, half = self.core, self.depth, self.chips // 2
        start, columns = self.last
        everything = pl.ds(start, columns)
        for chip in self.chips_at(distance):
            for step in range(1, self.frames):
                for way in (1, -1):
                    reach = way * (self.frames - step)
                    held, valid = self.group(reach)
                    landed = self.landings.pop(0)
                    made = self.copy(
                        self.total.at[chip, held, :, everything],
                        landed,
                        (self.chip * 2 + core, self.group(way)[0]),
                        valid,
                    )
                    self.at(self.time.scatter_ring(distance, step - 1), gated(valid, made.start))
                    before = self.group(-way)[1]
                    goes, there = self.group(reach - way)
                    comes = before if there is None else jnp.logical_and(before, there)
                    where = (chip, goes, slice(None), everything)
                    self.at(
                        self.time.scatter_ring(distance, step),
                        gated(comes, functools.partial(self.settle, made, where, landed)),
                    )
        if distance == 0:
            return
        whole = max(
            self.time.scatter_ring(distance, self.frames - 1),
            self.time.scatter_last(distance) if distance < half else 0,
        )
        for side, way in enumerate((1, -1)):
            part = everything
            if distance == half:
                part = pl.ds(start + side * columns // 2, columns // 2)
            goal = self.chip_at(way * distance)
            landed = self.landings.pop(0)
            made = self.copy(
                self.total.at[goal, depth, :, part],
                landed,
                (self.chip_at(way) * 2 + core, depth),
                None,
            )
            self.at(whole + 0.01, made.start)
            where = (self.chip_at(way * (distance - 1)), depth, slice(None), part)
            self.at(
                self.time.scatter_last(distance - 1),
                functools.partial(self.settle, made, where, landed),
            )

    def finish(self):
        self.out[...] = self.total[self.chip, self.depth].astype(self.out.dtype)


def landing_shapes(sizes, rows, columns, split):
    chips, frames = sizes
    (_, first), (_, last) = shares(columns, split)
    half = chips // 2
    shapes = [
        (frames, 2, rows, first // 2),
        (frames, max(2 * (half - 1), 1), rows, first),
        (2, frames, rows, first),
    ]
    if last:
        for distance in reversed(range(half + 1)):
            many = 1 if distance in (0, half) else 2
            shapes += [(rows, last)] * (many * 2 * (frames - 1))
            if distance:
                shapes += [(rows, last // 2 if distance == half else last)] * 2
    return shapes


class Traffic:
    def __init__(
        self, sizes, identity, shards=(), grads=(), swapped=(), swap_at=0, split=8, pace=1.0
    ):
        self.sizes, self.identity = sizes, identity
        self.shards, self.grads, self.swapped = list(shards), list(grads), list(swapped)
        self.swap_at, self.split, self.pace = swap_at, split, pace
        self.active = bool(self.shards or self.grads or self.swapped)

    def operands(self):
        return self.shards + self.grads + self.swapped

    def in_specs(self):
        return [pl.BlockSpec(memory_space=pl.ANY)] * len(self.operands())

    def out_shapes(self):
        chips, frames = self.sizes
        return (
            [jax.ShapeDtypeStruct((chips, 2, frames) + s.shape, s.dtype) for s in self.shards]
            + [jax.ShapeDtypeStruct(g.shape[3:], jnp.float32) for g in self.grads]
            + [jax.ShapeDtypeStruct(s.shape, s.dtype) for s in self.swapped]
        )

    def out_specs(self):
        anywhere = pl.BlockSpec(memory_space=pl.ANY)
        return (
            [anywhere] * len(self.shards)
            + [pl.BlockSpec(memory_space=pltpu.VMEM)] * len(self.grads)
            + [anywhere] * len(self.swapped)
        )

    def scratch(self):
        if not self.active:
            return []
        chips, frames = self.sizes
        shapes = []
        for grad in self.grads:
            shard = grad.shape[3:]
            shapes += [
                pltpu.VMEM((chips, frames) + shard, grad.dtype),
                pltpu.VMEM((frames, chips) + shard, grad.dtype),
            ]
            shapes += [pltpu.VMEM(shape, grad.dtype) for shape in landing_shapes(self.sizes, *shard, self.split)]
        copies = (2 * frames - 1) * (3 + chips) + chips * (2 * frames - 1)
        arrays = max(len(self.shards) + len(self.grads), 1)
        swaps = max(len(self.swapped), 1)
        return shapes + [
            pltpu.SemaphoreType.DMA((arrays, copies)),
            pltpu.SemaphoreType.DMA((arrays, copies)),
            pltpu.SemaphoreType.DMA((arrays, 2 * frames - 1)),
            pltpu.SemaphoreType.DMA((swaps * (frames // 2),)),
            pltpu.SemaphoreType.DMA((swaps * (frames // 2),)),
            pltpu.SemaphoreType.DMA((swaps,)),
        ]

    def plan(self, ins, outs, scratch):
        if not self.active:
            return []
        chips, frames = self.sizes
        scratch = list(scratch)
        send_sems, recv_sems, local_sems, swap_send, swap_recv, swap_local = scratch[-6:]
        spots = places(chips, frames)
        gathers, scatters = len(self.shards), len(self.grads)
        parts = []
        for at in range(gathers + scatters):
            sems = (send_sems.at[at], recv_sems.at[at], local_sems.at[at])
            if at < gathers:
                parts.append(Gather(spots, self.sizes, ins[at], outs[at], self.split, *sems))
                continue
            total, stage = scratch.pop(0), scratch.pop(0)
            many = len(landing_shapes(self.sizes, *outs[at].shape, self.split))
            landings = [scratch.pop(0) for _ in range(many)]
            parts.append(
                Scatter(
                    spots, self.sizes, ins[at], outs[at], total, stage, landings, self.split, *sems
                )
            )
        events = [event for part in parts for event in part.events]
        last = max([time for time, _ in events], default=1.0)
        ends = sum([part.ends for part in parts], [])
        if self.swapped:
            starts, waits = swap_frames(
                chips,
                frames,
                ins[gathers + scatters :],
                outs[gathers + scatters :],
                swap_send,
                swap_recv,
                swap_local,
            )
            events += [(self.swap_at, action) for action in starts]
            ends += waits
        events.append((-1, functools.partial(greet, chips, frames, bool(self.swapped))))
        events = sorted(events, key=lambda event: event[0])
        return [(max(time / last, 0.0) * 0.97, action) for time, action in events] + [
            (1.0, action) for action in ends
        ]


def run_plan(traffic, ins, outs, scratch, step, steps, late=False):
    if not traffic.active:
        return
    whens = [when for when, _ in traffic.plan(ins, outs, scratch)]
    due = [min(int(when * traffic.pace * steps), steps) for when in whens]

    def run(place):
        for at, (_, action) in zip(due, traffic.plan(ins, outs, scratch)):
            if at == place:
                action()

    if late:
        pl.when(step == steps - 1)(functools.partial(run, steps))
        return
    for place in sorted(set(due) - {steps}):
        pl.when(step == place)(functools.partial(run, place))


def traffic_kernel(traffic, *refs):
    count = len(traffic.operands())
    for _, action in traffic.plan(refs[:count], refs[count : 2 * count], refs[2 * count :]):
        action()


def move(traffic):
    return pl.pallas_call(
        functools.partial(traffic_kernel, traffic),
        out_shape=traffic.out_shapes(),
        in_specs=traffic.in_specs(),
        out_specs=traffic.out_specs(),
        scratch_shapes=traffic.scratch(),
        compiler_params=traffic_params(traffic),
    )(*traffic.operands())


def traffic_params(traffic):
    if not traffic.active:
        return pltpu.CompilerParams(vmem_limit_bytes=VMEM_BYTES)
    return pltpu.CompilerParams(
        collective_id=traffic.identity, has_side_effects=True, vmem_limit_bytes=VMEM_BYTES
    )


def layer_norm(values, norm_gain, norm_shift):
    centred = values - jnp.mean(values, axis=-1, keepdims=True)
    spread = jnp.mean(centred * centred, axis=-1, keepdims=True)
    return centred * lax.rsqrt(spread + EPS) * norm_gain + norm_shift


def bucket_of(relative):
    magnitude = jnp.abs(relative)
    above = jnp.zeros_like(relative)
    for threshold in LIMITS:
        above = above + (magnitude >= threshold).astype(jnp.int32)
    inner_bucket = jnp.where(magnitude < 8, magnitude, 7 + above)
    return inner_bucket + NB // 2 * (relative > 0).astype(jnp.int32)


def product(operand_a, operand_b):
    return jnp.dot(operand_a, operand_b, preferred_element_type=jnp.float32)


def weight_grad(operand_a, operand_b):
    return lax.dot_general(
        operand_a, operand_b, (((0,), (0,)), ((), ())), preferred_element_type=jnp.float32
    ).astype(jnp.bfloat16)


def back_product(operand_a, operand_b):
    return lax.dot_general(
        operand_a, operand_b, (((1,), (1,)), ((), ())), preferred_element_type=jnp.float32
    )


def gated_unit(paired):
    return paired[:, :C] * jax.nn.sigmoid(paired[:, C:])


def depth_post(depth_values, norm_gain, norm_shift):
    return jax.nn.silu(layer_norm(depth_values, norm_gain, norm_shift))


def norm_back(hidden, norm_gain, norm_shift, upstream):
    normed_unused, pull_back = jax.vjp(layer_norm, hidden, norm_gain, norm_shift)
    return pull_back(upstream)


TILE = 512
CHUNK = 64


def dot_nt(left, right):
    return lax.dot_general(left, right, (((1,), (1,)), ((), ())), preferred_element_type=jnp.float32)


def dot_nn(left, right):
    return lax.dot_general(left, right, (((1,), (0,)), ((), ())), preferred_element_type=jnp.float32)


def sigmoid(values):
    return 0.5 * jnp.tanh(0.5 * values) + 0.5


def norm_parts(values):
    centred = values - jnp.mean(values, axis=-1, keepdims=True)
    rstd = lax.rsqrt(jnp.mean(centred * centred, axis=-1, keepdims=True) + EPS)
    return centred * rstd, rstd


def gain_row(rows_ref, which):
    return rows_ref[1 + which : 2 + which, :]


def norm_chunk(values, rows_ref, which):
    scaled, _ = norm_parts(values)
    return scaled * gain_row(rows_ref, which) + rows_ref[6 + which : 7 + which, :]


def chunks(rows):
    def each(body):
        @pl.loop(0, rows // CHUNK)
        def _(at):
            body(pl.ds(pl.multiple_of(at * CHUNK, CHUNK), CHUNK))

    return each


def ffn_kernel(traffic, which, hidden_ref, norms_ref, w_in_ref, w_out_ref, *refs):
    moved = len(traffic.operands())
    ins, refs = refs[:moved], refs[moved:]
    out_ref, inner_ref, normed_ref, next_ref = refs[:4]
    outs, refs = refs[4 : 4 + moved], refs[4 + moved :]
    total, refs = refs[0], refs[1:]
    step, steps = pl.program_id(0), pl.num_programs(0)
    run_plan(traffic, ins, outs, refs, step, FFN_STEPS)
    each = chunks(hidden_ref.shape[0])

    @pl.when(step == 0)
    def _():
        def body(here):
            normed_ref[here, :] = norm_chunk(hidden_ref[here, :], norms_ref, which).astype(jnp.bfloat16)
            total[here, :] = jnp.zeros((CHUNK, total.shape[1]), jnp.float32)

        each(body)

    inner = dot_nn(normed_ref[...], w_in_ref[...])
    inner_ref[...] = inner.astype(jnp.bfloat16)
    total[...] += dot_nn((inner * sigmoid(inner)).astype(jnp.bfloat16), w_out_ref[...])

    @pl.when(step == steps - 1)
    def _():
        def body(here):
            hidden = hidden_ref[here, :] + 0.5 * total[here, :]
            out_ref[here, :] = hidden
            next_ref[here, :] = norm_chunk(hidden, norms_ref, which + 1).astype(jnp.bfloat16)

        each(body)

    run_plan(traffic, ins, outs, refs, step, FFN_STEPS, late=True)


FFN_STEPS = 8


def resident(shape):
    return pl.BlockSpec(shape, lambda step: (0,) * len(shape))


def ffn(hidden, norms, which, weight_in, weight_out, traffic):
    rows, width = hidden.shape
    tile = weight_in.shape[1] // FFN_STEPS
    return pl.pallas_call(
        functools.partial(ffn_kernel, traffic, which),
        grid=(FFN_STEPS,),
        out_shape=[
            jax.ShapeDtypeStruct((rows, width), jnp.float32),
            jax.ShapeDtypeStruct((rows, weight_in.shape[1]), jnp.bfloat16),
            jax.ShapeDtypeStruct((rows, width), jnp.bfloat16),
            jax.ShapeDtypeStruct((rows, width), jnp.bfloat16),
        ]
        + traffic.out_shapes(),
        in_specs=[
            resident((rows, width)),
            resident(norms.shape),
            pl.BlockSpec((width, tile), lambda step: (0, step)),
            pl.BlockSpec((tile, width), lambda step: (step, 0)),
        ]
        + traffic.in_specs(),
        out_specs=[
            resident((rows, width)),
            pl.BlockSpec((rows, tile), lambda step: (0, step)),
            resident((rows, width)),
            resident((rows, width)),
        ]
        + traffic.out_specs(),
        scratch_shapes=[pltpu.VMEM((rows, width), jnp.float32)] + traffic.scratch(),
        compiler_params=traffic_params(traffic),
    )(hidden, norms, weight_in, weight_out, *traffic.operands())


def ffn_back_kernel(
    traffic, which, hidden_ref, normed_ref, grad_ref, norms_ref, inner_ref, w_in_ref, w_out_ref, *refs
):
    moved = len(traffic.operands())
    ins, refs = refs[:moved], refs[moved:]
    out_ref, g_in_ref, g_out_ref, sums_ref = refs[:4]
    outs, refs = refs[4 : 4 + moved], refs[4 + moved :]
    (half_grad, turned, total), refs = refs[:3], refs[3:]
    step, steps = pl.program_id(0), pl.num_programs(0)
    run_plan(traffic, ins, outs, refs, step, FFN_STEPS)
    each = chunks(hidden_ref.shape[0])

    @pl.when(step == 0)
    def _():
        def body(here):
            half_grad[here, :] = (0.5 * grad_ref[here, :]).astype(jnp.bfloat16)
            total[here, :] = jnp.zeros((CHUNK, total.shape[1]), jnp.float32)

        each(body)
        turned[...] = normed_ref[...].T
        sums_ref[...] = jnp.zeros_like(sums_ref)

    inner = inner_ref[...].astype(jnp.float32)
    gate = sigmoid(inner)
    active = (inner * gate).astype(jnp.bfloat16)
    g_out_ref[...] = dot_nn(active.T, half_grad[...]).astype(jnp.bfloat16)
    slope = gate * (1.0 + inner * (1.0 - gate))
    grad_inner = (dot_nt(half_grad[...], w_out_ref[...]) * slope).astype(jnp.bfloat16)
    g_in_ref[...] = dot_nn(turned[...], grad_inner).astype(jnp.bfloat16)
    total[...] += dot_nt(grad_inner, w_in_ref[...])

    @pl.when(step == steps - 1)
    def _():
        def body(here):
            scaled, rstd = norm_parts(hidden_ref[here, :])
            upstream = total[here, :]
            sums_ref[0:1, :] += jnp.sum(upstream * scaled, axis=0, keepdims=True)
            sums_ref[1:2, :] += jnp.sum(upstream, axis=0, keepdims=True)
            weighted = upstream * gain_row(norms_ref, which)
            back = weighted - jnp.mean(weighted, axis=-1, keepdims=True)
            back = back - scaled * jnp.mean(weighted * scaled, axis=-1, keepdims=True)
            out_ref[here, :] = grad_ref[here, :] + rstd * back

        each(body)

    run_plan(traffic, ins, outs, refs, step, FFN_STEPS, late=True)


def ffn_back(hidden, normed, grad, norms, which, inner, weight_in, weight_out, traffic):
    rows, width = hidden.shape
    tile = weight_in.shape[1] // FFN_STEPS
    return pl.pallas_call(
        functools.partial(ffn_back_kernel, traffic, which),
        grid=(FFN_STEPS,),
        out_shape=[
            jax.ShapeDtypeStruct((rows, width), jnp.float32),
            jax.ShapeDtypeStruct(weight_in.shape, jnp.bfloat16),
            jax.ShapeDtypeStruct(weight_out.shape, jnp.bfloat16),
            jax.ShapeDtypeStruct((8, width), jnp.float32),
        ]
        + traffic.out_shapes(),
        in_specs=[
            resident((rows, width)),
            resident((rows, width)),
            resident((rows, width)),
            resident(norms.shape),
            pl.BlockSpec((rows, tile), lambda step: (0, step)),
            pl.BlockSpec((width, tile), lambda step: (0, step)),
            pl.BlockSpec((tile, width), lambda step: (step, 0)),
        ]
        + traffic.in_specs(),
        out_specs=[
            resident((rows, width)),
            pl.BlockSpec((width, tile), lambda step: (0, step)),
            pl.BlockSpec((tile, width), lambda step: (step, 0)),
            resident((8, width)),
        ]
        + traffic.out_specs(),
        scratch_shapes=[
            pltpu.VMEM((rows, width), jnp.bfloat16),
            pltpu.VMEM((width, rows), jnp.bfloat16),
            pltpu.VMEM((rows, width), jnp.float32),
        ]
        + traffic.scratch(),
        compiler_params=traffic_params(traffic),
    )(hidden, normed, grad, norms, inner, weight_in, weight_out, *traffic.operands())


QB = 128
PAIRS = H // 2
BAND = 3 * QB


def stacked(block):
    lanes = lax.broadcasted_iota(jnp.int32, block.shape, 1)
    nothing = jnp.zeros_like(block)
    return jnp.concatenate(
        [jnp.where(lanes < DH, block, nothing), jnp.where(lanes >= DH, block, nothing)], axis=0
    )


def own_halves(both):
    channels = lax.broadcasted_iota(jnp.int32, (2 * DH, QB), 0)
    return jnp.where(channels < DH, both[:, :QB], both[:, QB:]).T


def offset_rows(table):
    offsets = (jnp.arange(4, dtype=jnp.int32)[:, None] - 1) * QB - jnp.arange(QB, dtype=jnp.int32)
    onehot = (jnp.arange(NB)[:, None, None] == bucket_of(offsets)[None]).astype(jnp.float32)
    rows = jnp.dot(table, onehot.reshape(NB, 4 * QB), precision=lax.Precision.HIGHEST)
    return rows.reshape(PAIRS, 8, QB)


def fill_strip(strip, rows_ref, length):
    far = length - 2 * QB
    rows_of = lax.broadcasted_iota(jnp.int32, (QB, QB), 0)
    lanes_of = lax.broadcasted_iota(jnp.int32, (QB, QB), 1)
    for head in range(2):
        columns = slice(head * QB, (head + 1) * QB)
        turned = []
        for at in range(4):
            row = jnp.broadcast_to(rows_ref[0, head * 4 + at : head * 4 + at + 1, :], (QB, QB))
            turned.append(pltpu.roll(row, 0, 1, stride=1, stride_axis=0))
        for tile in range(3):
            strip[far + tile * QB : far + (tile + 1) * QB, columns] = jnp.where(
                lanes_of >= rows_of, turned[tile], turned[tile + 1]
            )

        @pl.loop(0, far // QB)
        def _(at):
            before, after = pl.multiple_of(at * QB, QB), pl.multiple_of(far + BAND + at * QB, QB)
            strip[pl.ds(before, QB), columns] = turned[0]
            strip[pl.ds(after, QB), columns] = turned[3]


def strip_start(rows, length):
    first = lax.rem(lax.axis_index("batch"), 2) * rows + pl.program_id(1) * QB
    return pl.multiple_of(length - QB - first, QB), first


def in_order(whole, own_ref, far_ref):
    rows = own_ref.shape[0]
    core = lax.rem(lax.axis_index("batch"), 2)
    whole[pl.ds(pl.multiple_of(core * rows, QB), rows), :] = own_ref[...]
    whole[pl.ds(pl.multiple_of((1 - core) * rows, QB), rows), :] = far_ref[...]


def attend_kernel(
    rows, length, traffic, rows_ref, q_ref, k_own_ref, v_own_ref, k_far_ref, v_far_ref, *refs
):
    moved = len(traffic.operands())
    ins, refs = refs[:moved], refs[moved:]
    (out_ref, exact_ref, log_ref), refs = refs[:3], refs[3:]
    outs, refs = refs[:moved], refs[moved:]
    (strip, score, prob, vt, k_all, v_all), refs = refs[:6], refs[6:]
    blocks = rows // QB
    step = pl.program_id(0) * blocks + pl.program_id(1)
    run_plan(traffic, ins, outs, refs, step, PAIRS * blocks)

    @pl.when(pl.program_id(1) == 0)
    def _():
        fill_strip(strip, rows_ref, length)
        in_order(k_all, k_own_ref, k_far_ref)
        in_order(v_all, v_own_ref, v_far_ref)
        vt[...] = v_all[...].T

    start, _ = strip_start(rows, length)
    score[...] = dot_nt(k_all[...], stacked(q_ref[...] * 0.125))

    def highest(at, most):
        here = pl.ds(pl.multiple_of(at * QB, QB), QB)
        values = score[here, :] + strip[pl.ds(pl.multiple_of(start + at * QB, QB), QB), :]
        score[here, :] = values
        return jnp.maximum(most, jnp.max(values.reshape(QB // 8, 8, 2 * QB), axis=0))

    most = lax.fori_loop(
        0, length // QB, highest, jnp.full((8, 2 * QB), -jnp.inf, jnp.float32), unroll=True
    )
    most = jnp.max(most, axis=0, keepdims=True)

    def weigh(at, total):
        here = pl.ds(pl.multiple_of(at * QB, QB), QB)
        values = jnp.exp(score[here, :] - most)
        prob[here, :] = values.astype(jnp.bfloat16)
        return total + jnp.sum(values.reshape(QB // 8, 8, 2 * QB), axis=0)

    total = lax.fori_loop(
        0, length // QB, weigh, jnp.zeros((8, 2 * QB), jnp.float32), unroll=True
    )
    total = jnp.sum(total, axis=0, keepdims=True)
    mixed = dot_nn(vt[...], prob[...]) / total
    exact_ref[...] = own_halves(mixed)
    out_ref[...] = exact_ref[...].astype(out_ref.dtype)
    log_ref[0] = most + jnp.log(total)
    run_plan(traffic, ins, outs, refs, step, PAIRS * blocks, late=True)


def attend(packed, far, offsets, traffic):
    rows = packed.shape[0]
    length = 2 * rows
    blocks = rows // QB
    return pl.pallas_call(
        functools.partial(attend_kernel, rows, length, traffic),
        grid=(PAIRS, blocks),
        out_shape=[
            jax.ShapeDtypeStruct((rows, D), jnp.bfloat16),
            jax.ShapeDtypeStruct((rows, D), jnp.float32),
            jax.ShapeDtypeStruct((PAIRS * blocks, 1, 2 * QB), jnp.float32),
        ]
        + traffic.out_shapes(),
        in_specs=[
            pl.BlockSpec((1, 8, QB), lambda p, b: (p, 0, 0)),
            pl.BlockSpec((QB, 2 * DH), lambda p, b: (b, p)),
            pl.BlockSpec((rows, 2 * DH), lambda p, b: (0, PAIRS + p)),
            pl.BlockSpec((rows, 2 * DH), lambda p, b: (0, 2 * PAIRS + p)),
            pl.BlockSpec((rows, 2 * DH), lambda p, b: (0, p)),
            pl.BlockSpec((rows, 2 * DH), lambda p, b: (0, PAIRS + p)),
        ]
        + traffic.in_specs(),
        out_specs=[
            pl.BlockSpec((QB, 2 * DH), lambda p, b: (b, p)),
            pl.BlockSpec((QB, 2 * DH), lambda p, b: (b, p)),
            pl.BlockSpec((1, 1, 2 * QB), lambda p, b: (p * blocks + b, 0, 0)),
        ]
        + traffic.out_specs(),
        scratch_shapes=[
            pltpu.VMEM((2 * length - QB, 2 * QB), jnp.float32),
            pltpu.VMEM((length, 2 * QB), jnp.float32),
            pltpu.VMEM((length, 2 * QB), jnp.bfloat16),
            pltpu.VMEM((2 * DH, length), jnp.bfloat16),
            pltpu.VMEM((length, 2 * DH), jnp.bfloat16),
            pltpu.VMEM((length, 2 * DH), jnp.bfloat16),
        ]
        + traffic.scratch(),
        compiler_params=traffic_params(traffic),
    )(offsets, packed, packed, packed, far, far, *traffic.operands())


def attend_back_kernel(
    rows,
    length,
    traffic,
    rows_ref,
    q_ref,
    k_own_ref,
    v_own_ref,
    k_far_ref,
    v_far_ref,
    g_ref,
    mixed_ref,
    log_ref,
    *refs,
):
    moved = len(traffic.operands())
    ins, refs = refs[:moved], refs[moved:]
    (dq_ref, dk_own_ref, dv_own_ref, dk_far_ref, dv_far_ref), refs = refs[:5], refs[5:]
    (near_ref, sums_ref), refs = refs[:2], refs[2:]
    outs, refs = refs[:moved], refs[moved:]
    (strip, score, slope, prob, change, kt, dk_sum, dv_sum, near), refs = refs[:9], refs[9:]
    (k_all, v_all), refs = refs[:2], refs[2:]
    block, blocks = pl.program_id(1), rows // QB
    step = pl.program_id(0) * blocks + block
    run_plan(traffic, ins, outs, refs, step, PAIRS * blocks)

    @pl.when(block == 0)
    def _():
        fill_strip(strip, rows_ref, length)
        in_order(k_all, k_own_ref, k_far_ref)
        in_order(v_all, v_own_ref, v_far_ref)
        kt[...] = k_all[...].T
        dk_sum[...] = jnp.zeros_like(dk_sum)
        dv_sum[...] = jnp.zeros_like(dv_sum)
        near[...] = jnp.zeros_like(near)
        change[0:QB, :] = jnp.zeros((QB, 2 * QB), jnp.bfloat16)
        change[length + QB : length + 2 * QB, :] = jnp.zeros((QB, 2 * QB), jnp.bfloat16)

    start, first = strip_start(rows, length)
    q_both = stacked(q_ref[...] * 0.125)
    g_both = stacked(g_ref[...])
    score[...] = dot_nt(k_all[...], q_both)
    slope[...] = dot_nt(v_all[...], g_both)
    log_total = log_ref[0]

    inner = (g_ref[...].astype(jnp.float32) * mixed_ref[...]).T
    centre = jnp.concatenate(
        [
            jnp.sum(inner[:DH, :], axis=0, keepdims=True),
            jnp.sum(inner[DH:, :], axis=0, keepdims=True),
        ],
        axis=1,
    )
    for at in range(length // QB):
        here = pl.ds(at * QB, QB)
        bias = strip[pl.ds(pl.multiple_of(start + at * QB, QB), QB), :]
        weights = jnp.exp(score[here, :] + bias - log_total)
        prob[here, :] = weights.astype(jnp.bfloat16)
        values = weights * (slope[here, :] - centre)
        change[pl.ds(at * QB + QB, QB), :] = values.astype(jnp.bfloat16)
        sums_ref[0, at : at + 1, :] = jnp.sum(values, axis=0, keepdims=True)

    dv_sum[...] += dot_nn(prob[...], g_both)
    moved = change[QB : QB + length, :]
    dk_sum[...] += dot_nn(moved, q_both)
    dq_ref[...] = (own_halves(dot_nn(kt[...], moved)) * 0.125).astype(dq_ref.dtype)
    near[...] += change[pl.ds(pl.multiple_of(first, QB), BAND), :].astype(jnp.float32)

    @pl.when(block == pl.num_programs(1) - 1)
    def _():
        core = lax.rem(lax.axis_index("batch"), 2)
        own = pl.ds(pl.multiple_of(core * rows, QB), rows)
        far = pl.ds(pl.multiple_of((1 - core) * rows, QB), rows)
        dk_own_ref[...] = dk_sum[own, :].astype(jnp.bfloat16)
        dv_own_ref[...] = dv_sum[own, :].astype(jnp.bfloat16)
        dk_far_ref[...] = dk_sum[far, :].astype(jnp.bfloat16)
        dv_far_ref[...] = dv_sum[far, :].astype(jnp.bfloat16)
        rows_of = lax.broadcasted_iota(jnp.int32, (QB, QB), 0)
        lanes_of = lax.broadcasted_iota(jnp.int32, (QB, QB), 1)
        for head in range(2):
            for tile in range(3):
                turned = near[tile * QB : (tile + 1) * QB, head * QB : (head + 1) * QB]
                step = 1
                while step < QB:
                    turned = jnp.where(
                        lax.rem(rows_of // step, 2) == 1, pltpu.roll(turned, QB - step, 1), turned
                    )
                    step *= 2
                upper = jnp.where((lanes_of >= 1) & (lanes_of + rows_of < QB), turned, 0.0)
                for half, piece in enumerate((upper, turned - upper)):
                    at = head * 6 + tile * 2 + half
                    near_ref[0, at : at + 1, :] = jnp.sum(piece, axis=0, keepdims=True)

    run_plan(traffic, ins, outs, refs, step, PAIRS * blocks, late=True)


def attend_back(packed, far, offsets, mixed, log_total, grads, traffic):
    rows = packed.shape[0]
    length = 2 * rows
    blocks = rows // QB
    big = (length, 2 * QB)
    return pl.pallas_call(
        functools.partial(attend_back_kernel, rows, length, traffic),
        grid=(PAIRS, blocks),
        out_shape=[
            jax.ShapeDtypeStruct((rows, D), jnp.bfloat16),
            jax.ShapeDtypeStruct((rows, D), jnp.bfloat16),
            jax.ShapeDtypeStruct((rows, D), jnp.bfloat16),
            jax.ShapeDtypeStruct((rows, D), jnp.bfloat16),
            jax.ShapeDtypeStruct((rows, D), jnp.bfloat16),
            jax.ShapeDtypeStruct((PAIRS, 12, QB), jnp.float32),
            jax.ShapeDtypeStruct((PAIRS * blocks, length // QB, 2 * QB), jnp.float32),
        ]
        + traffic.out_shapes(),
        in_specs=[
            pl.BlockSpec((1, 8, QB), lambda p, b: (p, 0, 0)),
            pl.BlockSpec((QB, 2 * DH), lambda p, b: (b, p)),
            pl.BlockSpec((rows, 2 * DH), lambda p, b: (0, PAIRS + p)),
            pl.BlockSpec((rows, 2 * DH), lambda p, b: (0, 2 * PAIRS + p)),
            pl.BlockSpec((rows, 2 * DH), lambda p, b: (0, p)),
            pl.BlockSpec((rows, 2 * DH), lambda p, b: (0, PAIRS + p)),
            pl.BlockSpec((QB, 2 * DH), lambda p, b: (b, p)),
            pl.BlockSpec((QB, 2 * DH), lambda p, b: (b, p)),
            pl.BlockSpec((1, 1, 2 * QB), lambda p, b: (p * blocks + b, 0, 0)),
        ]
        + traffic.in_specs(),
        out_specs=[
            pl.BlockSpec((QB, 2 * DH), lambda p, b: (b, p)),
            pl.BlockSpec((rows, 2 * DH), lambda p, b: (0, p)),
            pl.BlockSpec((rows, 2 * DH), lambda p, b: (0, p)),
            pl.BlockSpec((rows, 2 * DH), lambda p, b: (0, p)),
            pl.BlockSpec((rows, 2 * DH), lambda p, b: (0, p)),
            pl.BlockSpec((1, 12, QB), lambda p, b: (p, 0, 0)),
            pl.BlockSpec((1, length // QB, 2 * QB), lambda p, b: (p * blocks + b, 0, 0)),
        ]
        + traffic.out_specs(),
        scratch_shapes=[
            pltpu.VMEM((2 * length - QB, 2 * QB), jnp.float32),
            pltpu.VMEM(big, jnp.float32),
            pltpu.VMEM(big, jnp.float32),
            pltpu.VMEM(big, jnp.bfloat16),
            pltpu.VMEM((length + 2 * QB, 2 * QB), jnp.bfloat16),
            pltpu.VMEM((2 * DH, length), jnp.bfloat16),
            pltpu.VMEM((length, 2 * DH), jnp.float32),
            pltpu.VMEM((length, 2 * DH), jnp.float32),
            pltpu.VMEM((BAND, 2 * QB), jnp.float32),
            pltpu.VMEM((length, 2 * DH), jnp.bfloat16),
            pltpu.VMEM((length, 2 * DH), jnp.bfloat16),
        ]
        + traffic.scratch(),
        compiler_params=traffic_params(traffic),
    )(offsets, packed, packed, packed, far, far, grads, mixed, log_total, *traffic.operands())


def table_back(near, sums, first_block):
    blocks = sums.shape[0] // PAIRS
    count = sums.shape[1]
    lane = jnp.arange(QB, dtype=jnp.int32)[None, None, :]
    tile = jnp.arange(3, dtype=jnp.int32)[:, None, None]
    half = jnp.arange(2, dtype=jnp.int32)[None, :, None]
    behind = jnp.where(half == 0, jnp.where(lane == 0, QB, lane), jnp.where(lane == 0, 0, lane - QB))
    offsets = (tile - 1) * QB - behind
    onehot = (bucket_of(offsets)[..., None] == jnp.arange(NB)).astype(jnp.float32)
    close = jnp.einsum(
        "zthl,thlb->zb",
        near.reshape(H, 3, 2, QB),
        onehot,
        precision=lax.Precision.HIGHEST,
    )
    by_block = sums.reshape(PAIRS, blocks, count, 2, QB).sum(axis=4)
    here = first_block + jnp.arange(blocks, dtype=jnp.int32)[:, None]
    there = jnp.arange(count, dtype=jnp.int32)[None, :]
    below = jnp.einsum(
        "pbch,bc->ph", by_block, (there < here - 1).astype(jnp.float32), precision=lax.Precision.HIGHEST
    ).reshape(H)
    above = jnp.einsum(
        "pbch,bc->ph", by_block, (there > here + 1).astype(jnp.float32), precision=lax.Precision.HIGHEST
    ).reshape(H)
    spread = jnp.arange(NB)[None, :]
    close = close + jnp.where(spread == NB // 2 - 1, below[:, None], 0.0)
    return close + jnp.where(spread == NB - 1, above[:, None], 0.0)


EDGE = 16
LANES = 128
BLOCK = 128


def shifted_rows(window):
    for low in range(8):
        turned = pltpu.roll(window, window.shape[0] - low, 0) if low else window
        for high in range(4):
            offset = 8 * high + low
            if 1 <= offset <= KERNEL:
                yield offset, turned[8 * high : 8 * high + BLOCK, :]


def conv_kernel(traffic, padded_ref, channels_ref, *refs):
    moved = len(traffic.operands())
    ins, refs = refs[:moved], refs[moved:]
    (depth_ref, post_ref, mean_ref, rstd_ref), refs = refs[:4], refs[4:]
    outs, refs = refs[:moved], refs[moved:]
    step = pl.program_id(0)
    run_plan(traffic, ins, outs, refs, step, CONV_BLOCKS)
    first = pl.multiple_of(step * BLOCK, BLOCK)

    @pl.loop(0, C // LANES)
    def _(at):
        lanes = pl.ds(pl.multiple_of(at * LANES, LANES), LANES)
        window = padded_ref[pl.ds(first, BLOCK + 2 * EDGE), lanes].astype(jnp.float32)
        total = jnp.zeros((BLOCK, LANES), jnp.float32)
        for offset, rows in shifted_rows(window):
            total = total + rows * channels_ref[offset + 1 : offset + 2, lanes]
        depth_ref[:, lanes] = total

    @pl.loop(0, BLOCK // 16)
    def _(at):
        here = pl.ds(pl.multiple_of(at * 16, 16), 16)
        scaled, rstd = norm_parts(depth_ref[here, :])
        mean_ref[here, :] = jnp.mean(depth_ref[here, :], axis=-1, keepdims=True)
        rstd_ref[here, :] = rstd
        normed = scaled * channels_ref[0:1, :] + channels_ref[1:2, :]
        post_ref[here, :] = (normed * sigmoid(normed)).astype(jnp.bfloat16)

    run_plan(traffic, ins, outs, refs, step, CONV_BLOCKS, late=True)


CONV_BLOCKS = 5


def convolve(padded, channels, traffic):
    rows = padded.shape[0] - 2 * EDGE
    return pl.pallas_call(
        functools.partial(conv_kernel, traffic),
        grid=(CONV_BLOCKS,),
        out_shape=[
            jax.ShapeDtypeStruct((rows, C), jnp.float32),
            jax.ShapeDtypeStruct((rows, C), jnp.bfloat16),
            jax.ShapeDtypeStruct((rows, 1), jnp.float32),
            jax.ShapeDtypeStruct((rows, 1), jnp.float32),
        ]
        + traffic.out_shapes(),
        in_specs=[resident(padded.shape), resident(channels.shape)]
        + traffic.in_specs(),
        out_specs=[
            pl.BlockSpec((BLOCK, C), lambda step: (step, 0)),
            pl.BlockSpec((BLOCK, C), lambda step: (step, 0)),
            pl.BlockSpec((BLOCK, 1), lambda step: (step, 0)),
            pl.BlockSpec((BLOCK, 1), lambda step: (step, 0)),
        ]
        + traffic.out_specs(),
        scratch_shapes=traffic.scratch(),
        compiler_params=traffic_params(traffic),
    )(padded, channels, *traffic.operands())


def conv_back_kernel(traffic, change_ref, gated_ref, first_ref, second_ref, channels_ref, *refs):
    moved = len(traffic.operands())
    ins, refs = refs[:moved], refs[moved:]
    (g_first_ref, g_second_ref, g_taps_ref), refs = refs[:3], refs[3:]
    outs, refs = refs[:moved], refs[moved:]
    sums, refs = refs[0], refs[1:]
    step = pl.program_id(0)
    run_plan(traffic, ins, outs, refs, step, C // LANES)
    sums[...] = jnp.zeros_like(sums)

    @pl.loop(0, CONV_BLOCKS)
    def _(block):
        first = pl.multiple_of(block * BLOCK, BLOCK)
        here = pl.ds(first, BLOCK)
        around = pl.ds(first, BLOCK + 2 * EDGE)
        window = change_ref[around, :].astype(jnp.float32)
        total = jnp.zeros((BLOCK, LANES), jnp.float32)
        for offset, rows in shifted_rows(window):
            total = total + rows * channels_ref[KERNEL - offset + 2 : KERNEL - offset + 3, :]
        gate = sigmoid(second_ref[here, :].astype(jnp.float32))
        through = total * gate
        g_first_ref[here, :] = through.astype(jnp.bfloat16)
        g_second_ref[here, :] = (
            through * first_ref[here, :].astype(jnp.float32) * (1.0 - gate)
        ).astype(jnp.bfloat16)

        change = change_ref[pl.ds(pl.multiple_of(first + EDGE, EDGE), BLOCK), :].astype(jnp.float32)
        window = gated_ref[around, :].astype(jnp.float32)
        for offset, rows in shifted_rows(window):
            part = jnp.sum((rows * change).reshape(BLOCK // 8, 8, LANES), axis=0)
            sums[8 * (offset - 1) : 8 * offset, :] += part

    for tap in range(KERNEL):
        g_taps_ref[tap : tap + 1, :] = jnp.sum(sums[8 * tap : 8 * tap + 8, :], axis=0, keepdims=True)

    run_plan(traffic, ins, outs, refs, step, C // LANES, late=True)


def convolve_back(change, gated, paired, channels, traffic):
    rows = change.shape[0] - 2 * EDGE
    half = C // LANES
    column = pl.BlockSpec((rows, LANES), lambda step: (0, step))
    edged = pl.BlockSpec((rows + 2 * EDGE, LANES), lambda step: (0, step))
    return pl.pallas_call(
        functools.partial(conv_back_kernel, traffic),
        grid=(half,),
        out_shape=[
            jax.ShapeDtypeStruct((rows, C), jnp.bfloat16),
            jax.ShapeDtypeStruct((rows, C), jnp.bfloat16),
            jax.ShapeDtypeStruct((KERNEL, C), jnp.float32),
        ]
        + traffic.out_shapes(),
        in_specs=[
            edged,
            edged,
            column,
            pl.BlockSpec((rows, LANES), lambda step: (0, half + step)),
            pl.BlockSpec((KERNEL + 2, LANES), lambda step: (0, step)),
        ]
        + traffic.in_specs(),
        out_specs=[column, column, pl.BlockSpec((KERNEL, LANES), lambda step: (0, step))]
        + traffic.out_specs(),
        scratch_shapes=[pltpu.VMEM((8 * KERNEL, LANES), jnp.float32)] + traffic.scratch(),
        compiler_params=traffic_params(traffic),
    )(change, gated, paired, paired, channels, *traffic.operands())


def as_shard(array):
    rows = array.shape[0]
    return array if rows % 16 == 0 else array.reshape(16, rows * array.shape[1] // 16)


def as_weight(whole, like):
    devices = math.prod(whole.shape[:3])
    return whole.reshape(devices * like.shape[0], like.shape[1])


def as_parts(grad, sizes, like):
    chips, frames = sizes
    shard = as_shard(jnp.zeros(like.shape, jnp.bfloat16)).shape
    return grad.reshape((chips, 2, frames) + shard)


def pack_small(values, small_shapes):
    flat = jnp.concatenate([value.reshape(-1) for value in values])
    return jnp.pad(flat, (0, SMALL[0] * SMALL[1] - flat.shape[0])).reshape(SMALL)


def unpack_small(packed, at, many):
    count, size = many
    devices = packed.shape[0]
    piece = packed[:, at : at + count * size].reshape(devices, count, size).astype(jnp.float32)
    return jnp.moveaxis(piece, 0, 1).reshape(count, devices * size)


def repack_small(rows, devices):
    count = rows.shape[0]
    return jnp.moveaxis(rows.reshape(count, devices, -1), 1, 0).reshape(devices, -1)


def shards(
    frames_in,
    positions,
    mask_vector,
    norm_gains,
    norm_biases,
    depth_gain,
    depth_bias,
    early_in,
    early_out,
    qkv_weight,
    mixer_out,
    pointwise_in,
    pointwise_out,
    depth_kernel,
    late_in,
    late_out,
    position_bias,
    cotangent,
):
    groups, run, model_width = frames_in.shape
    line = lax.axis_size("frames")
    chips = lax.axis_size("batch") // 2
    sizes = (chips, line)
    devices = 2 * chips * line
    length = run * line
    rows = groups * run
    batch, depth = lax.axis_index("batch"), lax.axis_index("frames")
    core = lax.rem(batch, 2)
    first_frame = core * rows
    partner = [(at, at + 1 - 2 * (at % 2)) for at in range(2 * chips)]

    def from_other(array):
        return lax.ppermute(array, "batch", partner)

    big = [early_in, early_out, qkv_weight, mixer_out, pointwise_in, pointwise_out, late_in, late_out]
    small = [mask_vector, norm_gains, norm_biases, depth_gain, depth_bias, depth_kernel, position_bias]
    small_shapes = [value.shape for value in small]
    small_size = sum(math.prod(shape) for shape in small_shapes)
    shard_of = [as_shard(value) for value in big]
    gathered = move(
        Traffic(
            sizes,
            0,
            shards=shard_of[:2] + [pack_small(small, small_shapes)],
            swapped=[frames_in],
            swap_at=3.0,
        )
    )
    w_early_in, w_early_out = as_weight(gathered[0], early_in), as_weight(gathered[1], early_out)
    small_whole = gathered[2].reshape(devices, SMALL[0] * SMALL[1])
    model_rows = (1 + 2 * norm_gains.shape[0], mask_vector.shape[0])
    channel_rows = (2 + KERNEL, depth_gain.shape[0])
    channels_at = math.prod(model_rows)
    table_at = channels_at + math.prod(channel_rows)
    vectors = unpack_small(small_whole, 0, model_rows)
    channels = unpack_small(small_whole, channels_at, channel_rows)
    table = unpack_small(small_whole, table_at, (1, position_bias.shape[0])).reshape(H, NB)
    mask_full, gains, biases = vectors[0], vectors[1:6], vectors[6:11]
    channel_gain, channel_bias = channels[0], channels[1]
    frames_here = gathered[3].reshape(rows, D)

    both = jnp.where(core == 0, 0, 1)
    other_positions = from_other(positions)
    owner = depth // groups
    listed = jnp.where(owner == both, positions, other_positions)
    listed = lax.dynamic_index_in_dim(listed, lax.rem(depth, groups), 0, keepdims=False)
    frame_ids = first_frame + jnp.arange(rows, dtype=jnp.int32)
    masked = jnp.any(listed[:, None] == frame_ids[None, :], axis=0).reshape(rows, 1)

    offsets = offset_rows(table)

    def parts(grad, like):
        return as_parts(grad, sizes, like)

    hidden0 = jnp.where(masked, mask_full[None, :], frames_here.astype(jnp.float32))
    hidden1, inner1, normed1, normed2, *gathered = ffn(
        hidden0,
        vectors,
        0,
        w_early_in,
        w_early_out,
        Traffic(sizes, 1, shards=shard_of[2:4], swapped=[cotangent], swap_at=3.0, pace=2.0),
    )
    w_qkv, w_mixer = as_weight(gathered[0], qkv_weight), as_weight(gathered[1], mixer_out)
    upstream = gathered[2].reshape(rows, D).astype(jnp.float32)
    packed = product(normed2, w_qkv).astype(jnp.bfloat16)
    far = from_other(packed[:, D:])
    mixed_rows, mixed_exact, log_total, *gathered = attend(
        packed, far, offsets, Traffic(sizes, 2, shards=shard_of[4:6], pace=1.15)
    )
    w_point_in = as_weight(gathered[0], pointwise_in)
    w_point_out = as_weight(gathered[1], pointwise_out)
    hidden2 = hidden1 + product(mixed_rows, w_mixer)

    normed3 = layer_norm(hidden2, gains[2], biases[2]).astype(jnp.bfloat16)
    paired = product(normed3, w_point_in).astype(jnp.bfloat16)
    gated = gated_unit(paired.astype(jnp.float32)).astype(jnp.bfloat16)

    def with_edges(array):
        sent = jnp.where(core == 0, array[rows - EDGE :], array[:EDGE])
        edge = from_other(sent)
        nothing = jnp.zeros_like(edge)
        return jnp.concatenate(
            [jnp.where(core == 0, nothing, edge), array, jnp.where(core == 0, edge, nothing)], axis=0
        )

    padded = with_edges(gated)
    depth_values, post, depth_mean, depth_rstd, *gathered = convolve(
        padded, channels, Traffic(sizes, 3, shards=shard_of[6:], split=6, pace=2.4)
    )
    w_late_in, w_late_out = as_weight(gathered[0], late_in), as_weight(gathered[1], late_out)
    hidden3 = hidden2 + product(post, w_point_out)
    hidden4, inner5, normed5, activations = ffn(
        hidden3, vectors, 3, w_late_in, w_late_out, Traffic(sizes, None)
    )

    grad4, gain_grad4, bias_grad4 = norm_back(hidden4, gains[4], biases[4], upstream)
    grad3, late_in_grad, late_out_grad, norm_sums3 = ffn_back(
        hidden3, normed5, grad4, vectors, 3, inner5, w_late_in, w_late_out, Traffic(sizes, None)
    )
    grad_out3 = grad3.astype(jnp.bfloat16)
    pointwise_out_grad = weight_grad(post, grad_out3)
    grad_post = back_product(grad_out3, w_point_out)
    scaled = (depth_values - depth_mean) * depth_rstd
    shifted = scaled * channel_gain + channel_bias
    gate = jax.nn.sigmoid(shifted)
    grad_shifted = grad_post * gate * (1.0 + shifted * (1.0 - gate))
    channel_gain_grad = jnp.sum(grad_shifted * scaled, axis=0)
    channel_bias_grad = jnp.sum(grad_shifted, axis=0)
    weighted = grad_shifted * channel_gain
    grad_depth = depth_rstd * (
        weighted
        - jnp.mean(weighted, axis=-1, keepdims=True)
        - scaled * jnp.mean(weighted * scaled, axis=-1, keepdims=True)
    )
    grad_depth_low = grad_depth.astype(jnp.bfloat16)
    grad_first, grad_second, taps_grad, *sums_late = convolve_back(
        with_edges(grad_depth_low),
        padded,
        paired,
        channels,
        Traffic(
            sizes,
            4,
            grads=[parts(late_out_grad, late_out), parts(late_in_grad, late_in)],
            split=6,
        ),
    )
    grad_paired = jnp.concatenate([grad_first, grad_second], axis=1)
    pointwise_in_grad = weight_grad(normed3, grad_paired)
    grad_normed3 = back_product(grad_paired, w_point_in)
    grad_in3, gain_grad2, bias_grad2 = norm_back(hidden2, gains[2], biases[2], grad_normed3)
    grad2 = grad3 + grad_in3

    grad_out2 = grad2.astype(jnp.bfloat16)
    mixer_out_grad = weight_grad(mixed_rows, grad_out2)
    grad_mixed = back_product(grad_out2, w_mixer).astype(jnp.bfloat16)
    grad_queries, keys_own, values_own, keys_far, values_far, near, far_sums, *sums_depth = attend_back(
        packed,
        far,
        offsets,
        mixed_exact,
        log_total,
        grad_mixed,
        Traffic(
            sizes,
            5,
            grads=[parts(pointwise_out_grad, pointwise_out), parts(pointwise_in_grad, pointwise_in)],
        ),
    )
    table_grad = table_back(near, far_sums, core * (rows // QB)).reshape(H * NB)
    keys_there, values_there = from_other(keys_far), from_other(values_far)
    grad_packed = jnp.concatenate(
        [
            grad_queries,
            (keys_own.astype(jnp.float32) + keys_there.astype(jnp.float32)).astype(jnp.bfloat16),
            (values_own.astype(jnp.float32) + values_there.astype(jnp.float32)).astype(jnp.bfloat16),
        ],
        axis=-1,
    )
    qkv_grad = weight_grad(normed2, grad_packed)
    grad_normed2 = back_product(grad_packed, w_qkv)
    grad_in2, gain_grad1, bias_grad1 = norm_back(hidden1, gains[1], biases[1], grad_normed2)
    grad1 = grad2 + grad_in2
    grad0, early_in_grad, early_out_grad, norm_sums0, *sums_mixer = ffn_back(
        hidden0,
        normed1,
        grad1,
        vectors,
        0,
        inner1,
        w_early_in,
        w_early_out,
        Traffic(
            sizes,
            6,
            grads=[parts(mixer_out_grad, mixer_out), parts(qkv_grad, qkv_weight)],
            swapped=[activations.reshape(groups, run, D)],
            pace=1.3,
        ),
    )
    grad_frames = jnp.where(masked, 0.0, grad0).astype(jnp.bfloat16)
    mask_grad = jnp.sum(jnp.where(masked, grad0, 0.0), axis=0)
    vector_grads = jnp.concatenate(
        [
            row.reshape(1, D)
            for row in (
                mask_grad,
                norm_sums0[0],
                gain_grad1,
                gain_grad2,
                norm_sums3[0],
                gain_grad4,
                norm_sums0[1],
                bias_grad1,
                bias_grad2,
                norm_sums3[1],
                bias_grad4,
            )
        ]
    )
    channel_grads = jnp.concatenate(
        [channel_gain_grad.reshape(1, C), channel_bias_grad.reshape(1, C), taps_grad]
    )
    small_grads = jnp.concatenate(
        [
            repack_small(vector_grads, devices),
            repack_small(channel_grads, devices),
            table_grad.reshape(devices, -1),
        ],
        axis=1,
    )
    small_grads = jnp.pad(small_grads, ((0, 0), (0, SMALL[0] * SMALL[1] - small_size)))
    small_grads = small_grads.astype(jnp.bfloat16)

    sums_early = move(
        Traffic(
            sizes,
            7,
            grads=[
                parts(early_out_grad, early_out),
                parts(early_in_grad, early_in),
                small_grads.reshape((chips, 2, line) + SMALL),
            ],
            swapped=[grad_frames.reshape(groups, run, D)],
        )
    )
    small_sums = sums_early[2].reshape(-1)[:small_size]
    small_out, at = [], 0
    for shape in small_shapes:
        size = math.prod(shape)
        small_out.append(small_sums[at : at + size].reshape(shape))
        at += size
    return (
        sums_mixer[2],
        sums_early[3].astype(jnp.float32),
        small_out[0],
        small_out[1],
        small_out[2],
        small_out[3],
        small_out[4],
        sums_early[1].reshape(early_in.shape),
        sums_early[0].reshape(early_out.shape),
        sums_mixer[1].reshape(qkv_weight.shape),
        sums_mixer[0].reshape(mixer_out.shape),
        sums_depth[1].reshape(pointwise_in.shape),
        sums_depth[0].reshape(pointwise_out.shape),
        small_out[5],
        sums_late[1].reshape(late_in.shape),
        sums_late[0].reshape(late_out.shape),
        small_out[6],
    )


def solution(mesh):
    in_specs = (
        P("batch", "frames", None),
        P("batch", None),
        P(("batch", "frames")),
        P(None, ("batch", "frames")),
        P(None, ("batch", "frames")),
        P(("batch", "frames")),
        P(("batch", "frames")),
        P(("batch", "frames"), None),
        P(("batch", "frames"), None),
        P(("batch", "frames"), None),
        P(("batch", "frames"), None),
        P(("batch", "frames"), None),
        P(("batch", "frames"), None),
        P(None, ("batch", "frames")),
        P(("batch", "frames"), None),
        P(("batch", "frames"), None),
        P(("batch", "frames")),
        P("batch", "frames", None),
    )
    out_specs = (
        P("batch", "frames", None),
        P("batch", "frames", None),
        P(("batch", "frames")),
        P(None, ("batch", "frames")),
        P(None, ("batch", "frames")),
        P(("batch", "frames")),
        P(("batch", "frames")),
        P(("batch", "frames"), None),
        P(("batch", "frames"), None),
        P(("batch", "frames"), None),
        P(("batch", "frames"), None),
        P(("batch", "frames"), None),
        P(("batch", "frames"), None),
        P(None, ("batch", "frames")),
        P(("batch", "frames"), None),
        P(("batch", "frames"), None),
        P(("batch", "frames")),
    )
    return jax.shard_map(shards, mesh=mesh, in_specs=in_specs, out_specs=out_specs, check_vma=False)
```

```python
import functools
import math

import jax
import jax.numpy as jnp
from jax import lax
from jax.experimental import pallas as pl
from jax.experimental.pallas import tpu as pltpu
from jax.sharding import PartitionSpec as P

D = 1024
H = 16
DH = 64
C = 2048
KERNEL = 31
HALF = 15
NB = 32
EPS = 1e-05
LIMITS = (8, 12, 16, 24, 32, 48, 64, 96)
BOTH = ("batch", "frames")
SMALL = (16, 512)


MESH = pl.DeviceIdType.MESH
VMEM_BYTES = 58 * 1024 * 1024


def ring_spot(index, count):
    half = count // 2
    return index + (index // half) * (3 * half - 1 - 2 * index)


def places(chips, frames):
    batch, depth = lax.axis_index("batch"), lax.axis_index("frames")
    chip, core = batch // 2, lax.rem(batch, 2)
    spot = ring_spot(chip, chips)

    def chip_at(offset):
        return ring_spot(lax.rem(spot + offset + chips, chips), chips)

    return chip, core, depth, chip_at


def greet(chips, frames, partners):
    chip, core, depth, chip_at = places(chips, frames)
    barrier = pltpu.get_barrier_semaphore()
    for offset in (1, -1):
        pl.semaphore_signal(
            barrier, inc=1, device_id=(chip_at(offset) * 2 + core, depth), device_id_type=MESH
        )
    pl.semaphore_signal(
        barrier, inc=1, device_id=(chip * 2 + 1 - core, depth), device_id_type=MESH
    )

    @pl.when(depth > 0)
    def _():
        pl.semaphore_signal(barrier, inc=1, device_id=(chip * 2 + core, depth - 1), device_id_type=MESH)

    @pl.when(depth < frames - 1)
    def _():
        pl.semaphore_signal(barrier, inc=1, device_id=(chip * 2 + core, depth + 1), device_id_type=MESH)

    count = 3 + jnp.minimum(depth, 1) + jnp.minimum(frames - 1 - depth, 1)
    if partners:
        groups = frames // 2
        for place in range(groups):
            there, side = core * groups + place, depth // groups

            @pl.when(jnp.logical_or(there != depth, side != core))
            def _():
                pl.semaphore_signal(
                    barrier, inc=1, device_id=(chip * 2 + side, there), device_id_type=MESH
                )

        count = count + groups - (1 - jnp.abs(depth // groups - core))
    pl.semaphore_wait(barrier, count)


def swap_frames(chips, frames, sources, targets, send_sems, recv_sems, local_sem):
    chip, core, depth, chip_at = places(chips, frames)
    groups = frames // 2
    starts, ends = [], []
    for at, (source, target) in enumerate(zip(sources, targets)):
        for place in range(groups):
            there, side = core * groups + place, depth // groups
            mine = jnp.logical_and(there == depth, side == core)
            slot = lax.rem(depth, groups)
            remote = pltpu.make_async_remote_copy(
                src_ref=source.at[place],
                dst_ref=target.at[slot],
                send_sem=send_sems.at[at * groups + place],
                recv_sem=recv_sems.at[at * groups + slot],
                device_id=(chip * 2 + side, there),
                device_id_type=MESH,
            )
            arrival = pltpu.make_async_remote_copy(
                src_ref=source.at[place],
                dst_ref=target.at[place],
                send_sem=send_sems.at[at * groups + place],
                recv_sem=recv_sems.at[at * groups + place],
                device_id=(chip * 2 + side, there),
                device_id_type=MESH,
            )
            here = pltpu.make_async_copy(source.at[place], target.at[slot], local_sem.at[at])
            away = jnp.logical_not(mine)
            starts += [gated(away, remote.start), gated(mine, here.start)]
            ends += [
                gated(away, remote.wait_send),
                gated(away, arrival.wait_recv),
                gated(mine, here.wait),
            ]
    return starts, ends


def gated(condition, action):
    if condition is None:
        return action
    return lambda: pl.when(condition)(action)


def shares(columns, split):
    first = columns * split // 8
    if first % 256 or (columns - first) % 256:
        first = columns
    return (0, first), (first, columns - first)


class Timetable:
    def __init__(self, sizes, split):
        chips, frames = sizes
        half = chips // 2
        self.known = chips == 4 and frames == 4
        self.both = split < 8
        self.half, self.frames = half, frames

    def gather(self, distance, step):
        if not self.known:
            return distance + step + 0.1 * bool(step)
        if self.both:
            return ((0, 0.95, 2.45, 3.7), (1.0, 2.6, 3.75, 4.5), (3.0, 4.5, 4.9, 4.9))[step][distance]
        return ((0, 0.95, 1.95, 2.95), (1.0, 3.0, 4.5, 5.0), (3.5, 4.6, 5.6, 6.0))[step][distance]

    def gather_ring(self, distance, step):
        if not self.known:
            return distance + step
        return ((0, 1.0, 3.0), (1.0, 2.5, 4.25), (2.5, 4.25, 5.0), (4.0, 5.0, 5.25))[step][distance]

    def pair(self, distance):
        if not self.known:
            return distance + self.half + 0.5
        if self.both:
            return (3.05, 4.55, 5.05, 5.3)[distance]
        return (3.55, 4.65, 5.65, 6.05)[distance]

    def merge(self, distance):
        if not self.known:
            return 0.01 * (self.frames - distance)
        return (1.3, 1.0, 0.7, 0.35)[distance]

    def scatter(self, distance, step):
        if not self.known:
            return self.frames - 1 - distance + step
        if self.both:
            return ((4.29, 3.49, 2.69, 1.35), (5.1, 4.3, 3.5, 2.7))[step - 1][distance]
        return ((2.6, 2.2, 1.8, 1.4), (6.4, 5.4, 4.4, 3.4))[step - 1][distance]

    def scatter_ring(self, distance, step):
        if not self.known:
            return self.half - distance + step + 0.5
        return ((2.66, 1.33, 0.4), (3.46, 2.67, 1.34), (4.27, 3.47, 2.68), (5.0, 4.28, 3.48))[step][distance]

    def scatter_last(self, distance):
        if not self.known:
            return self.half - distance + self.frames - 1 + 0.5
        return (5.1, 4.29)[distance]


class Mover:
    def __init__(self, spots, sizes, split, send_sems, recv_sems):
        self.time = Timetable(sizes, split)
        self.chips, self.frames = sizes
        self.chip, self.core, self.depth, self.chip_at = spots
        self.send_sems, self.recv_sems = send_sems, recv_sems
        self.used = 0
        self.events = []
        self.departures = []

    def copy(self, source, target, device, condition):
        at = self.used
        self.used += 1
        made = pltpu.make_async_remote_copy(
            src_ref=source,
            dst_ref=target,
            send_sem=self.send_sems.at[at],
            recv_sem=self.recv_sems.at[at],
            device_id=device,
            device_id_type=MESH,
        )
        self.departures.append(gated(condition, made.wait_send))
        return made

    def at(self, time, *actions):
        self.events += [(time, action) for action in actions]

    def other_core(self):
        return (self.chip * 2 + 1 - self.core, self.depth)

    def group(self, offset):
        at = self.depth + offset
        if offset == 0:
            return at, None
        return jnp.clip(at, 0, self.frames - 1), jnp.logical_and(at >= 0, at < self.frames)

    def chips_at(self, distance):
        if distance == 0:
            return (self.chip,)
        if distance == self.chips // 2:
            return (self.chip_at(distance),)
        return (self.chip_at(distance), self.chip_at(-distance))

    def offsets(self, distance):
        return (0,) if distance == 0 else (-distance, distance)


class Gather(Mover):
    def __init__(self, spots, sizes, shard, whole, split, send_sems, recv_sems, local_sems):
        super().__init__(spots, sizes, split, send_sems, recv_sems)
        self.shard, self.whole = shard, whole
        self.first, self.last = shares(shard.shape[1], split)
        self.local = pltpu.make_async_copy(
            shard, whole.at[self.chip, self.core, self.depth], local_sems.at[0]
        )
        self.at(0, self.local.start)
        for distance in range(self.frames):
            self.spread(distance)
        if self.last[1]:
            for distance in range(self.chips // 2 + 1):
                self.spread_ring(distance)
        for distance in range(self.frames):
            self.hand_over(distance)
        self.ends = self.departures

    def spread(self, distance):
        chip, core, depth, half = self.chip, self.core, self.depth, self.chips // 2
        for offset in self.offsets(distance):
            held, valid = self.group(offset)
            start, columns = self.first
            block = self.whole.at[chip, core, held, :, pl.ds(start, columns)]
            source = block if distance else self.shard.at[:, pl.ds(start, columns)]
            for way in (1, -1):
                if distance + 1 == self.frames or offset * way > 0:
                    continue
                into, there = self.group(way)
                condition = there if valid is None else jnp.logical_and(valid, there)
                made = self.copy(source, block, (chip * 2 + core, into), condition)
                self.at(self.time.gather(distance, 0), gated(condition, made.start))
                comes = self.group(offset - way)[1]
                self.at(self.time.gather(distance + 1, 0), gated(comes, made.wait_recv))
            for step in range(1, half + 1):
                for side, way in enumerate((1, -1)):
                    part = pl.ds(start, columns)
                    if step == half:
                        part = pl.ds(start + side * columns // 2, columns // 2)
                    origin = self.chip_at(-way * (step - 1))
                    target = self.whole.at[origin, core, held, :, part]
                    given = self.shard.at[:, part] if distance == 0 and step == 1 else target
                    made = self.copy(given, target, (self.chip_at(way) * 2 + core, depth), valid)
                    self.at(self.time.gather(distance, step - 1), gated(valid, made.start))
                    self.at(self.time.gather(distance, step), gated(valid, made.wait_recv))

    def hand_over(self, distance):
        for offset in self.offsets(distance):
            held, valid = self.group(offset)
            line = self.whole.at[:, self.core, held]
            pair = self.copy(line, line, self.other_core(), valid)
            if distance == 0:
                self.at(self.time.pair(0), self.local.wait)
            self.at(self.time.pair(distance), gated(valid, pair.start))
            self.departures.append(gated(valid, pair.wait_recv))

    def spread_ring(self, distance):
        core, depth, half = self.core, self.depth, self.chips // 2
        start, columns = self.last
        everything = pl.ds(start, columns)
        if distance < half:
            step = distance + 1
            for side, way in enumerate((1, -1)):
                part = everything
                if step == half:
                    part = pl.ds(start + side * columns // 2, columns // 2)
                target = self.whole.at[self.chip_at(-way * distance), core, depth, :, part]
                given = target if distance else self.shard.at[:, part]
                made = self.copy(given, target, (self.chip_at(way) * 2 + core, depth), None)
                self.at(self.time.gather_ring(distance, 0), made.start)
                self.at(self.time.gather_ring(distance + 1, 0), made.wait_recv)
        for place, chip in enumerate(self.chips_at(distance)):
            for step in range(1, self.frames):
                for way in (1, -1):
                    held, there = self.group(-way * (step - 1))
                    into, beside = self.group(way)
                    valid = beside if there is None else jnp.logical_and(there, beside)
                    block = self.whole.at[chip, core, held, :, everything]
                    given = block if distance or step > 1 else self.shard.at[:, everything]
                    made = self.copy(given, block, (self.chip * 2 + core, into), valid)
                    self.at(self.time.gather_ring(distance, step - 1), gated(valid, made.start))
                    comes = self.group(-way * step)[1]
                    self.at(self.time.gather_ring(distance, step), gated(comes, made.wait_recv))


class Scatter(Mover):
    def __init__(
        self, spots, sizes, grads, out, total, stage, landings, split, send_sems, recv_sems, local_sems
    ):
        super().__init__(spots, sizes, split, send_sems, recv_sems)
        self.grads, self.out, self.total, self.stage = grads, out, total, stage
        (self.halves, self.fulls, self.lines), self.landings = landings[:3], list(landings[3:])
        self.local_sems = local_sems
        self.first, self.last = shares(out.shape[1], split)
        self.merges = 0
        for distance in reversed(range(self.frames)):
            self.collect(distance)
        if self.last[1]:
            for distance in reversed(range(self.chips // 2 + 1)):
                self.collect_ring(distance)
        self.ends = [self.finish] + self.departures

    def add(self, where, piece):
        total = self.total
        total[where] = total[where] + piece

    def merge(self, held, pair, load, stage):
        load.wait()
        pair.wait_recv()

        @pl.loop(0, self.chips)
        def _(chip):
            self.add((chip, held), stage[chip])

    def settle(self, made, where, landed):
        made.wait_recv()
        self.add(where, landed[...])

    def collect(self, distance):
        core, depth, half = self.core, self.depth, self.chips // 2
        for offset in self.offsets(distance):
            held, valid = self.group(offset)
            pair = self.copy(
                self.grads.at[:, 1 - core, held], self.total.at[:, held], self.other_core(), valid
            )
            stage = self.stage.at[held]
            load = pltpu.make_async_copy(
                self.grads.at[:, core, held], stage, self.local_sems.at[self.merges]
            )
            self.merges += 1
            begin = -0.01 * (distance + 1)
            self.at(begin, gated(valid, pair.start), gated(valid, load.start))
            self.at(
                self.time.merge(distance),
                gated(valid, functools.partial(self.merge, held, pair, load, stage)),
            )
            start, columns = self.first
            everything = pl.ds(start, columns)
            for step in range(1, half + 1):
                for side, way in enumerate((1, -1)):
                    part = everything
                    if step == 1:
                        part = pl.ds(start + side * columns // 2, columns // 2)
                    reach = half - step + 1
                    goal = self.chip_at(way * reach)
                    if step == 1:
                        landed = self.halves.at[held, side]
                    else:
                        landed = self.fulls.at[held, 2 * (step - 2) + side]
                    made = self.copy(
                        self.total.at[goal, held, :, part],
                        landed,
                        (self.chip_at(way) * 2 + core, depth),
                        valid,
                    )
                    ready = self.time.scatter(distance, step - 1) if step > 1 else self.time.merge(distance)
                    self.at(ready, gated(valid, made.start))
                    where = (self.chip_at(way * (reach - 1)), held, slice(None), part)
                    self.at(
                        self.time.scatter(distance, step),
                        gated(valid, functools.partial(self.settle, made, where, landed)),
                    )
            if distance == 0:
                continue
            way = 1 if offset > 0 else -1
            landed = self.lines.at[0 if way > 0 else 1, held]
            made = self.copy(
                self.total.at[self.chip, held, :, everything],
                landed,
                (self.chip * 2 + core, self.group(way)[0]),
                valid,
            )
            self.at(self.time.scatter(distance, half), gated(valid, made.start))
            before = self.group(-way)[1]
            goes, there = self.group(offset - way)
            comes = before if there is None else jnp.logical_and(before, there)
            where = (self.chip, goes, slice(None), everything)
            arrived = self.lines.at[0 if way > 0 else 1, goes]
            self.at(
                self.time.scatter(distance - 1, half) - 0.01,
                gated(comes, functools.partial(self.settle, made, where, arrived)),
            )

    def collect_ring(self, distance):
        core, depth, half = self.core, self.depth, self.chips // 2
        start, columns = self.last
        everything = pl.ds(start, columns)
        for chip in self.chips_at(distance):
            for step in range(1, self.frames):
                for way in (1, -1):
                    reach = way * (self.frames - step)
                    held, valid = self.group(reach)
                    landed = self.landings.pop(0)
                    made = self.copy(
                        self.total.at[chip, held, :, everything],
                        landed,
                        (self.chip * 2 + core, self.group(way)[0]),
                        valid,
                    )
                    self.at(self.time.scatter_ring(distance, step - 1), gated(valid, made.start))
                    before = self.group(-way)[1]
                    goes, there = self.group(reach - way)
                    comes = before if there is None else jnp.logical_and(before, there)
                    where = (chip, goes, slice(None), everything)
                    self.at(
                        self.time.scatter_ring(distance, step),
                        gated(comes, functools.partial(self.settle, made, where, landed)),
                    )
        if distance == 0:
            return
        whole = max(
            self.time.scatter_ring(distance, self.frames - 1),
            self.time.scatter_last(distance) if distance < half else 0,
        )
        for side, way in enumerate((1, -1)):
            part = everything
            if distance == half:
                part = pl.ds(start + side * columns // 2, columns // 2)
            goal = self.chip_at(way * distance)
            landed = self.landings.pop(0)
            made = self.copy(
                self.total.at[goal, depth, :, part],
                landed,
                (self.chip_at(way) * 2 + core, depth),
                None,
            )
            self.at(whole + 0.01, made.start)
            where = (self.chip_at(way * (distance - 1)), depth, slice(None), part)
            self.at(
                self.time.scatter_last(distance - 1),
                functools.partial(self.settle, made, where, landed),
            )

    def finish(self):
        self.out[...] = self.total[self.chip, self.depth].astype(self.out.dtype)


def landing_shapes(sizes, rows, columns, split):
    chips, frames = sizes
    (_, first), (_, last) = shares(columns, split)
    half = chips // 2
    shapes = [
        (frames, 2, rows, first // 2),
        (frames, max(2 * (half - 1), 1), rows, first),
        (2, frames, rows, first),
    ]
    if last:
        for distance in reversed(range(half + 1)):
            many = 1 if distance in (0, half) else 2
            shapes += [(rows, last)] * (many * 2 * (frames - 1))
            if distance:
                shapes += [(rows, last // 2 if distance == half else last)] * 2
    return shapes


class Traffic:
    def __init__(
        self, sizes, identity, shards=(), grads=(), swapped=(), swap_at=0, split=8, pace=1.0
    ):
        self.sizes, self.identity = sizes, identity
        self.shards, self.grads, self.swapped = list(shards), list(grads), list(swapped)
        self.swap_at, self.split, self.pace = swap_at, split, pace
        self.active = bool(self.shards or self.grads or self.swapped)

    def operands(self):
        return self.shards + self.grads + self.swapped

    def in_specs(self):
        return [pl.BlockSpec(memory_space=pl.ANY)] * len(self.operands())

    def out_shapes(self):
        chips, frames = self.sizes
        return (
            [jax.ShapeDtypeStruct((chips, 2, frames) + s.shape, s.dtype) for s in self.shards]
            + [jax.ShapeDtypeStruct(g.shape[3:], jnp.float32) for g in self.grads]
            + [jax.ShapeDtypeStruct(s.shape, s.dtype) for s in self.swapped]
        )

    def out_specs(self):
        anywhere = pl.BlockSpec(memory_space=pl.ANY)
        return (
            [anywhere] * len(self.shards)
            + [pl.BlockSpec(memory_space=pltpu.VMEM)] * len(self.grads)
            + [anywhere] * len(self.swapped)
        )

    def scratch(self):
        if not self.active:
            return []
        chips, frames = self.sizes
        shapes = []
        for grad in self.grads:
            shard = grad.shape[3:]
            shapes += [
                pltpu.VMEM((chips, frames) + shard, grad.dtype),
                pltpu.VMEM((frames, chips) + shard, grad.dtype),
            ]
            shapes += [pltpu.VMEM(shape, grad.dtype) for shape in landing_shapes(self.sizes, *shard, self.split)]
        copies = (2 * frames - 1) * (3 + chips) + chips * (2 * frames - 1)
        arrays = max(len(self.shards) + len(self.grads), 1)
        swaps = max(len(self.swapped), 1)
        return shapes + [
            pltpu.SemaphoreType.DMA((arrays, copies)),
            pltpu.SemaphoreType.DMA((arrays, copies)),
            pltpu.SemaphoreType.DMA((arrays, 2 * frames - 1)),
            pltpu.SemaphoreType.DMA((swaps * (frames // 2),)),
            pltpu.SemaphoreType.DMA((swaps * (frames // 2),)),
            pltpu.SemaphoreType.DMA((swaps,)),
        ]

    def plan(self, ins, outs, scratch):
        if not self.active:
            return []
        chips, frames = self.sizes
        scratch = list(scratch)
        send_sems, recv_sems, local_sems, swap_send, swap_recv, swap_local = scratch[-6:]
        spots = places(chips, frames)
        gathers, scatters = len(self.shards), len(self.grads)
        parts = []
        for at in range(gathers + scatters):
            sems = (send_sems.at[at], recv_sems.at[at], local_sems.at[at])
            if at < gathers:
                parts.append(Gather(spots, self.sizes, ins[at], outs[at], self.split, *sems))
                continue
            total, stage = scratch.pop(0), scratch.pop(0)
            many = len(landing_shapes(self.sizes, *outs[at].shape, self.split))
            landings = [scratch.pop(0) for _ in range(many)]
            parts.append(
                Scatter(
                    spots, self.sizes, ins[at], outs[at], total, stage, landings, self.split, *sems
                )
            )
        events = [event for part in parts for event in part.events]
        last = max([time for time, _ in events], default=1.0)
        ends = sum([part.ends for part in parts], [])
        if self.swapped:
            starts, waits = swap_frames(
                chips,
                frames,
                ins[gathers + scatters :],
                outs[gathers + scatters :],
                swap_send,
                swap_recv,
                swap_local,
            )
            events += [(self.swap_at, action) for action in starts]
            ends += waits
        events.append((-1, functools.partial(greet, chips, frames, bool(self.swapped))))
        events = sorted(events, key=lambda event: event[0])
        return [(max(time / last, 0.0) * 0.97, action) for time, action in events] + [
            (1.0, action) for action in ends
        ]


def run_plan(traffic, ins, outs, scratch, step, steps, late=False):
    if not traffic.active:
        return
    whens = [when for when, _ in traffic.plan(ins, outs, scratch)]
    due = [min(int(when * traffic.pace * steps), steps) for when in whens]

    def run(place):
        for at, (_, action) in zip(due, traffic.plan(ins, outs, scratch)):
            if at == place:
                action()

    if late:
        pl.when(step == steps - 1)(functools.partial(run, steps))
        return
    for place in sorted(set(due) - {steps}):
        pl.when(step == place)(functools.partial(run, place))


def traffic_kernel(traffic, *refs):
    count = len(traffic.operands())
    for _, action in traffic.plan(refs[:count], refs[count : 2 * count], refs[2 * count :]):
        action()


def move(traffic):
    return pl.pallas_call(
        functools.partial(traffic_kernel, traffic),
        out_shape=traffic.out_shapes(),
        in_specs=traffic.in_specs(),
        out_specs=traffic.out_specs(),
        scratch_shapes=traffic.scratch(),
        compiler_params=traffic_params(traffic),
    )(*traffic.operands())


def traffic_params(traffic):
    if not traffic.active:
        return pltpu.CompilerParams(vmem_limit_bytes=VMEM_BYTES)
    return pltpu.CompilerParams(
        collective_id=traffic.identity, has_side_effects=True, vmem_limit_bytes=VMEM_BYTES
    )


def layer_norm(values, norm_gain, norm_shift):
    centred = values - jnp.mean(values, axis=-1, keepdims=True)
    spread = jnp.mean(centred * centred, axis=-1, keepdims=True)
    return centred * lax.rsqrt(spread + EPS) * norm_gain + norm_shift


def bucket_of(relative):
    magnitude = jnp.abs(relative)
    above = jnp.zeros_like(relative)
    for threshold in LIMITS:
        above = above + (magnitude >= threshold).astype(jnp.int32)
    inner_bucket = jnp.where(magnitude < 8, magnitude, 7 + above)
    return inner_bucket + NB // 2 * (relative > 0).astype(jnp.int32)


def product(operand_a, operand_b):
    return jnp.dot(operand_a, operand_b, preferred_element_type=jnp.float32)


def weight_grad(operand_a, operand_b):
    return lax.dot_general(
        operand_a, operand_b, (((0,), (0,)), ((), ())), preferred_element_type=jnp.float32
    ).astype(jnp.bfloat16)


def back_product(operand_a, operand_b):
    return lax.dot_general(
        operand_a, operand_b, (((1,), (1,)), ((), ())), preferred_element_type=jnp.float32
    )


def gated_unit(paired):
    return paired[:, :C] * jax.nn.sigmoid(paired[:, C:])


def depth_post(depth_values, norm_gain, norm_shift):
    return jax.nn.silu(layer_norm(depth_values, norm_gain, norm_shift))


def norm_back(hidden, norm_gain, norm_shift, upstream):
    normed_unused, pull_back = jax.vjp(layer_norm, hidden, norm_gain, norm_shift)
    return pull_back(upstream)


TILE = 512
CHUNK = 64


def dot_nt(left, right):
    return lax.dot_general(left, right, (((1,), (1,)), ((), ())), preferred_element_type=jnp.float32)


def dot_nn(left, right):
    return lax.dot_general(left, right, (((1,), (0,)), ((), ())), preferred_element_type=jnp.float32)


def sigmoid(values):
    return 0.5 * jnp.tanh(0.5 * values) + 0.5


def norm_parts(values):
    centred = values - jnp.mean(values, axis=-1, keepdims=True)
    rstd = lax.rsqrt(jnp.mean(centred * centred, axis=-1, keepdims=True) + EPS)
    return centred * rstd, rstd


def gain_row(rows_ref, which):
    return rows_ref[1 + which : 2 + which, :]


def norm_chunk(values, rows_ref, which):
    scaled, _ = norm_parts(values)
    return scaled * gain_row(rows_ref, which) + rows_ref[6 + which : 7 + which, :]


def chunks(rows):
    def each(body):
        @pl.loop(0, rows // CHUNK)
        def _(at):
            body(pl.ds(pl.multiple_of(at * CHUNK, CHUNK), CHUNK))

    return each


def ffn_kernel(traffic, which, hidden_ref, norms_ref, w_in_ref, w_out_ref, *refs):
    moved = len(traffic.operands())
    ins, refs = refs[:moved], refs[moved:]
    out_ref, inner_ref, normed_ref, next_ref = refs[:4]
    outs, refs = refs[4 : 4 + moved], refs[4 + moved :]
    total, refs = refs[0], refs[1:]
    step, steps = pl.program_id(0), pl.num_programs(0)
    run_plan(traffic, ins, outs, refs, step, FFN_STEPS)
    each = chunks(hidden_ref.shape[0])

    @pl.when(step == 0)
    def _():
        def body(here):
            normed_ref[here, :] = norm_chunk(hidden_ref[here, :], norms_ref, which).astype(jnp.bfloat16)
            total[here, :] = jnp.zeros((CHUNK, total.shape[1]), jnp.float32)

        each(body)

    inner = dot_nn(normed_ref[...], w_in_ref[...])
    inner_ref[...] = inner.astype(jnp.bfloat16)
    total[...] += dot_nn((inner * sigmoid(inner)).astype(jnp.bfloat16), w_out_ref[...])

    @pl.when(step == steps - 1)
    def _():
        def body(here):
            hidden = hidden_ref[here, :] + 0.5 * total[here, :]
            out_ref[here, :] = hidden
            next_ref[here, :] = norm_chunk(hidden, norms_ref, which + 1).astype(jnp.bfloat16)

        each(body)

    run_plan(traffic, ins, outs, refs, step, FFN_STEPS, late=True)


FFN_STEPS = 8


def resident(shape):
    return pl.BlockSpec(shape, lambda step: (0,) * len(shape))


def ffn(hidden, norms, which, weight_in, weight_out, traffic):
    rows, width = hidden.shape
    tile = weight_in.shape[1] // FFN_STEPS
    return pl.pallas_call(
        functools.partial(ffn_kernel, traffic, which),
        grid=(FFN_STEPS,),
        out_shape=[
            jax.ShapeDtypeStruct((rows, width), jnp.float32),
            jax.ShapeDtypeStruct((rows, weight_in.shape[1]), jnp.bfloat16),
            jax.ShapeDtypeStruct((rows, width), jnp.bfloat16),
            jax.ShapeDtypeStruct((rows, width), jnp.bfloat16),
        ]
        + traffic.out_shapes(),
        in_specs=[
            resident((rows, width)),
            resident(norms.shape),
            pl.BlockSpec((width, tile), lambda step: (0, step)),
            pl.BlockSpec((tile, width), lambda step: (step, 0)),
        ]
        + traffic.in_specs(),
        out_specs=[
            resident((rows, width)),
            pl.BlockSpec((rows, tile), lambda step: (0, step)),
            resident((rows, width)),
            resident((rows, width)),
        ]
        + traffic.out_specs(),
        scratch_shapes=[pltpu.VMEM((rows, width), jnp.float32)] + traffic.scratch(),
        compiler_params=traffic_params(traffic),
    )(hidden, norms, weight_in, weight_out, *traffic.operands())


def norm_back_chunk(upstream, hidden, norms_ref, which, sums_ref, at):
    scaled, rstd = norm_parts(hidden)
    sums_ref[at : at + 1, :] += jnp.sum(upstream * scaled, axis=0, keepdims=True)
    sums_ref[at + 1 : at + 2, :] += jnp.sum(upstream, axis=0, keepdims=True)
    weighted = upstream * gain_row(norms_ref, which)
    back = weighted - jnp.mean(weighted, axis=-1, keepdims=True)
    return rstd * (back - scaled * jnp.mean(weighted * scaled, axis=-1, keepdims=True))


def ffn_back_kernel(
    traffic, which, last, hidden_ref, normed_ref, grad_ref, norms_ref, inner_ref, w_in_ref, w_out_ref, *refs
):
    if last:
        after_ref, refs = refs[0], refs[1:]
    moved = len(traffic.operands())
    ins, refs = refs[:moved], refs[moved:]
    out_ref, g_in_ref, g_out_ref, sums_ref = refs[:4]
    outs, refs = refs[4 : 4 + moved], refs[4 + moved :]
    (half_grad, turned, total), refs = refs[:3], refs[3:]
    if last:
        arriving, refs = refs[0], refs[1:]
    else:
        arriving = grad_ref
    step, steps = pl.program_id(0), pl.num_programs(0)
    run_plan(traffic, ins, outs, refs, step, FFN_STEPS)
    each = chunks(hidden_ref.shape[0])

    @pl.when(step == 0)
    def _():
        sums_ref[...] = jnp.zeros_like(sums_ref)

        def body(here):
            if last:
                upstream = grad_ref[here, :].astype(jnp.float32)
                arriving[here, :] = norm_back_chunk(
                    upstream, after_ref[here, :], norms_ref, which + 1, sums_ref, 2
                )
            half_grad[here, :] = (0.5 * arriving[here, :]).astype(jnp.bfloat16)
            total[here, :] = jnp.zeros((CHUNK, total.shape[1]), jnp.float32)

        each(body)
        turned[...] = normed_ref[...].T

    inner = inner_ref[...].astype(jnp.float32)
    gate = sigmoid(inner)
    active = (inner * gate).astype(jnp.bfloat16)
    g_out_ref[...] = dot_nn(active.T, half_grad[...]).astype(jnp.bfloat16)
    slope = gate * (1.0 + inner * (1.0 - gate))
    grad_inner = (dot_nt(half_grad[...], w_out_ref[...]) * slope).astype(jnp.bfloat16)
    g_in_ref[...] = dot_nn(turned[...], grad_inner).astype(jnp.bfloat16)
    total[...] += dot_nt(grad_inner, w_in_ref[...])

    @pl.when(step == steps - 1)
    def _():
        def body(here):
            out_ref[here, :] = arriving[here, :] + norm_back_chunk(
                total[here, :], hidden_ref[here, :], norms_ref, which, sums_ref, 0
            )

        each(body)

    run_plan(traffic, ins, outs, refs, step, FFN_STEPS, late=True)


def ffn_back(hidden, normed, grad, norms, which, inner, weight_in, weight_out, traffic, after=None):
    rows, width = hidden.shape
    last = after is not None
    tile = weight_in.shape[1] // FFN_STEPS
    return pl.pallas_call(
        functools.partial(ffn_back_kernel, traffic, which, last),
        grid=(FFN_STEPS,),
        out_shape=[
            jax.ShapeDtypeStruct((rows, width), jnp.float32),
            jax.ShapeDtypeStruct(weight_in.shape, jnp.bfloat16),
            jax.ShapeDtypeStruct(weight_out.shape, jnp.bfloat16),
            jax.ShapeDtypeStruct((8, width), jnp.float32),
        ]
        + traffic.out_shapes(),
        in_specs=[
            resident((rows, width)),
            resident((rows, width)),
            resident((rows, width)),
            resident(norms.shape),
            pl.BlockSpec((rows, tile), lambda step: (0, step)),
            pl.BlockSpec((width, tile), lambda step: (0, step)),
            pl.BlockSpec((tile, width), lambda step: (step, 0)),
        ]
        + [resident((rows, width))] * last
        + traffic.in_specs(),
        out_specs=[
            resident((rows, width)),
            pl.BlockSpec((width, tile), lambda step: (0, step)),
            pl.BlockSpec((tile, width), lambda step: (step, 0)),
            resident((8, width)),
        ]
        + traffic.out_specs(),
        scratch_shapes=[
            pltpu.VMEM((rows, width), jnp.bfloat16),
            pltpu.VMEM((width, rows), jnp.bfloat16),
            pltpu.VMEM((rows, width), jnp.float32),
        ]
        + [pltpu.VMEM((rows, width), jnp.float32)] * last
        + traffic.scratch(),
        compiler_params=traffic_params(traffic),
    )(
        hidden,
        normed,
        grad,
        norms,
        inner,
        weight_in,
        weight_out,
        *([after] if last else []),
        *traffic.operands(),
    )


QB = 128
PAIRS = H // 2
BAND = 3 * QB


def stacked(block):
    lanes = lax.broadcasted_iota(jnp.int32, block.shape, 1)
    nothing = jnp.zeros_like(block)
    return jnp.concatenate(
        [jnp.where(lanes < DH, block, nothing), jnp.where(lanes >= DH, block, nothing)], axis=0
    )


def own_halves(both):
    channels = lax.broadcasted_iota(jnp.int32, (2 * DH, QB), 0)
    return jnp.where(channels < DH, both[:, :QB], both[:, QB:]).T


def offset_rows(table):
    offsets = (jnp.arange(4, dtype=jnp.int32)[:, None] - 1) * QB - jnp.arange(QB, dtype=jnp.int32)
    onehot = (jnp.arange(NB)[:, None, None] == bucket_of(offsets)[None]).astype(jnp.float32)
    rows = jnp.dot(table, onehot.reshape(NB, 4 * QB), precision=lax.Precision.HIGHEST)
    return rows.reshape(PAIRS, 8, QB)


def fill_strip(strip, rows_ref, length):
    far = length - 2 * QB
    rows_of = lax.broadcasted_iota(jnp.int32, (QB, QB), 0)
    lanes_of = lax.broadcasted_iota(jnp.int32, (QB, QB), 1)
    for head in range(2):
        columns = slice(head * QB, (head + 1) * QB)
        turned = []
        for at in range(4):
            row = jnp.broadcast_to(rows_ref[0, head * 4 + at : head * 4 + at + 1, :], (QB, QB))
            turned.append(pltpu.roll(row, 0, 1, stride=1, stride_axis=0))
        for tile in range(3):
            strip[far + tile * QB : far + (tile + 1) * QB, columns] = jnp.where(
                lanes_of >= rows_of, turned[tile], turned[tile + 1]
            )

        @pl.loop(0, far // QB)
        def _(at):
            before, after = pl.multiple_of(at * QB, QB), pl.multiple_of(far + BAND + at * QB, QB)
            strip[pl.ds(before, QB), columns] = turned[0]
            strip[pl.ds(after, QB), columns] = turned[3]


def strip_start(rows, length):
    first = lax.rem(lax.axis_index("batch"), 2) * rows + pl.program_id(1) * QB
    return pl.multiple_of(length - QB - first, QB), first


def in_order(whole, own_ref, far_ref):
    rows = own_ref.shape[0]
    core = lax.rem(lax.axis_index("batch"), 2)
    whole[pl.ds(pl.multiple_of(core * rows, QB), rows), :] = own_ref[...]
    whole[pl.ds(pl.multiple_of((1 - core) * rows, QB), rows), :] = far_ref[...]


def attend_kernel(
    rows, length, traffic, rows_ref, q_ref, k_own_ref, v_own_ref, k_far_ref, v_far_ref, *refs
):
    moved = len(traffic.operands())
    ins, refs = refs[:moved], refs[moved:]
    (out_ref, exact_ref, log_ref), refs = refs[:3], refs[3:]
    outs, refs = refs[:moved], refs[moved:]
    (strip, score, prob, vt, k_all, v_all), refs = refs[:6], refs[6:]
    blocks = rows // QB
    step = pl.program_id(0) * blocks + pl.program_id(1)
    run_plan(traffic, ins, outs, refs, step, PAIRS * blocks)

    @pl.when(pl.program_id(1) == 0)
    def _():
        fill_strip(strip, rows_ref, length)
        in_order(k_all, k_own_ref, k_far_ref)
        in_order(v_all, v_own_ref, v_far_ref)
        vt[...] = v_all[...].T

    start, _ = strip_start(rows, length)
    score[...] = dot_nt(k_all[...], stacked(q_ref[...] * 0.125))

    def highest(at, most):
        here = pl.ds(pl.multiple_of(at * QB, QB), QB)
        values = score[here, :] + strip[pl.ds(pl.multiple_of(start + at * QB, QB), QB), :]
        score[here, :] = values
        return jnp.maximum(most, jnp.max(values.reshape(QB // 8, 8, 2 * QB), axis=0))

    most = lax.fori_loop(
        0, length // QB, highest, jnp.full((8, 2 * QB), -jnp.inf, jnp.float32), unroll=True
    )
    most = jnp.max(most, axis=0, keepdims=True)

    def weigh(at, total):
        here = pl.ds(pl.multiple_of(at * QB, QB), QB)
        values = jnp.exp(score[here, :] - most)
        prob[here, :] = values.astype(jnp.bfloat16)
        return total + jnp.sum(values.reshape(QB // 8, 8, 2 * QB), axis=0)

    total = lax.fori_loop(
        0, length // QB, weigh, jnp.zeros((8, 2 * QB), jnp.float32), unroll=True
    )
    total = jnp.sum(total, axis=0, keepdims=True)
    mixed = dot_nn(vt[...], prob[...]) / total
    exact_ref[...] = own_halves(mixed)
    out_ref[...] = exact_ref[...].astype(out_ref.dtype)
    log_ref[0] = most + jnp.log(total)
    run_plan(traffic, ins, outs, refs, step, PAIRS * blocks, late=True)


def attend(packed, far, offsets, traffic):
    rows = packed.shape[0]
    length = 2 * rows
    blocks = rows // QB
    return pl.pallas_call(
        functools.partial(attend_kernel, rows, length, traffic),
        grid=(PAIRS, blocks),
        out_shape=[
            jax.ShapeDtypeStruct((rows, D), jnp.bfloat16),
            jax.ShapeDtypeStruct((rows, D), jnp.float32),
            jax.ShapeDtypeStruct((PAIRS * blocks, 1, 2 * QB), jnp.float32),
        ]
        + traffic.out_shapes(),
        in_specs=[
            pl.BlockSpec((1, 8, QB), lambda p, b: (p, 0, 0)),
            pl.BlockSpec((QB, 2 * DH), lambda p, b: (b, p)),
            pl.BlockSpec((rows, 2 * DH), lambda p, b: (0, PAIRS + p)),
            pl.BlockSpec((rows, 2 * DH), lambda p, b: (0, 2 * PAIRS + p)),
            pl.BlockSpec((rows, 2 * DH), lambda p, b: (0, p)),
            pl.BlockSpec((rows, 2 * DH), lambda p, b: (0, PAIRS + p)),
        ]
        + traffic.in_specs(),
        out_specs=[
            pl.BlockSpec((QB, 2 * DH), lambda p, b: (b, p)),
            pl.BlockSpec((QB, 2 * DH), lambda p, b: (b, p)),
            pl.BlockSpec((1, 1, 2 * QB), lambda p, b: (p * blocks + b, 0, 0)),
        ]
        + traffic.out_specs(),
        scratch_shapes=[
            pltpu.VMEM((2 * length - QB, 2 * QB), jnp.float32),
            pltpu.VMEM((length, 2 * QB), jnp.float32),
            pltpu.VMEM((length, 2 * QB), jnp.bfloat16),
            pltpu.VMEM((2 * DH, length), jnp.bfloat16),
            pltpu.VMEM((length, 2 * DH), jnp.bfloat16),
            pltpu.VMEM((length, 2 * DH), jnp.bfloat16),
        ]
        + traffic.scratch(),
        compiler_params=traffic_params(traffic),
    )(offsets, packed, packed, packed, far, far, *traffic.operands())


def attend_back_kernel(
    rows,
    length,
    traffic,
    rows_ref,
    q_ref,
    k_own_ref,
    v_own_ref,
    k_far_ref,
    v_far_ref,
    g_ref,
    mixed_ref,
    log_ref,
    *refs,
):
    moved = len(traffic.operands())
    ins, refs = refs[:moved], refs[moved:]
    (dq_ref, dk_own_ref, dv_own_ref, dk_far_ref, dv_far_ref), refs = refs[:5], refs[5:]
    (near_ref, sums_ref), refs = refs[:2], refs[2:]
    outs, refs = refs[:moved], refs[moved:]
    (strip, score, slope, prob, change, kt, dk_sum, dv_sum, near), refs = refs[:9], refs[9:]
    (k_all, v_all), refs = refs[:2], refs[2:]
    block, blocks = pl.program_id(1), rows // QB
    step = pl.program_id(0) * blocks + block
    run_plan(traffic, ins, outs, refs, step, PAIRS * blocks)

    @pl.when(block == 0)
    def _():
        fill_strip(strip, rows_ref, length)
        in_order(k_all, k_own_ref, k_far_ref)
        in_order(v_all, v_own_ref, v_far_ref)
        kt[...] = k_all[...].T
        dk_sum[...] = jnp.zeros_like(dk_sum)
        dv_sum[...] = jnp.zeros_like(dv_sum)
        near[...] = jnp.zeros_like(near)
        change[0:QB, :] = jnp.zeros((QB, 2 * QB), jnp.bfloat16)
        change[length + QB : length + 2 * QB, :] = jnp.zeros((QB, 2 * QB), jnp.bfloat16)

    start, first = strip_start(rows, length)
    q_both = stacked(q_ref[...] * 0.125)
    g_both = stacked(g_ref[...])
    score[...] = dot_nt(k_all[...], q_both)
    slope[...] = dot_nt(v_all[...], g_both)
    log_total = log_ref[0]

    inner = (g_ref[...].astype(jnp.float32) * mixed_ref[...]).T
    centre = jnp.concatenate(
        [
            jnp.sum(inner[:DH, :], axis=0, keepdims=True),
            jnp.sum(inner[DH:, :], axis=0, keepdims=True),
        ],
        axis=1,
    )
    for at in range(length // QB):
        here = pl.ds(at * QB, QB)
        bias = strip[pl.ds(pl.multiple_of(start + at * QB, QB), QB), :]
        weights = jnp.exp(score[here, :] + bias - log_total)
        prob[here, :] = weights.astype(jnp.bfloat16)
        values = weights * (slope[here, :] - centre)
        change[pl.ds(at * QB + QB, QB), :] = values.astype(jnp.bfloat16)
        sums_ref[0, at : at + 1, :] = jnp.sum(values, axis=0, keepdims=True)

    dv_sum[...] += dot_nn(prob[...], g_both)
    moved = change[QB : QB + length, :]
    dk_sum[...] += dot_nn(moved, q_both)
    dq_ref[...] = (own_halves(dot_nn(kt[...], moved)) * 0.125).astype(dq_ref.dtype)
    near[...] += change[pl.ds(pl.multiple_of(first, QB), BAND), :].astype(jnp.float32)

    @pl.when(block == pl.num_programs(1) - 1)
    def _():
        core = lax.rem(lax.axis_index("batch"), 2)
        own = pl.ds(pl.multiple_of(core * rows, QB), rows)
        far = pl.ds(pl.multiple_of((1 - core) * rows, QB), rows)
        dk_own_ref[...] = dk_sum[own, :].astype(jnp.bfloat16)
        dv_own_ref[...] = dv_sum[own, :].astype(jnp.bfloat16)
        dk_far_ref[...] = dk_sum[far, :].astype(jnp.bfloat16)
        dv_far_ref[...] = dv_sum[far, :].astype(jnp.bfloat16)
        rows_of = lax.broadcasted_iota(jnp.int32, (QB, QB), 0)
        lanes_of = lax.broadcasted_iota(jnp.int32, (QB, QB), 1)
        for head in range(2):
            for tile in range(3):
                turned = near[tile * QB : (tile + 1) * QB, head * QB : (head + 1) * QB]
                step = 1
                while step < QB:
                    turned = jnp.where(
                        lax.rem(rows_of // step, 2) == 1, pltpu.roll(turned, QB - step, 1), turned
                    )
                    step *= 2
                upper = jnp.where((lanes_of >= 1) & (lanes_of + rows_of < QB), turned, 0.0)
                for half, piece in enumerate((upper, turned - upper)):
                    at = head * 6 + tile * 2 + half
                    near_ref[0, at : at + 1, :] = jnp.sum(piece, axis=0, keepdims=True)

    run_plan(traffic, ins, outs, refs, step, PAIRS * blocks, late=True)


def attend_back(packed, far, offsets, mixed, log_total, grads, traffic):
    rows = packed.shape[0]
    length = 2 * rows
    blocks = rows // QB
    big = (length, 2 * QB)
    return pl.pallas_call(
        functools.partial(attend_back_kernel, rows, length, traffic),
        grid=(PAIRS, blocks),
        out_shape=[
            jax.ShapeDtypeStruct((rows, D), jnp.bfloat16),
            jax.ShapeDtypeStruct((rows, D), jnp.bfloat16),
            jax.ShapeDtypeStruct((rows, D), jnp.bfloat16),
            jax.ShapeDtypeStruct((rows, D), jnp.bfloat16),
            jax.ShapeDtypeStruct((rows, D), jnp.bfloat16),
            jax.ShapeDtypeStruct((PAIRS, 12, QB), jnp.float32),
            jax.ShapeDtypeStruct((PAIRS * blocks, length // QB, 2 * QB), jnp.float32),
        ]
        + traffic.out_shapes(),
        in_specs=[
            pl.BlockSpec((1, 8, QB), lambda p, b: (p, 0, 0)),
            pl.BlockSpec((QB, 2 * DH), lambda p, b: (b, p)),
            pl.BlockSpec((rows, 2 * DH), lambda p, b: (0, PAIRS + p)),
            pl.BlockSpec((rows, 2 * DH), lambda p, b: (0, 2 * PAIRS + p)),
            pl.BlockSpec((rows, 2 * DH), lambda p, b: (0, p)),
            pl.BlockSpec((rows, 2 * DH), lambda p, b: (0, PAIRS + p)),
            pl.BlockSpec((QB, 2 * DH), lambda p, b: (b, p)),
            pl.BlockSpec((QB, 2 * DH), lambda p, b: (b, p)),
            pl.BlockSpec((1, 1, 2 * QB), lambda p, b: (p * blocks + b, 0, 0)),
        ]
        + traffic.in_specs(),
        out_specs=[
            pl.BlockSpec((QB, 2 * DH), lambda p, b: (b, p)),
            pl.BlockSpec((rows, 2 * DH), lambda p, b: (0, p)),
            pl.BlockSpec((rows, 2 * DH), lambda p, b: (0, p)),
            pl.BlockSpec((rows, 2 * DH), lambda p, b: (0, p)),
            pl.BlockSpec((rows, 2 * DH), lambda p, b: (0, p)),
            pl.BlockSpec((1, 12, QB), lambda p, b: (p, 0, 0)),
            pl.BlockSpec((1, length // QB, 2 * QB), lambda p, b: (p * blocks + b, 0, 0)),
        ]
        + traffic.out_specs(),
        scratch_shapes=[
            pltpu.VMEM((2 * length - QB, 2 * QB), jnp.float32),
            pltpu.VMEM(big, jnp.float32),
            pltpu.VMEM(big, jnp.float32),
            pltpu.VMEM(big, jnp.bfloat16),
            pltpu.VMEM((length + 2 * QB, 2 * QB), jnp.bfloat16),
            pltpu.VMEM((2 * DH, length), jnp.bfloat16),
            pltpu.VMEM((length, 2 * DH), jnp.float32),
            pltpu.VMEM((length, 2 * DH), jnp.float32),
            pltpu.VMEM((BAND, 2 * QB), jnp.float32),
            pltpu.VMEM((length, 2 * DH), jnp.bfloat16),
            pltpu.VMEM((length, 2 * DH), jnp.bfloat16),
        ]
        + traffic.scratch(),
        compiler_params=traffic_params(traffic),
    )(offsets, packed, packed, packed, far, far, grads, mixed, log_total, *traffic.operands())


def table_back(near, sums, first_block):
    blocks = sums.shape[0] // PAIRS
    count = sums.shape[1]
    lane = jnp.arange(QB, dtype=jnp.int32)[None, None, :]
    tile = jnp.arange(3, dtype=jnp.int32)[:, None, None]
    half = jnp.arange(2, dtype=jnp.int32)[None, :, None]
    behind = jnp.where(half == 0, jnp.where(lane == 0, QB, lane), jnp.where(lane == 0, 0, lane - QB))
    offsets = (tile - 1) * QB - behind
    onehot = (bucket_of(offsets)[..., None] == jnp.arange(NB)).astype(jnp.float32)
    close = jnp.einsum(
        "zthl,thlb->zb",
        near.reshape(H, 3, 2, QB),
        onehot,
        precision=lax.Precision.HIGHEST,
    )
    by_block = sums.reshape(PAIRS, blocks, count, 2, QB).sum(axis=4)
    here = first_block + jnp.arange(blocks, dtype=jnp.int32)[:, None]
    there = jnp.arange(count, dtype=jnp.int32)[None, :]
    below = jnp.einsum(
        "pbch,bc->ph", by_block, (there < here - 1).astype(jnp.float32), precision=lax.Precision.HIGHEST
    ).reshape(H)
    above = jnp.einsum(
        "pbch,bc->ph", by_block, (there > here + 1).astype(jnp.float32), precision=lax.Precision.HIGHEST
    ).reshape(H)
    spread = jnp.arange(NB)[None, :]
    close = close + jnp.where(spread == NB // 2 - 1, below[:, None], 0.0)
    return close + jnp.where(spread == NB - 1, above[:, None], 0.0)


EDGE = 16
LANES = 128
BLOCK = 128


def shifted_rows(window):
    for low in range(8):
        turned = pltpu.roll(window, window.shape[0] - low, 0) if low else window
        for high in range(4):
            offset = 8 * high + low
            if 1 <= offset <= KERNEL:
                yield offset, turned[8 * high : 8 * high + BLOCK, :]


def conv_kernel(traffic, padded_ref, channels_ref, *refs):
    moved = len(traffic.operands())
    ins, refs = refs[:moved], refs[moved:]
    (depth_ref, post_ref, mean_ref, rstd_ref), refs = refs[:4], refs[4:]
    outs, refs = refs[:moved], refs[moved:]
    step = pl.program_id(0)
    run_plan(traffic, ins, outs, refs, step, CONV_BLOCKS)
    first = pl.multiple_of(step * BLOCK, BLOCK)

    @pl.loop(0, C // LANES)
    def _(at):
        lanes = pl.ds(pl.multiple_of(at * LANES, LANES), LANES)
        window = padded_ref[pl.ds(first, BLOCK + 2 * EDGE), lanes].astype(jnp.float32)
        total = jnp.zeros((BLOCK, LANES), jnp.float32)
        for offset, rows in shifted_rows(window):
            total = total + rows * channels_ref[offset + 1 : offset + 2, lanes]
        depth_ref[:, lanes] = total

    @pl.loop(0, BLOCK // 16)
    def _(at):
        here = pl.ds(pl.multiple_of(at * 16, 16), 16)
        scaled, rstd = norm_parts(depth_ref[here, :])
        mean_ref[here, :] = jnp.mean(depth_ref[here, :], axis=-1, keepdims=True)
        rstd_ref[here, :] = rstd
        normed = scaled * channels_ref[0:1, :] + channels_ref[1:2, :]
        post_ref[here, :] = (normed * sigmoid(normed)).astype(jnp.bfloat16)

    run_plan(traffic, ins, outs, refs, step, CONV_BLOCKS, late=True)


CONV_BLOCKS = 5


def convolve(padded, channels, traffic):
    rows = padded.shape[0] - 2 * EDGE
    return pl.pallas_call(
        functools.partial(conv_kernel, traffic),
        grid=(CONV_BLOCKS,),
        out_shape=[
            jax.ShapeDtypeStruct((rows, C), jnp.float32),
            jax.ShapeDtypeStruct((rows, C), jnp.bfloat16),
            jax.ShapeDtypeStruct((rows, 1), jnp.float32),
            jax.ShapeDtypeStruct((rows, 1), jnp.float32),
        ]
        + traffic.out_shapes(),
        in_specs=[resident(padded.shape), resident(channels.shape)]
        + traffic.in_specs(),
        out_specs=[
            pl.BlockSpec((BLOCK, C), lambda step: (step, 0)),
            pl.BlockSpec((BLOCK, C), lambda step: (step, 0)),
            pl.BlockSpec((BLOCK, 1), lambda step: (step, 0)),
            pl.BlockSpec((BLOCK, 1), lambda step: (step, 0)),
        ]
        + traffic.out_specs(),
        scratch_shapes=traffic.scratch(),
        compiler_params=traffic_params(traffic),
    )(padded, channels, *traffic.operands())


def conv_back_kernel(traffic, change_ref, gated_ref, first_ref, second_ref, channels_ref, *refs):
    moved = len(traffic.operands())
    ins, refs = refs[:moved], refs[moved:]
    (g_first_ref, g_second_ref, g_taps_ref), refs = refs[:3], refs[3:]
    outs, refs = refs[:moved], refs[moved:]
    sums, refs = refs[0], refs[1:]
    step = pl.program_id(0)
    run_plan(traffic, ins, outs, refs, step, C // LANES)
    sums[...] = jnp.zeros_like(sums)

    @pl.loop(0, CONV_BLOCKS)
    def _(block):
        first = pl.multiple_of(block * BLOCK, BLOCK)
        here = pl.ds(first, BLOCK)
        around = pl.ds(first, BLOCK + 2 * EDGE)
        window = change_ref[around, :].astype(jnp.float32)
        total = jnp.zeros((BLOCK, LANES), jnp.float32)
        for offset, rows in shifted_rows(window):
            total = total + rows * channels_ref[KERNEL - offset + 2 : KERNEL - offset + 3, :]
        gate = sigmoid(second_ref[here, :].astype(jnp.float32))
        through = total * gate
        g_first_ref[here, :] = through.astype(jnp.bfloat16)
        g_second_ref[here, :] = (
            through * first_ref[here, :].astype(jnp.float32) * (1.0 - gate)
        ).astype(jnp.bfloat16)

        change = change_ref[pl.ds(pl.multiple_of(first + EDGE, EDGE), BLOCK), :].astype(jnp.float32)
        window = gated_ref[around, :].astype(jnp.float32)
        for offset, rows in shifted_rows(window):
            part = jnp.sum((rows * change).reshape(BLOCK // 8, 8, LANES), axis=0)
            sums[8 * (offset - 1) : 8 * offset, :] += part

    for tap in range(KERNEL):
        g_taps_ref[tap : tap + 1, :] = jnp.sum(sums[8 * tap : 8 * tap + 8, :], axis=0, keepdims=True)

    run_plan(traffic, ins, outs, refs, step, C // LANES, late=True)


def convolve_back(change, gated, paired, channels, traffic):
    rows = change.shape[0] - 2 * EDGE
    half = C // LANES
    column = pl.BlockSpec((rows, LANES), lambda step: (0, step))
    edged = pl.BlockSpec((rows + 2 * EDGE, LANES), lambda step: (0, step))
    return pl.pallas_call(
        functools.partial(conv_back_kernel, traffic),
        grid=(half,),
        out_shape=[
            jax.ShapeDtypeStruct((rows, C), jnp.bfloat16),
            jax.ShapeDtypeStruct((rows, C), jnp.bfloat16),
            jax.ShapeDtypeStruct((KERNEL, C), jnp.float32),
        ]
        + traffic.out_shapes(),
        in_specs=[
            edged,
            edged,
            column,
            pl.BlockSpec((rows, LANES), lambda step: (0, half + step)),
            pl.BlockSpec((KERNEL + 2, LANES), lambda step: (0, step)),
        ]
        + traffic.in_specs(),
        out_specs=[column, column, pl.BlockSpec((KERNEL, LANES), lambda step: (0, step))]
        + traffic.out_specs(),
        scratch_shapes=[pltpu.VMEM((8 * KERNEL, LANES), jnp.float32)] + traffic.scratch(),
        compiler_params=traffic_params(traffic),
    )(change, gated, paired, paired, channels, *traffic.operands())


def as_shard(array):
    rows = array.shape[0]
    return array if rows % 16 == 0 else array.reshape(16, rows * array.shape[1] // 16)


def as_weight(whole, like):
    devices = math.prod(whole.shape[:3])
    return whole.reshape(devices * like.shape[0], like.shape[1])


def as_parts(grad, sizes, like):
    chips, frames = sizes
    shard = as_shard(jnp.zeros(like.shape, jnp.bfloat16)).shape
    return grad.reshape((chips, 2, frames) + shard)


def pack_small(values, small_shapes):
    flat = jnp.concatenate([value.reshape(-1) for value in values])
    return jnp.pad(flat, (0, SMALL[0] * SMALL[1] - flat.shape[0])).reshape(SMALL)


def unpack_small(packed, at, many):
    count, size = many
    devices = packed.shape[0]
    piece = packed[:, at : at + count * size].reshape(devices, count, size).astype(jnp.float32)
    return jnp.moveaxis(piece, 0, 1).reshape(count, devices * size)


def repack_small(rows, devices):
    count = rows.shape[0]
    return jnp.moveaxis(rows.reshape(count, devices, -1), 1, 0).reshape(devices, -1)


def shards(
    frames_in,
    positions,
    mask_vector,
    norm_gains,
    norm_biases,
    depth_gain,
    depth_bias,
    early_in,
    early_out,
    qkv_weight,
    mixer_out,
    pointwise_in,
    pointwise_out,
    depth_kernel,
    late_in,
    late_out,
    position_bias,
    cotangent,
):
    groups, run, model_width = frames_in.shape
    line = lax.axis_size("frames")
    chips = lax.axis_size("batch") // 2
    sizes = (chips, line)
    devices = 2 * chips * line
    length = run * line
    rows = groups * run
    batch, depth = lax.axis_index("batch"), lax.axis_index("frames")
    core = lax.rem(batch, 2)
    first_frame = core * rows
    partner = [(at, at + 1 - 2 * (at % 2)) for at in range(2 * chips)]

    def from_other(array):
        return lax.ppermute(array, "batch", partner)

    big = [early_in, early_out, qkv_weight, mixer_out, pointwise_in, pointwise_out, late_in, late_out]
    small = [mask_vector, norm_gains, norm_biases, depth_gain, depth_bias, depth_kernel, position_bias]
    small_shapes = [value.shape for value in small]
    small_size = sum(math.prod(shape) for shape in small_shapes)
    shard_of = [as_shard(value) for value in big]
    gathered = move(
        Traffic(
            sizes,
            0,
            shards=shard_of[:2] + [pack_small(small, small_shapes)],
            swapped=[frames_in],
            swap_at=3.0,
        )
    )
    w_early_in, w_early_out = as_weight(gathered[0], early_in), as_weight(gathered[1], early_out)
    small_whole = gathered[2].reshape(devices, SMALL[0] * SMALL[1])
    model_rows = (1 + 2 * norm_gains.shape[0], mask_vector.shape[0])
    channel_rows = (2 + KERNEL, depth_gain.shape[0])
    channels_at = math.prod(model_rows)
    table_at = channels_at + math.prod(channel_rows)
    vectors = unpack_small(small_whole, 0, model_rows)
    channels = unpack_small(small_whole, channels_at, channel_rows)
    table = unpack_small(small_whole, table_at, (1, position_bias.shape[0])).reshape(H, NB)
    mask_full, gains, biases = vectors[0], vectors[1:6], vectors[6:11]
    channel_gain, channel_bias = channels[0], channels[1]
    frames_here = gathered[3].reshape(rows, D)

    both = jnp.where(core == 0, 0, 1)
    other_positions = from_other(positions)
    owner = depth // groups
    listed = jnp.where(owner == both, positions, other_positions)
    listed = lax.dynamic_index_in_dim(listed, lax.rem(depth, groups), 0, keepdims=False)
    frame_ids = first_frame + jnp.arange(rows, dtype=jnp.int32)
    masked = jnp.any(listed[:, None] == frame_ids[None, :], axis=0).reshape(rows, 1)

    offsets = offset_rows(table)

    def parts(grad, like):
        return as_parts(grad, sizes, like)

    hidden0 = jnp.where(masked, mask_full[None, :], frames_here.astype(jnp.float32))
    hidden1, inner1, normed1, normed2, *gathered = ffn(
        hidden0,
        vectors,
        0,
        w_early_in,
        w_early_out,
        Traffic(sizes, 1, shards=shard_of[2:4], swapped=[cotangent], swap_at=3.0, pace=2.0),
    )
    w_qkv, w_mixer = as_weight(gathered[0], qkv_weight), as_weight(gathered[1], mixer_out)
    upstream = gathered[2].reshape(rows, D)
    packed = product(normed2, w_qkv).astype(jnp.bfloat16)
    far = from_other(packed[:, D:])
    mixed_rows, mixed_exact, log_total, *gathered = attend(
        packed, far, offsets, Traffic(sizes, 2, shards=shard_of[4:6], pace=1.15)
    )
    w_point_in = as_weight(gathered[0], pointwise_in)
    w_point_out = as_weight(gathered[1], pointwise_out)
    hidden2 = hidden1 + product(mixed_rows, w_mixer)

    normed3 = layer_norm(hidden2, gains[2], biases[2]).astype(jnp.bfloat16)
    paired = product(normed3, w_point_in).astype(jnp.bfloat16)
    gated = gated_unit(paired.astype(jnp.float32)).astype(jnp.bfloat16)

    def with_edges(array):
        sent = jnp.where(core == 0, array[rows - EDGE :], array[:EDGE])
        edge = from_other(sent)
        nothing = jnp.zeros_like(edge)
        return jnp.concatenate(
            [jnp.where(core == 0, nothing, edge), array, jnp.where(core == 0, edge, nothing)], axis=0
        )

    padded = with_edges(gated)
    depth_values, post, depth_mean, depth_rstd, *gathered = convolve(
        padded, channels, Traffic(sizes, 3, shards=shard_of[6:], split=6, pace=2.4)
    )
    w_late_in, w_late_out = as_weight(gathered[0], late_in), as_weight(gathered[1], late_out)
    hidden3 = hidden2 + product(post, w_point_out)
    hidden4, inner5, normed5, activations = ffn(
        hidden3, vectors, 3, w_late_in, w_late_out, Traffic(sizes, None)
    )

    grad3, late_in_grad, late_out_grad, norm_sums3 = ffn_back(
        hidden3,
        normed5,
        upstream,
        vectors,
        3,
        inner5,
        w_late_in,
        w_late_out,
        Traffic(sizes, None),
        after=hidden4,
    )
    grad_out3 = grad3.astype(jnp.bfloat16)
    pointwise_out_grad = weight_grad(post, grad_out3)
    grad_post = back_product(grad_out3, w_point_out)
    scaled = (depth_values - depth_mean) * depth_rstd
    shifted = scaled * channel_gain + channel_bias
    gate = jax.nn.sigmoid(shifted)
    grad_shifted = grad_post * gate * (1.0 + shifted * (1.0 - gate))
    channel_gain_grad = jnp.sum(grad_shifted * scaled, axis=0)
    channel_bias_grad = jnp.sum(grad_shifted, axis=0)
    weighted = grad_shifted * channel_gain
    grad_depth = depth_rstd * (
        weighted
        - jnp.mean(weighted, axis=-1, keepdims=True)
        - scaled * jnp.mean(weighted * scaled, axis=-1, keepdims=True)
    )
    grad_depth_low = grad_depth.astype(jnp.bfloat16)
    grad_first, grad_second, taps_grad, *sums_late = convolve_back(
        with_edges(grad_depth_low),
        padded,
        paired,
        channels,
        Traffic(
            sizes,
            4,
            grads=[parts(late_out_grad, late_out), parts(late_in_grad, late_in)],
            split=6,
        ),
    )
    grad_paired = jnp.concatenate([grad_first, grad_second], axis=1)
    pointwise_in_grad = weight_grad(normed3, grad_paired)
    grad_normed3 = back_product(grad_paired, w_point_in)
    grad_in3, gain_grad2, bias_grad2 = norm_back(hidden2, gains[2], biases[2], grad_normed3)
    grad2 = grad3 + grad_in3

    grad_out2 = grad2.astype(jnp.bfloat16)
    mixer_out_grad = weight_grad(mixed_rows, grad_out2)
    grad_mixed = back_product(grad_out2, w_mixer).astype(jnp.bfloat16)
    grad_queries, keys_own, values_own, keys_far, values_far, near, far_sums, *sums_depth = attend_back(
        packed,
        far,
        offsets,
        mixed_exact,
        log_total,
        grad_mixed,
        Traffic(
            sizes,
            5,
            grads=[parts(pointwise_out_grad, pointwise_out), parts(pointwise_in_grad, pointwise_in)],
            swapped=[activations.reshape(groups, run, D)],
        ),
    )
    table_grad = table_back(near, far_sums, core * (rows // QB)).reshape(H * NB)
    keys_there, values_there = from_other(keys_far), from_other(values_far)
    grad_packed = jnp.concatenate(
        [
            grad_queries,
            (keys_own.astype(jnp.float32) + keys_there.astype(jnp.float32)).astype(jnp.bfloat16),
            (values_own.astype(jnp.float32) + values_there.astype(jnp.float32)).astype(jnp.bfloat16),
        ],
        axis=-1,
    )
    qkv_grad = weight_grad(normed2, grad_packed)
    grad_normed2 = back_product(grad_packed, w_qkv)
    grad_in2, gain_grad1, bias_grad1 = norm_back(hidden1, gains[1], biases[1], grad_normed2)
    grad1 = grad2 + grad_in2
    grad0, early_in_grad, early_out_grad, norm_sums0, *sums_mixer = ffn_back(
        hidden0,
        normed1,
        grad1,
        vectors,
        0,
        inner1,
        w_early_in,
        w_early_out,
        Traffic(
            sizes,
            6,
            grads=[parts(mixer_out_grad, mixer_out), parts(qkv_grad, qkv_weight)],
            split=6,
            pace=1.2,
        ),
    )
    grad_frames = jnp.where(masked, 0.0, grad0).astype(jnp.bfloat16)
    mask_grad = jnp.sum(jnp.where(masked, grad0, 0.0), axis=0)
    vector_grads = jnp.concatenate(
        [
            row.reshape(1, D)
            for row in (
                mask_grad,
                norm_sums0[0],
                gain_grad1,
                gain_grad2,
                norm_sums3[0],
                norm_sums3[2],
                norm_sums0[1],
                bias_grad1,
                bias_grad2,
                norm_sums3[1],
                norm_sums3[3],
            )
        ]
    )
    channel_grads = jnp.concatenate(
        [channel_gain_grad.reshape(1, C), channel_bias_grad.reshape(1, C), taps_grad]
    )
    small_grads = jnp.concatenate(
        [
            repack_small(vector_grads, devices),
            repack_small(channel_grads, devices),
            table_grad.reshape(devices, -1),
        ],
        axis=1,
    )
    small_grads = jnp.pad(small_grads, ((0, 0), (0, SMALL[0] * SMALL[1] - small_size)))
    small_grads = small_grads.astype(jnp.bfloat16)

    sums_early = move(
        Traffic(
            sizes,
            7,
            grads=[
                parts(early_out_grad, early_out),
                parts(early_in_grad, early_in),
                small_grads.reshape((chips, 2, line) + SMALL),
            ],
            swapped=[grad_frames.reshape(groups, run, D)],
        )
    )
    small_sums = sums_early[2].reshape(-1)[:small_size]
    small_out, at = [], 0
    for shape in small_shapes:
        size = math.prod(shape)
        small_out.append(small_sums[at : at + size].reshape(shape))
        at += size
    return (
        sums_depth[2],
        sums_early[3].astype(jnp.float32),
        small_out[0],
        small_out[1],
        small_out[2],
        small_out[3],
        small_out[4],
        sums_early[1].reshape(early_in.shape),
        sums_early[0].reshape(early_out.shape),
        sums_mixer[1].reshape(qkv_weight.shape),
        sums_mixer[0].reshape(mixer_out.shape),
        sums_depth[1].reshape(pointwise_in.shape),
        sums_depth[0].reshape(pointwise_out.shape),
        small_out[5],
        sums_late[1].reshape(late_in.shape),
        sums_late[0].reshape(late_out.shape),
        small_out[6],
    )


def solution(mesh):
    in_specs = (
        P("batch", "frames", None),
        P("batch", None),
        P(("batch", "frames")),
        P(None, ("batch", "frames")),
        P(None, ("batch", "frames")),
        P(("batch", "frames")),
        P(("batch", "frames")),
        P(("batch", "frames"), None),
        P(("batch", "frames"), None),
        P(("batch", "frames"), None),
        P(("batch", "frames"), None),
        P(("batch", "frames"), None),
        P(("batch", "frames"), None),
        P(None, ("batch", "frames")),
        P(("batch", "frames"), None),
        P(("batch", "frames"), None),
        P(("batch", "frames")),
        P("batch", "frames", None),
    )
    out_specs = (
        P("batch", "frames", None),
        P("batch", "frames", None),
        P(("batch", "frames")),
        P(None, ("batch", "frames")),
        P(None, ("batch", "frames")),
        P(("batch", "frames")),
        P(("batch", "frames")),
        P(("batch", "frames"), None),
        P(("batch", "frames"), None),
        P(("batch", "frames"), None),
        P(("batch", "frames"), None),
        P(("batch", "frames"), None),
        P(("batch", "frames"), None),
        P(None, ("batch", "frames")),
        P(("batch", "frames"), None),
        P(("batch", "frames"), None),
        P(("batch", "frames")),
    )
    return jax.shard_map(shards, mesh=mesh, in_specs=in_specs, out_specs=out_specs, check_vma=False)
```
